768 devices in a mesh: gx: 96 (over z, y), gy: 8 (over x, core).
Axes of the slice: x: 4, y: 8, z: 12, core: 2. Of those that a mesh axis runs over, the one named last changes fastest.
Arguments:
- populations: float32 [19, 768, 128, 128], P(None, 'gx', 'gy'), may hold values from 0.03 to 0.08
- concentration: float32 [2, 768, 128, 128], P(None, 'gx', 'gy'), may hold values from 0.5 to 1.5
- potential: float32 [768, 128, 128], P('gx', 'gy'), may hold values from -3 to 3
- permittivity: float32 [768, 128, 128], P('gx', 'gy'), may hold values from 1 to 10
- fluid_mask: int32 [768, 128, 128], P('gx', 'gy'), may hold values 0 or 1
- owners: int32 [96, 8], P('gx', 'gy'), may hold values from 0 to 7, each once within a row
Outputs:
- final_populations: float32 [19, 768, 128, 128], P(None, 'gx', 'gy')
- final_potential: float32 [768, 128, 128], P('gx', 'gy')
- migrated: float32 [2, 768, 128, 128], P(None, 'gx', 'gy')
The draws below stay inside these ranges and needn't reach their ends.
Inputs may be any that keep to these rules, and one draw needn't show every extreme that they name: Each row of owners is a permutation of the slab indices across the flow.
All inputs are finite; a program needn't handle non-finite values. No bound on the sum of `fluid_mask` on one device may be relied on, other than what follows from the above.
Results may differ from the reference program's by a relative error of at most 0.00012.
Values sent between devices are 32-bit elements; how exact they have to be, the bound alone decides.
No kernel may reach another device: no remote copies, remote signals or barrier semaphores. Data moves between devices by JAX's collectives and lax.ppermute only.
A program may use at most 32 MiB of HBM per device.

```python
import math
import jax
import jax.numpy as jnp
from jax import lax

CX = 8
CY = 16
NZ = 128
STEPS = 2
SWEEPS = 4
NX = 768
NY = 128
N_GX = 96
N_GY = 8


def place_ends(values, key, low, largest):
    shape = values.shape
    spot = [jax.random.randint(jax.random.fold_in(key, axis), (), 0, shape[axis]) for axis in range(len(shape))]
    values = values.at[tuple(spot)].set(low)
    longest = shape.index(max(shape))
    spot[longest] = (spot[longest] + 1) % shape[longest]
    return values.at[tuple(spot)].set(largest)


def block_levels(stream_key, extent, shards, smallest, top_value):
    factor_of = 1.0
    for position, blocks in shards:
        draws = jax.random.uniform(jax.random.fold_in(jax.random.fold_in(stream_key, 6), position), (blocks,), jnp.float32, smallest / len(shards), top_value / len(shards))
        factor_of = factor_of * jnp.repeat(jnp.exp(draws), extent[position] // blocks).reshape((-1,) + (1,) * (len(extent) - 1 - position))
    return factor_of


def gaussian(own_key, shape, spread, reach, shards=(), held_as=jnp.bfloat16):
    values = spread * jax.random.normal(own_key, shape, jnp.float32)
    if shards:
        values = values * block_levels(own_key, shape, shards, -0.22, 0.18)
    return jnp.clip(values, -reach, reach).astype(held_as)


def setup_inputs(seed: int = 0) -> dict:
    arg_keys = jax.random.split(jax.random.key(seed), 7)
    populations = jnp.clip(0.03 + 0.04999999888241291 * jax.random.uniform(arg_keys[0], (19, NX, NY, NZ), jnp.float32) ** block_levels(arg_keys[0], (19, NX, NY, NZ), ((1, 96), (2, 8)), -0.2, 0.2), 0.03, 0.08)
    concentration = jnp.clip(0.5 + 1.0 * jax.random.uniform(arg_keys[1], (2, NX, NY, NZ), jnp.float32) ** block_levels(arg_keys[1], (2, NX, NY, NZ), ((1, 96), (2, 8)), -0.2, 0.2), 0.5, 1.5)
    potential = gaussian(arg_keys[2], (NX, NY, NZ), 0.5, 3.0, ((0, 96), (1, 8)), jnp.float32)
    permittivity = jnp.clip(jnp.exp(math.log(10.0) - 2.3025851 * jax.random.uniform(arg_keys[3], (NX, NY, NZ), jnp.float32) ** block_levels(arg_keys[3], (NX, NY, NZ), ((0, 96), (1, 8)), -0.2, 0.2)), 1.0, 10.0)
    fluid_mask = place_ends((jax.random.randint(arg_keys[4], (NX, NY, NZ), 0, 4) < 3).astype(jnp.int32), jax.random.fold_in(arg_keys[4], 1), 0, 1)
    owners = jax.vmap(lambda own: jax.random.permutation(own, N_GY))(jax.random.split(arg_keys[5], N_GX)).reshape((N_GX, N_GY)).astype(jnp.int32)
    return dict(populations=populations, concentration=concentration, potential=potential, permittivity=permittivity, fluid_mask=fluid_mask, owners=owners)


LATTICE_VELOCITY = ((0, 0, 0), (1, 0, 0), (-1, 0, 0), (0, 1, 0), (0, -1, 0), (0, 0, 1), (0, 0, -1),
                    (1, 1, 0), (-1, -1, 0), (1, -1, 0), (-1, 1, 0), (1, 0, 1), (-1, 0, -1), (1, 0, -1),
                    (-1, 0, 1), (0, 1, 1), (0, -1, -1), (0, 1, -1), (0, -1, 1))
LATTICE_WEIGHT = (1.0 / 3.0,) + (1.0 / 18.0,) * 6 + (1.0 / 36.0,) * 12
OPPOSITE = (0, 2, 1, 4, 3, 6, 5, 8, 7, 10, 9, 12, 11, 14, 13, 16, 15, 18, 17)
RELAX_TIME = 0.8
COUPLING = 0.05
DRIVE_FORCE = 0.001
DIFFUSIVITY = (0.1, 0.15)
VALENCE = (1.0, -1.0)


def collide_cells(popul, fluid, force):
    lattice = jnp.array(LATTICE_VELOCITY, jnp.float32)
    weight = jnp.array(LATTICE_WEIGHT, jnp.float32).reshape(19, 1, 1, 1)
    density = jnp.sum(popul, axis=0)
    moment = jnp.einsum("ic,ixyz->cxyz", lattice, popul, precision=lax.Precision.HIGHEST)
    velocity = fluid * (moment + 0.5 * force) / density
    shifted = (moment + RELAX_TIME * force) / density
    projected = jnp.einsum("ic,cxyz->ixyz", lattice, shifted, precision=lax.Precision.HIGHEST)
    square = jnp.sum(shifted * shifted, axis=0)
    equilibrium = weight * density * (1.0 + 3.0 * projected + 4.5 * projected * projected - 1.5 * square)
    relaxed = popul - (popul - equilibrium) / RELAX_TIME
    return fluid * relaxed, relaxed, velocity


def face_flux(conc_a, conc_b, pot_a, pot_b, vel_a, vel_b, fluid_a, fluid_b):
    diffus = jnp.array(DIFFUSIVITY, jnp.float32).reshape(2, 1, 1, 1)
    valence = jnp.array(VALENCE, jnp.float32).reshape(2, 1, 1, 1)
    drift = valence * 0.5 * (conc_a + conc_b) * (pot_b - pot_a)
    return fluid_a * fluid_b * (-diffus * ((conc_b - conc_a) + drift) + 0.25 * (vel_a + vel_b) * (conc_a + conc_b))


def jacobi_full(poten, permit, charge):
    numer = jnp.zeros_like(poten)
    denom = jnp.zeros_like(poten)
    for axis_index in range(3):
        for offset in (-1, 1):
            face = 0.5 * (permit + jnp.roll(permit, offset, axis_index))
            numer = numer + face * jnp.roll(poten, offset, axis_index)
            denom = denom + face
    return (numer + charge) / denom


def reference(populations, concentration, potential, permittivity, fluid_mask, owners):
    fluid = fluid_mask.astype(jnp.float32)
    popul, conc, poten = populations, concentration, potential
    along = jnp.array([1.0, 0.0, 0.0], jnp.float32).reshape(3, 1, 1, 1)
    for step_index in range(STEPS):
        charge = VALENCE[0] * conc[0] + VALENCE[1] * conc[1]
        for sweep_index in range(SWEEPS):
            poten = jacobi_full(poten, permittivity, charge)
        field = jnp.stack([-0.5 * (jnp.roll(poten, -1, a) - jnp.roll(poten, 1, a)) for a in range(3)])
        force = fluid * (COUPLING * charge * field + DRIVE_FORCE * along)
        leaving, relaxed, velocity = collide_cells(popul, fluid, force)
        rows = []
        for index in range(19):
            shift_by = LATTICE_VELOCITY[index]
            arrived = jnp.roll(leaving[index], shift_by, (0, 1, 2))
            source = jnp.roll(fluid, shift_by, (0, 1, 2))
            rows.append(fluid * (arrived + (1.0 - source) * relaxed[OPPOSITE[index]]) + (1.0 - fluid) * popul[index])
        total = jnp.zeros_like(conc)
        for axis_index in range(3):
            outflow = face_flux(conc, jnp.roll(conc, -1, axis_index + 1), poten, jnp.roll(poten, -1, axis_index),
                                velocity[axis_index], jnp.roll(velocity[axis_index], -1, axis_index),
                                fluid, jnp.roll(fluid, -1, axis_index))
            total = total + outflow - jnp.roll(outflow, 1, axis_index + 1)
        conc = conc - total
        popul = jnp.stack(rows)
    blocks = conc.reshape(2, N_GX, CX, N_GY, CY, NZ)
    picks = jnp.broadcast_to(owners.astype(jnp.int32).reshape(1, N_GX, 1, N_GY, 1, 1), blocks.shape)
    migrated = jnp.take_along_axis(blocks, picks, axis=3).reshape(conc.shape)
    return popul, poten, migrated
```

```python
import jax
import jax.numpy as jnp
from jax import lax
from jax.experimental import pallas as pl
from jax.experimental.pallas import tpu as pltpu
from jax.sharding import PartitionSpec as P

STEPS = 2
SWEEPS = 4
VEL = (
    (0, 0, 0), (1, 0, 0), (-1, 0, 0), (0, 1, 0), (0, -1, 0), (0, 0, 1), (0, 0, -1),
    (1, 1, 0), (-1, -1, 0), (1, -1, 0), (-1, 1, 0), (1, 0, 1), (-1, 0, -1), (1, 0, -1),
    (-1, 0, 1), (0, 1, 1), (0, -1, -1), (0, 1, -1), (0, -1, 1),
)
WEIGHT = (1.0 / 3.0,) + (1.0 / 18.0,) * 6 + (1.0 / 36.0,) * 12
OPP = (0, 2, 1, 4, 3, 6, 5, 8, 7, 10, 9, 12, 11, 14, 13, 16, 15, 18, 17)
TAU = 0.8
COUPLING = 0.05
DRIVE = 0.001
DIFF = (0.1, 0.15)
VALENCE = (1.0, -1.0)

CX, CY, NZ = 8, 16, 128
EX, EY = 20, 32
F32 = jnp.float32

X_IN_LO = tuple(i for i in range(19) if VEL[i][0] == 1)
X_IN_HI = tuple(i for i in range(19) if VEL[i][0] == -1)
Y_IN_LO = tuple(i for i in range(19) if VEL[i][1] == 1)
Y_IN_HI = tuple(i for i in range(19) if VEL[i][1] == -1)
LO_LO, HI_LO = VEL.index((1, 1, 0)), VEL.index((-1, 1, 0))
LO_HI, HI_HI = VEL.index((1, -1, 0)), VEL.index((-1, -1, 0))


def shape(*dims):
    return jax.ShapeDtypeStruct(dims, F32)


def turn(v, by, axis):
    return pltpu.roll(v, by % v.shape[axis], axis)


class Plan:
    def __init__(self, first):
        self.first = first
        self.x_perm = 6 if first else None
        at = 12 if first else 6
        self.x_charge = at
        self.x_conc = at + 5
        at += 7
        if first:
            self.x_fluid = at
            at += 1
        self.x_pop = at
        self.x_dm = at + 5
        self.x_planes = at + 9
        self.y_perm = 8 if first else None
        at = 16 if first else 8
        self.y_charge = at
        self.y_misc = at + 8
        self.y_rows = at + 24
        self.c_charge = 12 if first else 6
        self.c_misc = self.c_charge + 5
        self.c_tiles = self.c_charge + 6


ONE, TWO = Plan(True), Plan(False)


def pack_x(plan, out, low, phi, charge, conc, pop, dm, perm=None, fluid=None):
    deep = slice(0, 6) if low else slice(2, 8)
    out[0:6] = phi[deep]
    if plan.first:
        out[6:12] = perm[deep]
        out[plan.x_fluid] = fluid[0 if low else 7]
    out[plan.x_charge : plan.x_charge + 5] = charge[0:5] if low else charge[3:8]
    edge = 0 if low else 7
    out[plan.x_conc] = conc[0, edge]
    out[plan.x_conc + 1] = conc[1, edge]
    for k, i in enumerate(X_IN_HI if low else X_IN_LO):
        out[plan.x_pop + k] = pop[i, edge]
    for k in range(4):
        out[plan.x_dm + k] = dm[k, edge]


def pack_y(plan, out, low, phi, charge, conc, pop, dm, perm=None, fluid=None):
    tile = slice(0, 8) if low else slice(8, 16)
    row = slice(0, 1) if low else slice(15, 16)
    out[:, 0:8] = phi[:, tile]
    if plan.first:
        out[:, 8:16] = perm[:, tile]
    out[:, plan.y_charge : plan.y_charge + 8] = charge[:, tile]
    rows = [conc[0, :, row], conc[1, :, row]]
    rows.append(fluid[:, row] if plan.first else conc[0, :, row])
    rows += [pop[i, :, row] for i in (Y_IN_HI if low else Y_IN_LO)]
    rows += [dm[k, :, row] for k in range(4)]
    for k, values in enumerate(rows):
        out[:, plan.y_misc + k : plan.y_misc + k + 1] = values


def moments(load):
    dens = load(0)
    mom = [None, None, None]
    for i in range(1, 19):
        v = load(i)
        dens = dens + v
        for c in range(3):
            if VEL[i][c]:
                t = v if VEL[i][c] > 0 else -v
                mom[c] = t if mom[c] is None else mom[c] + t
    return [dens] + mom


def first_kernel(pop, conc, phi, perm, mask, x_hi, x_lo, y_hi, y_lo, dm, charge, fluid):
    charge[...] = conc[0] - conc[1]
    fluid[...] = mask[...].astype(F32)

    def plane(x, _):
        for k, v in enumerate(moments(lambda i: pop[i, x])):
            dm[k, x] = v
        return 0

    lax.fori_loop(0, CX, plane, 0)
    for low, xo, yo in ((False, x_hi, y_hi), (True, x_lo, y_lo)):
        pack_x(ONE, xo, low, phi, charge, conc, pop, dm, perm, fluid)
        pack_y(ONE, yo, low, phi, charge, conc, pop, dm, perm, fluid)


def corner_kernel(plan, xl, xh, c_hi, c_lo):
    for out, tile, row, picks in (
        (c_hi, slice(8, 16), slice(15, 16), (LO_LO, HI_LO)),
        (c_lo, slice(0, 8), slice(0, 1), (LO_HI, HI_HI)),
    ):
        for side, x, names in ((0, xl, X_IN_LO), (1, xh, X_IN_HI)):
            out[side, 0 : plan.c_misc] = x[0 : plan.c_misc, tile]
            pop_at = plan.x_pop + names.index(picks[side])
            rows = [x[plan.x_fluid if plan.first else pop_at, row], x[pop_at, row]]
            rows += [x[plan.x_dm + k, row] for k in range(4)]
            for k, v in enumerate(rows):
                out[side, plan.c_misc, k : k + 1] = v


def lay(ext, own, xl, xh, yl, yh, cl, ch, lo, depth):
    a = 6 - depth
    ext[6:14, 8:24] = own
    ext[a:6, 8:24] = xl
    ext[14 : 14 + depth, 8:24] = xh
    ext[6:14, 0:8] = yl
    ext[6:14, 24:32] = yh
    for part, rows in ((cl, slice(0, 8)), (ch, slice(24, 32))):
        ext[a:6, rows] = part[0, lo : lo + depth]
        ext[14 : 14 + depth, rows] = part[1, lo : lo + depth]


def step(plan, own, msgs, state, work, outs, next_msgs):
    phi, conc, pop, dm, charge_own = own
    xl, xh, yl, yh, cl, ch = msgs
    coef, inv, fl = state
    pa, pb, ce, dn, mm, cc, ypl, yph, vel, lv = work
    pop_out, phi_out, conc_out = outs
    lay(pa, phi[...], xl[0:6], xh[0:6], yl[:, 0:8], yh[:, 0:8], cl, ch, 0, 6)
    q, w = plan.x_charge, plan.y_charge
    lay(ce, charge_own, xl[q : q + 5], xh[q : q + 5], yl[:, w : w + 8], yh[:, w : w + 8],
        cl, ch, plan.c_charge, 5)
    ym = plan.y_misc
    for s in range(2):
        cc[s, 1:9, 8:24] = conc[s]
        cc[s, 0, 8:24] = xl[plan.x_conc + s]
        cc[s, 9, 8:24] = xh[plan.x_conc + s]
        cc[s, 1:9, 7:8] = yl[:, ym + s : ym + s + 1]
        cc[s, 1:9, 24:25] = yh[:, ym + s : ym + s + 1]
    for k, ext in enumerate((dn, mm.at[0], mm.at[1], mm.at[2])):
        ext[1:9, 8:24] = dm[k]
        ext[0, 8:24] = xl[plan.x_dm + k]
        ext[9, 8:24] = xh[plan.x_dm + k]
        for y, c, r in ((yl, cl, 7), (yh, ch, 24)):
            ext[1:9, r : r + 1] = y[:, ym + 8 + k : ym + 9 + k]
            for side, p in ((0, 0), (1, 9)):
                ext[p, r : r + 1] = c[side, plan.c_misc, 2 + k : 3 + k]
    for k in range(5):
        ypl[k, :, 7:8] = yl[:, ym + 3 + k : ym + 4 + k]
        yph[k, :, 0:1] = yh[:, ym + 3 + k : ym + 4 + k]

    src, dst = pa, pb
    for sweep in range(SWEEPS):

        def relax(x, _, src=src, dst=dst):
            mid = src[x]
            acc = ce[x] * inv[x]
            acc += coef[0, x] * src[x - 1] + coef[1, x] * src[x + 1]
            acc += coef[2, x] * turn(mid, 1, 0) + coef[3, x] * turn(mid, -1, 0)
            acc += coef[4, x] * turn(mid, 1, 1) + coef[5, x] * turn(mid, -1, 1)
            dst[x] = acc
            return 0

        lax.fori_loop(1 + sweep, 19 - sweep, relax, 0, unroll=2)
        src, dst = dst, src
    fin = src
    phi_out[...] = fin[6:14, 8:24]

    bad = float("nan")

    def shared(p):
        mid = fin[p + 5]
        grad = [
            -0.5 * (fin[p + 6] - fin[p + 4]),
            -0.5 * (turn(mid, -1, 0) - turn(mid, 1, 0)),
            -0.5 * (turn(mid, -1, 1) - turn(mid, 1, 1)),
        ]
        f = fl[p]
        scale = COUPLING * ce[p + 5]
        force = [f * (scale * g + d) if d else f * (scale * g) for g, d in zip(grad, (DRIVE, 0, 0))]
        dens = dn[p]
        over = 1.0 / dens
        mom = [mm[c, p] for c in range(3)]
        for c in range(3):
            vel[c, p] = f * (mom[c] + 0.5 * force[c]) * over
        sh = [(mom[c] + TAU * force[c]) * over for c in range(3)]
        base = 1.0 - 1.5 * (sh[0] * sh[0] + sh[1] * sh[1] + sh[2] * sh[2])
        return f != 0.0, dens * (1.0 / TAU), sh, base

    def relaxed_of(i, pop_i, part, rows):
        _, dens, sh, base = part
        pr = None
        for c in range(3):
            if VEL[i][c]:
                t = sh[c][rows] if VEL[i][c] > 0 else -sh[c][rows]
                pr = t if pr is None else pr + t
        poly = base[rows]
        if pr is not None:
            poly = poly + pr * (3.0 + 4.5 * pr)
        return (1.0 - 1.0 / TAU) * pop_i + (WEIGHT[i] * dens[rows]) * poly

    lo_t, mid_t, hi_t = slice(0, 8), slice(8, 24), slice(24, 32)

    def emit(i, p, pop_i, part, rows):
        value = relaxed_of(i, pop_i, part, rows)
        lv[i, p, rows] = jnp.where(part[0][rows], value, bad)
        return value

    def collide(p, _):
        part = shared(p)
        is_fluid = part[0][mid_t]
        x = p - 1
        for i in range(19):
            if i > OPP[i]:
                continue
            j = OPP[i]
            pi = pop[i, x]
            ri = relaxed_of(i, pi, part, mid_t)
            if i == j:
                pop_out[i, x] = jnp.where(is_fluid, ri, pi)
                continue
            pj = pop[j, x]
            rj = relaxed_of(j, pj, part, mid_t)
            lv[i, p, mid_t] = jnp.where(is_fluid, ri, bad)
            lv[j, p, mid_t] = jnp.where(is_fluid, rj, bad)
            pop_out[i, x] = jnp.where(is_fluid, rj, pi)
            pop_out[j, x] = jnp.where(is_fluid, ri, pj)
        for k, i in enumerate(Y_IN_LO):
            emit(i, p, ypl[k, x], part, lo_t)
        for k, i in enumerate(Y_IN_HI):
            emit(i, p, yph[k, x], part, hi_t)
        return 0

    lax.fori_loop(1, 9, collide, 0)
    for p, side, x, names, low_pop, high_pop in (
        (0, 0, xl, X_IN_LO, LO_LO, LO_HI),
        (9, 1, xh, X_IN_HI, HI_LO, HI_HI),
    ):
        part = shared(p)
        for k, i in enumerate(names):
            emit(i, p, x[plan.x_pop + k], part, mid_t)
        for c, r, i in ((cl, 7, low_pop), (ch, 24, high_pop)):
            one = [part[0][r : r + 1], part[1][r : r + 1], [s[r : r + 1] for s in part[2]], part[3][r : r + 1]]
            value = relaxed_of(i, c[side, plan.c_misc, 1:2], one, slice(None))
            lv[i, p, r : r + 1] = jnp.where(one[0], value, bad)

    def flux(s, ca, cb, pot_a, pot_b, ua, ub, wall):
        total = ca + cb
        speed = 0.25 * (ua + ub) - (0.5 * DIFF[s] * VALENCE[s]) * (pot_b - pot_a)
        return wall * (total * speed - DIFF[s] * (cb - ca))

    def x_face(s, p):
        wall = fl[p, mid_t] * fl[p + 1, mid_t]
        return flux(s, cc[s, p, mid_t], cc[s, p + 1, mid_t], fin[p + 5, mid_t], fin[p + 6, mid_t],
                    vel[0, p, mid_t], vel[0, p + 1, mid_t], wall)

    def ions(p, before):
        after = []
        f, pot, vy = fl[p], fin[p + 5], vel[1, p]
        for s in range(2):
            face = x_face(s, p)
            total = face - before[s]
            after.append(face)
            c = cc[s, p]
            face = flux(s, c, turn(c, -1, 0), pot, turn(pot, -1, 0), vy, turn(vy, -1, 0), f * turn(f, -1, 0))
            total = total + (face - turn(face, 1, 0))[mid_t]
            fm, cm, pm, vz = f[mid_t], c[mid_t], pot[mid_t], vel[2, p, mid_t]
            face = flux(s, cm, turn(cm, -1, 1), pm, turn(pm, -1, 1), vz, turn(vz, -1, 1), fm * turn(fm, -1, 1))
            total = total + face - turn(face, 1, 1)
            conc_out[s, p - 1] = cm - total
        return tuple(after)

    lax.fori_loop(1, 9, ions, (x_face(0, 0), x_face(1, 0)))

    def stream(x, _):
        f = fl[x + 1, mid_t] != 0.0
        for i in range(1, 19):
            ex, ey, ez = VEL[i]
            came = lv[i, x + 1 - ex, 8 - ey : 24 - ey]
            if ez:
                came = turn(came, ez, 1)
            pop_out[i, x] = jnp.where(f & (came == came), came, pop_out[i, x])
        if next_msgs is not None:
            for k, v in enumerate(moments(lambda i: pop_out[i, x])):
                next_msgs[4][k, x] = v
        return 0

    lax.fori_loop(0, CX, stream, 0)
    if next_msgs is not None:
        x_hi, x_lo, y_hi, y_lo, dm_out, charge_out = next_msgs
        charge_out[...] = conc_out[0] - conc_out[1]
        for low, xo, yo in ((False, x_hi, y_hi), (True, x_lo, y_lo)):
            pack_x(TWO, xo, low, phi_out, charge_out, conc_out, pop_out, dm_out)
            pack_y(TWO, yo, low, phi_out, charge_out, conc_out, pop_out, dm_out)


def step_one_kernel(pop, conc, phi, perm, dm, fluid, xl, xh, yl, yh, cl, ch,
                    pop_out, phi_out, conc_out, x_hi, x_lo, y_hi, y_lo, dm_out, coef, inv, fl,
                    pe, charge_out, *work):
    lay(pe, perm[...], xl[6:12], xh[6:12], yl[:, 8:16], yh[:, 8:16], cl, ch, 6, 6)

    def coefs(x, _):
        mid = pe[x]
        faces = [0.5 * (mid + other) for other in (
            pe[x - 1], pe[x + 1], turn(mid, 1, 0), turn(mid, -1, 0), turn(mid, 1, 1), turn(mid, -1, 1))]
        over = 1.0 / (faces[0] + faces[1] + faces[2] + faces[3] + faces[4] + faces[5])
        inv[x] = over
        for k in range(6):
            coef[k, x] = faces[k] * over
        return 0

    lax.fori_loop(1, 19, coefs, 0)
    fl[1:9, 8:24] = fluid[...]
    fl[0, 8:24] = xl[ONE.x_fluid]
    fl[9, 8:24] = xh[ONE.x_fluid]
    for y, c, r in ((yl, cl, 7), (yh, ch, 24)):
        fl[1:9, r : r + 1] = y[:, ONE.y_misc + 2 : ONE.y_misc + 3]
        for side, p in ((0, 0), (1, 9)):
            fl[p, r : r + 1] = c[side, ONE.c_misc, 0:1]
    step(ONE, (phi, conc, pop, dm, conc[0] - conc[1]), (xl, xh, yl, yh, cl, ch), (coef, inv, fl), work,
         (pop_out, phi_out, conc_out), (x_hi, x_lo, y_hi, y_lo, dm_out, charge_out))


def step_two_kernel(pop, conc, phi, dm, coef, inv, fl, xl, xh, yl, yh, cl, ch,
                    pop_out, phi_out, conc_out, *work):
    step(TWO, (phi, conc, pop, dm, conc[0] - conc[1]), (xl, xh, yl, yh, cl, ch), (coef, inv, fl), work,
         (pop_out, phi_out, conc_out), None)


def call(kernel, outs, args, scratch=()):
    return pl.pallas_call(
        kernel,
        out_shape=outs,
        in_specs=[pl.BlockSpec(memory_space=pltpu.VMEM)] * len(args),
        out_specs=[pl.BlockSpec(memory_space=pltpu.VMEM)] * len(outs),
        scratch_shapes=[pltpu.VMEM(s, F32) for s in scratch],
        compiler_params=pltpu.CompilerParams(vmem_limit_bytes=48 * 1024 * 1024),
    )(*args)


WORK = (
    (EX, EY, NZ), (EX, EY, NZ), (EX, EY, NZ),
    (10, EY, NZ), (3, 10, EY, NZ), (2, 10, EY, NZ),
    (5, CX, 8, NZ), (5, CX, 8, NZ),
    (3, 10, EY, NZ), (19, 10, EY, NZ),
)


def shift(values, axis, by):
    n = lax.axis_size(axis)
    return lax.ppermute(values, axis, [(i, (i + by) % n) for i in range(n)])


def exchange(plan, x_hi, x_lo, y_hi, y_lo):
    yl, yh = shift(y_hi, "gy", 1), shift(y_lo, "gy", -1)
    xl, xh = shift(x_hi, "gx", 1), shift(x_lo, "gx", -1)
    tiles = shape(2, plan.c_tiles, 8, NZ)
    c_hi, c_lo = call(lambda *r: corner_kernel(plan, *r), (tiles, tiles), (xl, xh))
    cl, ch = shift(c_hi, "gy", 1), shift(c_lo, "gy", -1)
    return xl, xh, yl, yh, cl, ch


def messages(plan):
    x, y = shape(plan.x_planes, CY, NZ), shape(CX, plan.y_rows, NZ)
    return (x, x, y, y)


def migrate(conc, owners):
    row = lax.all_gather(owners.reshape(1), "gy", axis=0, tiled=True)
    me = lax.axis_index("gy")
    mate = lax.ppermute(conc, "gy", [(i, i ^ 1) for i in range(8)])
    odd = (me % 2) == 1
    even_block = jnp.where(odd, mate, conc)
    odd_block = jnp.where(odd, conc, mate)

    def block_for(dest):
        return jnp.where(row[dest] % 2 == 1, odd_block, even_block)

    result = block_for(me)
    distance = ((me // 2) - (row[me] // 2)) % 4
    for d in (1, 2, 3):
        got = shift(block_for((me + 2 * d) % 8), "gy", 2 * d)
        result = jnp.where(distance == d, got, result)
    return result


def body(populations, concentration, potential, permittivity, fluid_mask, owners):
    block = shape(CX, CY, NZ)
    pops, ions, four = shape(19, CX, CY, NZ), shape(2, CX, CY, NZ), shape(4, CX, CY, NZ)
    *sent, dm, _, fluid = call(
        first_kernel, messages(ONE) + (four, block, block),
        (populations, concentration, potential, permittivity, fluid_mask))
    got = exchange(ONE, *sent)
    pop, phi, conc, *rest = call(
        step_one_kernel,
        (pops, block, ions) + messages(TWO) + (four, shape(6, EX, EY, NZ), shape(EX, EY, NZ), shape(10, EY, NZ)),
        (populations, concentration, potential, permittivity, dm, fluid) + got,
        ((EX, EY, NZ), (CX, CY, NZ)) + WORK)
    sent, (dm, coef, inv, fl) = rest[:4], rest[4:]
    got = exchange(TWO, *sent)
    pop, phi, conc = call(
        step_two_kernel, (pops, block, ions), (pop, conc, phi, dm, coef, inv, fl) + got, WORK)
    return (pop, phi, migrate(conc, owners))


def solution(mesh):
    in_specs = (
        P(None, "gx", "gy", None),
        P(None, "gx", "gy", None),
        P("gx", "gy", None),
        P("gx", "gy", None),
        P("gx", "gy", None),
        P("gx", "gy"),
    )
    out_specs = (P(None, "gx", "gy", None), P("gx", "gy", None), P(None, "gx", "gy", None))
    return jax.shard_map(body, mesh=mesh, in_specs=in_specs, out_specs=out_specs, check_vma=False)
```

```python
import jax
import jax.numpy as jnp
from jax import lax
from jax.experimental import pallas as pl
from jax.experimental.pallas import tpu as pltpu
from jax.sharding import PartitionSpec as P

STEPS = 2
SWEEPS = 4
VEL = (
    (0, 0, 0), (1, 0, 0), (-1, 0, 0), (0, 1, 0), (0, -1, 0), (0, 0, 1), (0, 0, -1),
    (1, 1, 0), (-1, -1, 0), (1, -1, 0), (-1, 1, 0), (1, 0, 1), (-1, 0, -1), (1, 0, -1),
    (-1, 0, 1), (0, 1, 1), (0, -1, -1), (0, 1, -1), (0, -1, 1),
)
WEIGHT = (1.0 / 3.0,) + (1.0 / 18.0,) * 6 + (1.0 / 36.0,) * 12
OPP = (0, 2, 1, 4, 3, 6, 5, 8, 7, 10, 9, 12, 11, 14, 13, 16, 15, 18, 17)
TAU = 0.8
COUPLING = 0.05
DRIVE = 0.001
DIFF = (0.1, 0.15)
VALENCE = (1.0, -1.0)

CX, CY, NZ = 8, 16, 128
EX, EY = 20, 32
F32 = jnp.float32

X_IN_LO = tuple(i for i in range(19) if VEL[i][0] == 1)
X_IN_HI = tuple(i for i in range(19) if VEL[i][0] == -1)
Y_IN_LO = tuple(i for i in range(19) if VEL[i][1] == 1)
Y_IN_HI = tuple(i for i in range(19) if VEL[i][1] == -1)
LO_LO, HI_LO = VEL.index((1, 1, 0)), VEL.index((-1, 1, 0))
LO_HI, HI_HI = VEL.index((1, -1, 0)), VEL.index((-1, -1, 0))


def shape(*dims):
    return jax.ShapeDtypeStruct(dims, F32)


def turn(v, by, axis):
    return pltpu.roll(v, by % v.shape[axis], axis)


class Plan:
    def __init__(self, first):
        self.first = first
        self.x_perm = 6 if first else None
        at = 12 if first else 6
        self.x_charge = at
        self.x_conc = at + 5
        at += 7
        if first:
            self.x_fluid = at
            at += 1
        self.x_pop = at
        self.x_dm = at + 5
        self.x_planes = at + 9
        self.y_perm = 8 if first else None
        at = 16 if first else 8
        self.y_charge = at
        self.y_misc = at + 8
        self.y_rows = at + 24
        self.c_charge = 12 if first else 6
        self.c_misc = self.c_charge + 5
        self.c_tiles = self.c_charge + 6


ONE, TWO = Plan(True), Plan(False)


def pack_x(plan, out, low, phi, charge, conc, pop, dm, perm=None, fluid=None):
    deep = slice(0, 6) if low else slice(2, 8)
    out[0:6] = phi[deep]
    if plan.first:
        out[6:12] = perm[deep]
        out[plan.x_fluid] = fluid[0 if low else 7]
    out[plan.x_charge : plan.x_charge + 5] = charge[0:5] if low else charge[3:8]
    edge = 0 if low else 7
    out[plan.x_conc] = conc[0, edge]
    out[plan.x_conc + 1] = conc[1, edge]
    for k, i in enumerate(X_IN_HI if low else X_IN_LO):
        out[plan.x_pop + k] = pop[i, edge]
    for k in range(4):
        out[plan.x_dm + k] = dm[k, edge]


def pack_y(plan, out, low, owner, phi, charge, conc, pop, dm, perm=None, fluid=None):
    tile = slice(0, 8) if low else slice(8, 16)
    row = slice(0, 1) if low else slice(15, 16)
    out[:, 0:8] = phi[:, tile]
    if plan.first:
        out[:, 8:16] = perm[:, tile]
    out[:, plan.y_charge : plan.y_charge + 8] = charge[:, tile]
    rows = [conc[0, :, row], conc[1, :, row]]
    rows.append(fluid[:, row] if plan.first else conc[0, :, row])
    rows += [pop[i, :, row] for i in (Y_IN_HI if low else Y_IN_LO)]
    rows += [dm[k, :, row] for k in range(4)]
    for k, values in enumerate(rows):
        out[:, plan.y_misc + k : plan.y_misc + k + 1] = values
    out[0, plan.y_misc + 12 : plan.y_misc + 13] = owner


def moments(load):
    dens = load(0)
    mom = [None, None, None]
    for i in range(1, 19):
        v = load(i)
        dens = dens + v
        for c in range(3):
            if VEL[i][c]:
                t = v if VEL[i][c] > 0 else -v
                mom[c] = t if mom[c] is None else mom[c] + t
    return [dens] + mom


def first_kernel(owner, *refs):
    far, near, sems = refs[:5], refs[13:18], refs[18]
    pop, conc, phi, perm, mask = near
    x_hi, x_lo, y_hi, y_lo, dm, charge, fluid, owner_row = refs[5:13]
    copies = [pltpu.make_async_copy(a, b, sems.at[k]) for k, (a, b) in enumerate(zip(far, near))]
    for copy in copies:
        copy.start()
    owner_row[...] = jnp.full((8, NZ), owner[0, 0], jnp.int32).astype(F32)
    for copy in copies:
        copy.wait()
    charge[...] = conc[0] - conc[1]
    fluid[...] = mask[...].astype(F32)

    def plane(x, _):
        for k, v in enumerate(moments(lambda i: pop[i, x])):
            dm[k, x] = v
        return 0

    lax.fori_loop(0, CX, plane, 0)
    for low, xo, yo in ((False, x_hi, y_hi), (True, x_lo, y_lo)):
        pack_x(ONE, xo, low, phi, charge, conc, pop, dm, perm, fluid)
        pack_y(ONE, yo, low, owner_row[0:1], phi, charge, conc, pop, dm, perm, fluid)


def corner_kernel(plan, xl, xh, c_hi, c_lo):
    for out, tile, row, picks in (
        (c_hi, slice(8, 16), slice(15, 16), (LO_LO, HI_LO)),
        (c_lo, slice(0, 8), slice(0, 1), (LO_HI, HI_HI)),
    ):
        for side, x, names in ((0, xl, X_IN_LO), (1, xh, X_IN_HI)):
            out[side, 0 : plan.c_misc] = x[0 : plan.c_misc, tile]
            pop_at = plan.x_pop + names.index(picks[side])
            rows = [x[plan.x_fluid if plan.first else pop_at, row], x[pop_at, row]]
            rows += [x[plan.x_dm + k, row] for k in range(4)]
            for k, v in enumerate(rows):
                out[side, plan.c_misc, k : k + 1] = v


def lay(ext, own, xl, xh, yl, yh, cl, ch, lo, depth):
    a = 6 - depth
    ext[6:14, 8:24] = own
    ext[a:6, 8:24] = xl
    ext[14 : 14 + depth, 8:24] = xh
    ext[6:14, 0:8] = yl
    ext[6:14, 24:32] = yh
    for part, rows in ((cl, slice(0, 8)), (ch, slice(24, 32))):
        ext[a:6, rows] = part[0, lo : lo + depth]
        ext[14 : 14 + depth, rows] = part[1, lo : lo + depth]


def lay_all(plan, phi, conc, dm, charge_own, msgs, pa, ce, dn, mm, cc):
    xl, xh, yl, yh, cl, ch = msgs
    lay(pa, phi[...], xl[0:6], xh[0:6], yl[:, 0:8], yh[:, 0:8], cl, ch, 0, 6)
    q, w = plan.x_charge, plan.y_charge
    lay(ce, charge_own, xl[q : q + 5], xh[q : q + 5], yl[:, w : w + 8], yh[:, w : w + 8],
        cl, ch, plan.c_charge, 5)
    ym = plan.y_misc
    for s in range(2):
        cc[s, 1:9, 8:24] = conc[s]
        cc[s, 0, 8:24] = xl[plan.x_conc + s]
        cc[s, 9, 8:24] = xh[plan.x_conc + s]
        cc[s, 1:9, 7:8] = yl[:, ym + s : ym + s + 1]
        cc[s, 1:9, 24:25] = yh[:, ym + s : ym + s + 1]
    for k, ext in enumerate((dn, mm.at[0], mm.at[1], mm.at[2])):
        ext[1:9, 8:24] = dm[k]
        ext[0, 8:24] = xl[plan.x_dm + k]
        ext[9, 8:24] = xh[plan.x_dm + k]
        for y, c, r in ((yl, cl, 7), (yh, ch, 24)):
            ext[1:9, r : r + 1] = y[:, ym + 8 + k : ym + 9 + k]
            for side, p in ((0, 0), (1, 9)):
                ext[p, r : r + 1] = c[side, plan.c_misc, 2 + k : 3 + k]


LO_T, MID_T, HI_T = slice(0, 8), slice(8, 24), slice(24, 32)


def sweeps(coef, inv, ce, src, dst):
    for sweep in range(SWEEPS):

        def relax(x, _, src=src, dst=dst):
            mid = src[x]
            acc = ce[x] * inv[x]
            acc += coef[0, x] * src[x - 1] + coef[1, x] * src[x + 1]
            acc += coef[2, x] * turn(mid, 1, 0) + coef[3, x] * turn(mid, -1, 0)
            acc += coef[4, x] * turn(mid, 1, 1) + coef[5, x] * turn(mid, -1, 1)
            dst[x] = acc
            return 0

        lax.fori_loop(1 + sweep, 19 - sweep, relax, 0, unroll=6)
        src, dst = dst, src
    return src


def motion(fin, ce, fl, dn, mm, vel, sh):
    def plane(p, _):
        mid = fin[p + 5]
        grad = [
            -0.5 * (fin[p + 6] - fin[p + 4]),
            -0.5 * (turn(mid, -1, 0) - turn(mid, 1, 0)),
            -0.5 * (turn(mid, -1, 1) - turn(mid, 1, 1)),
        ]
        f = fl[p]
        scale = COUPLING * ce[p + 5]
        force = [f * (scale * g + d) if d else f * (scale * g) for g, d in zip(grad, (DRIVE, 0, 0))]
        dens = dn[p]
        over = 1.0 / dens
        mom = [mm[c, p] for c in range(3)]
        for c in range(3):
            vel[c, p] = f * (mom[c] + 0.5 * force[c]) * over
        u = [(mom[c] + TAU * force[c]) * over for c in range(3)]
        for c in range(3):
            sh[c, p] = u[c]
        sh[3, p] = 1.0 - 1.5 * (u[0] * u[0] + u[1] * u[1] + u[2] * u[2])
        sh[4, p] = dens * (1.0 / TAU)
        return 0

    lax.fori_loop(0, 10, plane, 0, unroll=2)


def ions(fin, fl, cc, vel, store):
    def flux(s, ca, cb, pot_a, pot_b, ua, ub, wall):
        total = ca + cb
        speed = 0.25 * (ua + ub) - (0.5 * DIFF[s] * VALENCE[s]) * (pot_b - pot_a)
        return wall * (total * speed - DIFF[s] * (cb - ca))

    def x_face(s, p):
        wall = fl[p, MID_T] * fl[p + 1, MID_T]
        return flux(s, cc[s, p, MID_T], cc[s, p + 1, MID_T], fin[p + 5, MID_T], fin[p + 6, MID_T],
                    vel[0, p, MID_T], vel[0, p + 1, MID_T], wall)

    def plane(p, before):
        after = []
        f, pot, vy = fl[p], fin[p + 5], vel[1, p]
        for s in range(2):
            face = x_face(s, p)
            total = face - before[s]
            after.append(face)
            c = cc[s, p]
            face = flux(s, c, turn(c, -1, 0), pot, turn(pot, -1, 0), vy, turn(vy, -1, 0), f * turn(f, -1, 0))
            total = total + (face - turn(face, 1, 0))[MID_T]
            fm, cm, pm, vz = f[MID_T], c[MID_T], pot[MID_T], vel[2, p, MID_T]
            face = flux(s, cm, turn(cm, -1, 1), pm, turn(pm, -1, 1), vz, turn(vz, -1, 1), fm * turn(fm, -1, 1))
            total = total + face - turn(face, 1, 1)
            store(s, p - 1, cm - total)
        return tuple(after)

    lax.fori_loop(1, 9, plane, (x_face(0, 0), x_face(1, 0)), unroll=4)


def collide_and_stream(plan, pop, fl, sh, msgs, lv, pop_out, dm_out):
    xl, xh, yl, yh, cl, ch = msgs
    ym = plan.y_misc
    bad = float("nan")

    def load(p, rows):
        return [sh[c, p, rows] for c in range(5)] + [fl[p, rows] != 0.0]

    def relaxed_of(i, pop_i, part):
        pr = None
        for c in range(3):
            if VEL[i][c]:
                t = part[c] if VEL[i][c] > 0 else -part[c]
                pr = t if pr is None else pr + t
        poly = part[3]
        if pr is not None:
            poly = poly + pr * (3.0 + 4.5 * pr)
        return (1.0 - 1.0 / TAU) * pop_i + (WEIGHT[i] * part[4]) * poly

    def collide(p, _):
        x = p - 1
        part = load(p, MID_T)
        wet = part[5]
        for i in range(19):
            j = OPP[i]
            if i > j:
                continue
            pi = pop[i, x]
            ri = relaxed_of(i, pi, part)
            if i == j:
                pop_out[i, x] = jnp.where(wet, ri, pi)
                continue
            pj = pop[j, x]
            rj = relaxed_of(j, pj, part)
            lv[i, p, MID_T] = jnp.where(wet, ri, bad)
            lv[j, p, MID_T] = jnp.where(wet, rj, bad)
            pop_out[i, x] = jnp.where(wet, rj, pi)
            pop_out[j, x] = jnp.where(wet, ri, pj)
        for y, names, r in ((yl, Y_IN_LO, 7), (yh, Y_IN_HI, 24)):
            row = slice(r, r + 1)
            part = load(p, row)
            for k, i in enumerate(names):
                value = relaxed_of(i, y[x, ym + 3 + k : ym + 4 + k], part)
                lv[i, p, row] = jnp.where(part[5], value, bad)
        return 0

    lax.fori_loop(1, 9, collide, 0)
    for p, side, x, names, low_pop, high_pop in (
        (0, 0, xl, X_IN_LO, LO_LO, LO_HI),
        (9, 1, xh, X_IN_HI, HI_LO, HI_HI),
    ):
        part = load(p, MID_T)
        for k, i in enumerate(names):
            lv[i, p, MID_T] = jnp.where(part[5], relaxed_of(i, x[plan.x_pop + k], part), bad)
        for c, r, i in ((cl, 7, low_pop), (ch, 24, high_pop)):
            row = slice(r, r + 1)
            part = load(p, row)
            lv[i, p, row] = jnp.where(part[5], relaxed_of(i, c[side, plan.c_misc, 1:2], part), bad)

    def stream(x, _):
        wet = fl[x + 1, MID_T] != 0.0
        for i in range(1, 19):
            ex, ey, ez = VEL[i]
            came = lv[i, x + 1 - ex, 8 - ey : 24 - ey]
            if ez:
                came = turn(came, ez, 1)
            pop_out[i, x] = jnp.where(wet & (came == came), came, pop_out[i, x])
        if dm_out is not None:
            for k, v in enumerate(moments(lambda i: pop_out[i, x])):
                dm_out[k, x] = v
        return 0

    lax.fori_loop(0, CX, stream, 0, unroll=2)


def step_one_kernel(pop, conc, phi, perm, dm, fluid, owner_two, xl, xh, yl, yh, cl, ch,
                    pop_out, phi_out, conc_out, x_hi, x_lo, y_hi, y_lo, dm_out, coef, inv, fl,
                    pe, charge, pa, pb, ce, dn, mm, cc, vel, sh, lv):
    msgs = (xl, xh, yl, yh, cl, ch)
    lay(pe, perm[...], xl[6:12], xh[6:12], yl[:, 8:16], yh[:, 8:16], cl, ch, 6, 6)

    def coefs(x, _):
        mid = pe[x]
        faces = [0.5 * (mid + other) for other in (
            pe[x - 1], pe[x + 1], turn(mid, 1, 0), turn(mid, -1, 0), turn(mid, 1, 1), turn(mid, -1, 1))]
        over = 1.0 / (faces[0] + faces[1] + faces[2] + faces[3] + faces[4] + faces[5])
        inv[x] = over
        for k in range(6):
            coef[k, x] = faces[k] * over
        return 0

    lax.fori_loop(1, 19, coefs, 0, unroll=6)
    fl[1:9, 8:24] = fluid[...]
    fl[0, 8:24] = xl[ONE.x_fluid]
    fl[9, 8:24] = xh[ONE.x_fluid]
    for y, c, r in ((yl, cl, 7), (yh, ch, 24)):
        fl[1:9, r : r + 1] = y[:, ONE.y_misc + 2 : ONE.y_misc + 3]
        for side, p in ((0, 0), (1, 9)):
            fl[p, r : r + 1] = c[side, ONE.c_misc, 0:1]
    lay_all(ONE, phi, conc, dm, conc[0] - conc[1], msgs, pa, ce, dn, mm, cc)
    fin = sweeps(coef, inv, ce, pa, pb)
    phi_out[...] = fin[6:14, MID_T]
    motion(fin, ce, fl, dn, mm, vel, sh)

    def store(s, x, values):
        conc_out[s, x] = values

    ions(fin, fl, cc, vel, store)
    collide_and_stream(ONE, pop, fl, sh, msgs, lv, pop_out, dm_out)
    charge[...] = conc_out[0] - conc_out[1]
    above = yh[0, ONE.y_misc + 12 : ONE.y_misc + 13]
    for low, xo, yo, owner in ((False, x_hi, y_hi, owner_two[0:1]), (True, x_lo, y_lo, above)):
        pack_x(TWO, xo, low, phi_out, charge, conc_out, pop_out, dm_out)
        pack_y(TWO, yo, low, owner, phi_out, charge, conc_out, pop_out, dm_out)


def ions_two_kernel(conc, phi, dm, coef, inv, fl, xl, xh, yl, yh, cl, ch,
                    phi_out, slab, sh, pa, pb, ce, dn, mm, cc, vel):
    lay_all(TWO, phi, conc, dm, conc[0] - conc[1], (xl, xh, yl, yh, cl, ch), pa, ce, dn, mm, cc)
    fin = sweeps(coef, inv, ce, pa, pb)
    phi_out[...] = fin[6:14, MID_T]
    motion(fin, ce, fl, dn, mm, vel, sh)

    def store(s, x, values):
        slab[s * CX + x] = values

    ions(fin, fl, cc, vel, store)
    slab[2 * CX, 0:8] = jnp.broadcast_to(yl[0, TWO.y_misc + 12 : TWO.y_misc + 13], (8, NZ))


def flow_two_kernel(pop, fl, sh, xl, xh, yl, yh, cl, ch, pop_out, lv):
    collide_and_stream(TWO, pop, fl, sh, (xl, xh, yl, yh, cl, ch), lv, pop_out, None)


def owner_kernel(yl, out):
    out[...] = jnp.broadcast_to(yl[0, ONE.y_misc + 12 : ONE.y_misc + 13], (8, NZ))


def route_kernel(mine, other, yh, owner_two, *outs):
    me = jnp.full((1, NZ), lax.axis_index("gy"), jnp.int32).astype(F32)
    wanted = (yh[0, TWO.y_misc + 12 : TWO.y_misc + 13], other[2 * CX, 0:1], owner_two[0:1])
    for want, out in zip(wanted, outs):
        pick = want == me
        for s in range(2):
            for x in range(CX):
                out[s, x] = jnp.where(pick, mine[s * CX + x], other[s * CX + x])


def arrive_kernel(mine, other, one, two, three, owner_row, out):
    me = jnp.full((1, NZ), lax.axis_index("gy"), jnp.int32).astype(F32)
    away = me - owner_row[0:1]
    away = jnp.where(away < 0, away + 8.0, away)
    for s in range(2):
        for x in range(CX):
            v = jnp.where(away < 0.5, mine[s * CX + x], other[s * CX + x])
            v = jnp.where(away > 1.5, one[s, x], v)
            v = jnp.where(away > 3.5, two[s, x], v)
            out[s, x] = jnp.where(away > 5.5, three[s, x], v)


VMEM, FAR, SMEM = (pl.BlockSpec(memory_space=m) for m in (pltpu.VMEM, pltpu.HBM, pltpu.SMEM))


def call(kernel, outs, args, scratch=(), specs=None, flops=0):
    return pl.pallas_call(
        kernel,
        out_shape=outs,
        in_specs=specs or [VMEM] * len(args),
        out_specs=[VMEM] * len(outs),
        scratch_shapes=[pltpu.VMEM(s, F32) if isinstance(s, tuple) else s for s in scratch],
        compiler_params=pltpu.CompilerParams(vmem_limit_bytes=24 * 1024 * 1024),
        cost_estimate=pl.CostEstimate(flops=flops, bytes_accessed=0, transcendentals=0) if flops else None,
    )(*args)


HALO = (EX, EY, NZ)
RIM = (10, EY, NZ)
FIELDS = (HALO, HALO, HALO, RIM, (3,) + RIM, (2,) + RIM, (3,) + RIM)


def shift(values, axis, by):
    n = lax.axis_size(axis)
    return lax.ppermute(values, axis, [(i, (i + by) % n) for i in range(n)])


def exchange(plan, x_hi, x_lo, y_hi, y_lo):
    yl, yh = shift(y_hi, "gy", 1), shift(y_lo, "gy", -1)
    xl, xh = shift(x_hi, "gx", 1), shift(x_lo, "gx", -1)
    tiles = shape(2, plan.c_tiles, 8, NZ)
    c_hi, c_lo = call(lambda *r: corner_kernel(plan, *r), (tiles, tiles), (xl, xh))
    cl, ch = shift(c_hi, "gy", 1), shift(c_lo, "gy", -1)
    return xl, xh, yl, yh, cl, ch


def messages(plan):
    x, y = shape(plan.x_planes, CY, NZ), shape(CX, plan.y_rows, NZ)
    return (x, x, y, y)


def body(populations, concentration, potential, permittivity, fluid_mask, owners):
    block, row = shape(CX, CY, NZ), shape(8, NZ)
    pops, both, four = shape(19, CX, CY, NZ), shape(2, CX, CY, NZ), shape(4, CX, CY, NZ)
    *sent, dm, _, fluid, owner = call(
        first_kernel, messages(ONE) + (four, block, block, row),
        (owners,) + tuple(pltpu.with_memory_space_constraint(v, pltpu.HBM) for v in (
            populations, concentration, potential, permittivity, fluid_mask)),
        (pops.shape, both.shape, block.shape, block.shape, pltpu.VMEM(block.shape, jnp.int32),
         pltpu.SemaphoreType.DMA((5,))),
        [SMEM] + [FAR] * 5)
    got = exchange(ONE, *sent)
    (owner_one,) = call(owner_kernel, (row,), (got[2],))
    owner_two = shift(owner_one, "gy", 1)
    pop, phi, conc, *rest = call(
        step_one_kernel,
        (pops, block, both) + messages(TWO) + (four, shape(6, *HALO), shape(*HALO), shape(*RIM)),
        (populations, concentration, potential, permittivity, dm, fluid, owner_two) + got,
        (HALO, block.shape) + FIELDS + ((5,) + RIM, (19,) + RIM))
    sent, (dm, coef, inv, fl) = rest[:4], rest[4:]
    got = exchange(TWO, *sent)
    phi, mine, sh = call(
        ions_two_kernel, (block, shape(2 * CX + 1, CY, NZ), shape(5, *RIM)),
        (conc, phi, dm, coef, inv, fl) + got, FIELDS)
    other = shift(mine, "gy", 1)
    (pop,) = call(flow_two_kernel, (pops,), (pop, fl, sh) + got, ((19,) + RIM,), flops=40_000_000)
    routed = call(route_kernel, (both, both, both), (mine, other, got[3], owner_two))
    came = [shift(v, "gy", d) for v, d in zip(routed, (2, 4, 6))]
    (migrated,) = call(arrive_kernel, (both,), (mine, other, *came, owner))
    return (pop, phi, migrated)


def solution(mesh):
    in_specs = (
        P(None, "gx", "gy", None),
        P(None, "gx", "gy", None),
        P("gx", "gy", None),
        P("gx", "gy", None),
        P("gx", "gy", None),
        P("gx", "gy"),
    )
    out_specs = (P(None, "gx", "gy", None), P("gx", "gy", None), P(None, "gx", "gy", None))
    return jax.shard_map(body, mesh=mesh, in_specs=in_specs, out_specs=out_specs, check_vma=False)
```

```python
import jax
import jax.numpy as jnp
from jax import lax
from jax.experimental import pallas as pl
from jax.experimental.pallas import tpu as pltpu
from jax.sharding import PartitionSpec as P

STEPS = 2
SWEEPS = 4
VEL = (
    (0, 0, 0), (1, 0, 0), (-1, 0, 0), (0, 1, 0), (0, -1, 0), (0, 0, 1), (0, 0, -1),
    (1, 1, 0), (-1, -1, 0), (1, -1, 0), (-1, 1, 0), (1, 0, 1), (-1, 0, -1), (1, 0, -1),
    (-1, 0, 1), (0, 1, 1), (0, -1, -1), (0, 1, -1), (0, -1, 1),
)
WEIGHT = (1.0 / 3.0,) + (1.0 / 18.0,) * 6 + (1.0 / 36.0,) * 12
OPP = (0, 2, 1, 4, 3, 6, 5, 8, 7, 10, 9, 12, 11, 14, 13, 16, 15, 18, 17)
TAU = 0.8
COUPLING = 0.05
DRIVE = 0.001
DIFF = (0.1, 0.15)
VALENCE = (1.0, -1.0)

CX, CY, NZ = 8, 16, 128
EX, EY = 20, 32
F32 = jnp.float32

X_IN_LO = tuple(i for i in range(19) if VEL[i][0] == 1)
X_IN_HI = tuple(i for i in range(19) if VEL[i][0] == -1)
Y_IN_LO = tuple(i for i in range(19) if VEL[i][1] == 1)
Y_IN_HI = tuple(i for i in range(19) if VEL[i][1] == -1)
LO_LO, HI_LO = VEL.index((1, 1, 0)), VEL.index((-1, 1, 0))
LO_HI, HI_HI = VEL.index((1, -1, 0)), VEL.index((-1, -1, 0))


def shape(*dims):
    return jax.ShapeDtypeStruct(dims, F32)


def turn(v, by, axis):
    return pltpu.roll(v, by % v.shape[axis], axis)


class Plan:
    def __init__(self, first):
        self.first = first
        rows = [("phi", 6)] + [("perm", 6)] * first + [("charge", 4), ("conc", 2)] + [("fluid", 1)] * first
        self.y = {}
        at = 0
        for name, n in rows + [("pop", 5), ("dm", 4), ("owner", 1)]:
            self.y[name] = at
            at += n
        self.y_rows = -(-at // 8) * 8
        self.skip = 0 if first else 2
        planes = [("phi", 6 - self.skip)] + [("perm", 6)] * first + [("charge", 4), ("conc", 2)]
        planes += [("fluid", 1)] * first + [("pop", 5), ("dm", 4), ("cphi", 3)]
        planes += [("cperm", 3)] * first + [("ccharge", 2), ("cmisc", 1)]
        self.x = {}
        at = 0
        for name, n in planes:
            self.x[name] = at
            at += n
        self.x_planes = at


ONE, TWO = Plan(True), Plan(False)
DEEP = ((1, 6, 6, 1), (2, 5, 5, 2), (3, 4, 4, 3))
CHARGE = ((1, 5, 4, 2), (2, 4, 3, 3))


def pack_y(plan, out, low, owner, phi, charge, conc, pop, dm, perm=None, fluid=None):
    y = plan.y
    six = slice(0, 6) if low else slice(10, 16)
    four = slice(1, 5) if low else slice(11, 15)
    row = slice(0, 1) if low else slice(15, 16)
    out[:, 0:6] = phi[:, six]
    if plan.first:
        out[:, y["perm"] : y["perm"] + 6] = perm[:, six]
        out[:, y["fluid"] : y["fluid"] + 1] = fluid[:, row]
    out[:, y["charge"] : y["charge"] + 4] = charge[:, four]
    for s in range(2):
        out[:, y["conc"] + s : y["conc"] + s + 1] = conc[s, :, row]
    for k, i in enumerate(Y_IN_HI if low else Y_IN_LO):
        out[:, y["pop"] + k : y["pop"] + k + 1] = pop[i, :, row]
    for k in range(4):
        out[:, y["dm"] + k : y["dm"] + k + 1] = dm[k, :, row]
    out[0, y["owner"] : y["owner"] + 1] = owner


def pack_x(plan, out, low, yl, yh, phi, charge, conc, pop, dm, perm=None, fluid=None):
    x, y = plan.x, plan.y

    def at(depth):
        return depth - 1 if low else CX - depth

    def spread(to, field, first, last):
        lo = min(at(first), at(last))
        out[to : to + last - first + 1] = field[lo : lo + last - first + 1]

    spread(0, phi, 1 + plan.skip, 6)
    spread(x["charge"], charge, 2, 5)
    edge = at(1)
    for s in range(2):
        out[x["conc"] + s] = conc[s, edge]
    if plan.first:
        spread(x["perm"], perm, 1, 6)
        out[x["fluid"]] = fluid[edge]
    for k, i in enumerate(X_IN_HI if low else X_IN_LO):
        out[x["pop"] + k] = pop[i, edge]
    for k in range(4):
        out[x["dm"] + k] = dm[k, edge]
    for name in ("phi", "perm")[: 1 + plan.first]:
        for k, (d, n, e, m) in enumerate(DEEP):
            c, r = x["c" + name] + k, y[name]
            out[c, 8 - n : 8] = yl[at(d), r + 6 - n : r + 6]
            out[c, 0:m] = yl[at(e), r + 6 - m : r + 6]
            out[c, 8 : 8 + n] = yh[at(d), r : r + n]
            out[c, 16 - m : 16] = yh[at(e), r : r + m]
    q, o = y["charge"], y["conc"]

    def near(msg, depth):
        return msg[at(depth), o : o + 1] - msg[at(depth), o + 1 : o + 2]

    for k, (d, n, e, m) in enumerate(CHARGE):
        c = x["ccharge"] + k
        out[c, 8 - n : 7] = yl[at(d), q + 5 - n : q + 4]
        out[c, 7:8] = near(yl, d)
        out[c, 0 : m - 1] = yl[at(e), q + 5 - m : q + 4]
        out[c, m - 1 : m] = near(yl, e)
        out[c, 8:9] = near(yh, d)
        out[c, 9 : 8 + n] = yh[at(d), q : q + n - 1]
        out[c, 16 - m : 17 - m] = near(yh, e)
        out[c, 17 - m : 16] = yh[at(e), q : q + m - 1]
    for r, msg, names, pick in ((0, yl, Y_IN_LO, HI_LO if low else LO_LO), (8, yh, Y_IN_HI, HI_HI if low else LO_HI)):
        take = [(1, y["pop"] + names.index(pick))] + [(2 + k, y["dm"] + k) for k in range(4)]
        if plan.first:
            take.append((0, y["fluid"]))
        for to, source in take:
            out[x["cmisc"], r + to : r + to + 1] = msg[edge, source : source + 1]
        out[x["cmisc"], r + 6 : r + 7] = near(msg, 5)


def lay(ext, own, name, depth, pairs, plan, xl, xh, yl, yh):
    x, y = plan.x, plan.y
    skip = plan.skip if name == "phi" else 0
    n = 6 - skip
    ext[6:14, 8:24] = own
    ext[0:n, 8:24] = xl[x[name] : x[name] + n]
    ext[14 + skip : 20, 8:24] = xh[x[name] : x[name] + n]
    ext[6:14, 2:8] = yl[:, y[name] : y[name] + 6]
    ext[6:14, 24:30] = yh[:, y[name] : y[name] + 6]
    corners(ext, x["c" + name], pairs, xl, xh)


def corners(ext, at, pairs, xl, xh):
    for k, (d, n, e, m) in enumerate(pairs):
        for msg, p, q in ((xl, 6 - d, 6 - e), (xh, 13 + d, 13 + e)):
            ext[p, 8 - n : 8] = msg[at + k, 8 - n : 8]
            ext[q, 8 - m : 8] = msg[at + k, 0:m]
            ext[p, 24 : 24 + n] = msg[at + k, 8 : 8 + n]
            ext[q, 24 : 24 + m] = msg[at + k, 16 - m : 16]


def moments(load):
    dens = load(0)
    mom = [None, None, None]
    for i in range(1, 19):
        v = load(i)
        dens = dens + v
        for c in range(3):
            if VEL[i][c]:
                t = v if VEL[i][c] > 0 else -v
                mom[c] = t if mom[c] is None else mom[c] + t
    return [dens] + mom


def first_kernel(owner, *refs):
    far, near, sems = refs[:5], refs[11:16], refs[16]
    pop, conc, phi, perm, mask = near
    y_hi, y_lo, dm, charge, fluid, owner_row = refs[5:11]
    copies = [pltpu.make_async_copy(a, b, sems.at[k]) for k, (a, b) in enumerate(zip(far, near))]
    for copy in copies:
        copy.start()
    owner_row[...] = jnp.full((8, NZ), owner[0, 0], jnp.int32).astype(F32)
    for copy in copies:
        copy.wait()
    charge[...] = conc[0] - conc[1]
    fluid[...] = mask[...].astype(F32)

    def plane(x, _):
        for k, v in enumerate(moments(lambda i: pop[i, x])):
            dm[k, x] = v
        return 0

    lax.fori_loop(0, CX, plane, 0, unroll=2)
    for low, yo in ((False, y_hi), (True, y_lo)):
        pack_y(ONE, yo, low, owner_row[0:1], phi, charge, conc, pop, dm, perm, fluid)


def x_one_kernel(phi, charge, conc, pop, dm, perm, fluid, yl, yh, x_hi, x_lo, owner):
    for low, xo in ((False, x_hi), (True, x_lo)):
        pack_x(ONE, xo, low, yl, yh, phi, charge, conc, pop, dm, perm, fluid)
    owner[...] = jnp.broadcast_to(yl[0, ONE.y["owner"] : ONE.y["owner"] + 1], (8, NZ))


def x_two_kernel(phi, charge, conc, pop, dm, yl, yh, x_hi, x_lo):
    for low, xo in ((False, x_hi), (True, x_lo)):
        pack_x(TWO, xo, low, yl, yh, phi, charge, conc, pop, dm)


def lay_all(plan, phi, conc, dm, charge, msgs, pa, ce, dn, mm, cc):
    xl, xh, yl, yh = msgs
    x, y = plan.x, plan.y
    lay(pa, phi[...], "phi", 6, DEEP, plan, xl, xh, yl, yh)
    ce[6:14, 8:24] = charge[...]
    q = x["charge"]
    ce[1:5, 8:24] = xl[q : q + 4]
    ce[15:19, 8:24] = xh[q : q + 4]
    c = x["conc"]
    ce[5, 8:24] = xl[c] - xl[c + 1]
    ce[14, 8:24] = xh[c] - xh[c + 1]
    q, c = y["charge"], y["conc"]
    ce[6:14, 3:7] = yl[:, q : q + 4]
    ce[6:14, 7:8] = yl[:, c : c + 1] - yl[:, c + 1 : c + 2]
    ce[6:14, 24:25] = yh[:, c : c + 1] - yh[:, c + 1 : c + 2]
    ce[6:14, 25:29] = yh[:, q : q + 4]
    corners(ce, x["ccharge"], CHARGE, xl, xh)
    m = x["cmisc"]
    for msg, p in ((xl, 1), (xh, 18)):
        ce[p, 7:8] = msg[m, 6:7]
        ce[p, 24:25] = msg[m, 14:15]
    for s in range(2):
        cc[s, 1:9, 8:24] = conc[s]
        cc[s, 0, 8:24] = xl[x["conc"] + s]
        cc[s, 9, 8:24] = xh[x["conc"] + s]
        cc[s, 1:9, 7:8] = yl[:, c + s : c + s + 1]
        cc[s, 1:9, 24:25] = yh[:, c + s : c + s + 1]
    for k, ext in enumerate((dn, mm.at[0], mm.at[1], mm.at[2])):
        ext[1:9, 8:24] = dm[k]
        for msg, p in ((xl, 0), (xh, 9)):
            ext[p, 8:24] = msg[x["dm"] + k]
            ext[p, 7:8] = msg[m, 2 + k : 3 + k]
            ext[p, 24:25] = msg[m, 10 + k : 11 + k]
        for msg, r in ((yl, 7), (yh, 24)):
            ext[1:9, r : r + 1] = msg[:, y["dm"] + k : y["dm"] + k + 1]


LO_T, MID_T, HI_T = slice(0, 8), slice(8, 24), slice(24, 32)


def sweeps(coef, inv, ce, src, dst):
    for sweep in range(SWEEPS):

        def relax(x, _, src=src, dst=dst):
            mid = src[x]
            acc = ce[x] * inv[x]
            acc += coef[0, x] * src[x - 1] + coef[1, x] * src[x + 1]
            acc += coef[2, x] * turn(mid, 1, 0) + coef[3, x] * turn(mid, -1, 0)
            acc += coef[4, x] * turn(mid, 1, 1) + coef[5, x] * turn(mid, -1, 1)
            dst[x] = acc
            return 0

        lax.fori_loop(1 + sweep, 19 - sweep, relax, 0, unroll=6)
        src, dst = dst, src
    return src


def motion(fin, ce, fl, dn, mm, vel, sh):
    def plane(p, _):
        mid = fin[p + 5]
        grad = [
            -0.5 * (fin[p + 6] - fin[p + 4]),
            -0.5 * (turn(mid, -1, 0) - turn(mid, 1, 0)),
            -0.5 * (turn(mid, -1, 1) - turn(mid, 1, 1)),
        ]
        f = fl[p]
        scale = COUPLING * ce[p + 5]
        force = [f * (scale * g + d) if d else f * (scale * g) for g, d in zip(grad, (DRIVE, 0, 0))]
        dens = dn[p]
        over = 1.0 / dens
        mom = [mm[c, p] for c in range(3)]
        for c in range(3):
            vel[c, p] = f * (mom[c] + 0.5 * force[c]) * over
        u = [(mom[c] + TAU * force[c]) * over for c in range(3)]
        for c in range(3):
            sh[c, p] = u[c]
        sh[3, p] = 1.0 - 1.5 * (u[0] * u[0] + u[1] * u[1] + u[2] * u[2])
        sh[4, p] = dens * (1.0 / TAU)
        return 0

    lax.fori_loop(0, 10, plane, 0, unroll=2)


def ions(fin, fl, cc, vel, store):
    def flux(s, ca, cb, pot_a, pot_b, ua, ub, wall):
        total = ca + cb
        speed = 0.25 * (ua + ub) - (0.5 * DIFF[s] * VALENCE[s]) * (pot_b - pot_a)
        return wall * (total * speed - DIFF[s] * (cb - ca))

    def x_face(s, p):
        wall = fl[p, MID_T] * fl[p + 1, MID_T]
        return flux(s, cc[s, p, MID_T], cc[s, p + 1, MID_T], fin[p + 5, MID_T], fin[p + 6, MID_T],
                    vel[0, p, MID_T], vel[0, p + 1, MID_T], wall)

    def plane(p, before):
        after = []
        f, pot, vy = fl[p], fin[p + 5], vel[1, p]
        for s in range(2):
            face = x_face(s, p)
            total = face - before[s]
            after.append(face)
            c = cc[s, p]
            face = flux(s, c, turn(c, -1, 0), pot, turn(pot, -1, 0), vy, turn(vy, -1, 0), f * turn(f, -1, 0))
            total = total + (face - turn(face, 1, 0))[MID_T]
            fm, cm, pm, vz = f[MID_T], c[MID_T], pot[MID_T], vel[2, p, MID_T]
            face = flux(s, cm, turn(cm, -1, 1), pm, turn(pm, -1, 1), vz, turn(vz, -1, 1), fm * turn(fm, -1, 1))
            total = total + face - turn(face, 1, 1)
            store(s, p - 1, cm - total)
        return tuple(after)

    lax.fori_loop(1, 9, plane, (x_face(0, 0), x_face(1, 0)), unroll=4)


def collide_and_stream(plan, pop, fl, sh, msgs, lv, pop_out, dm_out):
    xl, xh, yl, yh = msgs
    y_pop, x_pop, misc = plan.y["pop"], plan.x["pop"], plan.x["cmisc"]
    bad = float("nan")

    def load(p, rows):
        return [sh[c, p, rows] for c in range(5)] + [fl[p, rows] != 0.0]

    def relaxed_of(i, pop_i, part):
        pr = None
        for c in range(3):
            if VEL[i][c]:
                t = part[c] if VEL[i][c] > 0 else -part[c]
                pr = t if pr is None else pr + t
        poly = part[3]
        if pr is not None:
            poly = poly + pr * (3.0 + 4.5 * pr)
        return (1.0 - 1.0 / TAU) * pop_i + (WEIGHT[i] * part[4]) * poly

    def collide(p, _):
        x = p - 1
        part = load(p, MID_T)
        wet = part[5]
        for i in range(19):
            j = OPP[i]
            if i > j:
                continue
            pi = pop[i, x]
            ri = relaxed_of(i, pi, part)
            if i == j:
                pop_out[i, x] = jnp.where(wet, ri, pi)
                continue
            pj = pop[j, x]
            rj = relaxed_of(j, pj, part)
            lv[i, p, MID_T] = jnp.where(wet, ri, bad)
            lv[j, p, MID_T] = jnp.where(wet, rj, bad)
            pop_out[i, x] = jnp.where(wet, rj, pi)
            pop_out[j, x] = jnp.where(wet, ri, pj)
        for y, names, r in ((yl, Y_IN_LO, 7), (yh, Y_IN_HI, 24)):
            row = slice(r, r + 1)
            part = load(p, row)
            for k, i in enumerate(names):
                value = relaxed_of(i, y[x, y_pop + k : y_pop + k + 1], part)
                lv[i, p, row] = jnp.where(part[5], value, bad)
        return 0

    lax.fori_loop(1, 9, collide, 0)
    for p, x, names, low_pop, high_pop in (
        (0, xl, X_IN_LO, LO_LO, LO_HI),
        (9, xh, X_IN_HI, HI_LO, HI_HI),
    ):
        part = load(p, MID_T)
        for k, i in enumerate(names):
            lv[i, p, MID_T] = jnp.where(part[5], relaxed_of(i, x[x_pop + k], part), bad)
        for c, r, i in ((1, 7, low_pop), (9, 24, high_pop)):
            row = slice(r, r + 1)
            part = load(p, row)
            lv[i, p, row] = jnp.where(part[5], relaxed_of(i, x[misc, c : c + 1], part), bad)

    def stream(x, _):
        wet = fl[x + 1, MID_T] != 0.0
        for i in range(1, 19):
            ex, ey, ez = VEL[i]
            came = lv[i, x + 1 - ex, 8 - ey : 24 - ey]
            if ez:
                came = turn(came, ez, 1)
            pop_out[i, x] = jnp.where(wet & (came == came), came, pop_out[i, x])
        if dm_out is not None:
            for k, v in enumerate(moments(lambda i: pop_out[i, x])):
                dm_out[k, x] = v
        return 0

    lax.fori_loop(0, CX, stream, 0, unroll=2)


def step_one_kernel(pop, conc, phi, perm, dm, charge, fluid, owner_two, yl, yh, xl, xh,
                    pop_out, phi_out, conc_out, charge_out, y_hi, y_lo, dm_out, rim, coef, inv, fl,
                    pe, pa, pb, ce, dn, mm, cc, vel, sh, lv):
    msgs = (xl, xh, yl, yh)
    lay(pe, perm[...], "perm", 6, DEEP, ONE, xl, xh, yl, yh)

    def coefs(x, _):
        mid = pe[x]
        faces = [0.5 * (mid + other) for other in (
            pe[x - 1], pe[x + 1], turn(mid, 1, 0), turn(mid, -1, 0), turn(mid, 1, 1), turn(mid, -1, 1))]
        over = 1.0 / (faces[0] + faces[1] + faces[2] + faces[3] + faces[4] + faces[5])
        inv[x] = over
        for k in range(6):
            coef[k, x] = faces[k] * over
        return 0

    lax.fori_loop(1, 19, coefs, 0, unroll=6)
    fl[1:9, 8:24] = fluid[...]
    x, y = ONE.x, ONE.y
    for msg, p in ((xl, 0), (xh, 9)):
        fl[p, 8:24] = msg[x["fluid"]]
        fl[p, 7:8] = msg[x["cmisc"], 0:1]
        fl[p, 24:25] = msg[x["cmisc"], 8:9]
    fl[1:9, 7:8] = yl[:, y["fluid"] : y["fluid"] + 1]
    fl[1:9, 24:25] = yh[:, y["fluid"] : y["fluid"] + 1]
    lay_all(ONE, phi, conc, dm, charge, msgs, pa, ce, dn, mm, cc)
    fin = sweeps(coef, inv, ce, pa, pb)
    phi_out[...] = fin[6:14, MID_T]
    rim[0:2] = fin[4:6, MID_T]
    rim[2:4] = fin[14:16, MID_T]
    motion(fin, ce, fl, dn, mm, vel, sh)

    def store(s, x, values):
        conc_out[s, x] = values

    ions(fin, fl, cc, vel, store)
    collide_and_stream(ONE, pop, fl, sh, msgs, lv, pop_out, dm_out)
    charge_out[...] = conc_out[0] - conc_out[1]
    above = yh[0, y["owner"] : y["owner"] + 1]
    for low, yo, owner in ((False, y_hi, owner_two[0:1]), (True, y_lo, above)):
        pack_y(TWO, yo, low, owner, phi_out, charge_out, conc_out, pop_out, dm_out)


def ions_two_kernel(conc, phi, charge, dm, rim, coef, inv, fl, yl, yh, xl, xh,
                    phi_out, slab, sh, pa, pb, ce, dn, mm, cc, vel):
    lay_all(TWO, phi, conc, dm, charge, (xl, xh, yl, yh), pa, ce, dn, mm, cc)
    pa[4:6, MID_T] = rim[0:2]
    pa[14:16, MID_T] = rim[2:4]
    fin = sweeps(coef, inv, ce, pa, pb)
    phi_out[...] = fin[6:14, MID_T]
    motion(fin, ce, fl, dn, mm, vel, sh)

    def store(s, x, values):
        slab[s * CX + x] = values

    ions(fin, fl, cc, vel, store)
    slab[2 * CX, 0:8] = jnp.broadcast_to(yl[0, TWO.y["owner"] : TWO.y["owner"] + 1], (8, NZ))


def flow_two_kernel(pop, fl, sh, yl, yh, xl, xh, pop_out, lv):
    collide_and_stream(TWO, pop, fl, sh, (xl, xh, yl, yh), lv, pop_out, None)


def route_kernel(mine, other, yh, owner, owner_two, out, wanted):
    me = lax.axis_index("gy")
    wanted[0] = owner[...]
    wanted[1, 0:1] = yh[0, TWO.y["owner"] : TWO.y["owner"] + 1]
    wanted[2] = other[2 * CX, 0:8]
    wanted[3] = owner_two[...]
    row = jnp.full((1, NZ), me, jnp.int32).astype(F32)
    for k in range(4):
        pick = wanted[lax.rem(k - me // 2 + 4, 4), 0:1] == row
        for x in range(2 * CX):
            out[k, x] = jnp.where(pick, mine[x], other[x])


def arrive_kernel(owner, came, out):
    me = lax.axis_index("gy")
    away = lax.rem(me - owner[0, 0] + 8, 8)
    out[...] = came[lax.rem(me // 2 - away // 2 + 4, 4)]


VMEM, FAR, SMEM = (pl.BlockSpec(memory_space=m) for m in (pltpu.VMEM, pltpu.HBM, pltpu.SMEM))


def call(kernel, outs, args, scratch=(), specs=None, flops=0):
    return pl.pallas_call(
        kernel,
        out_shape=outs,
        in_specs=specs or [VMEM] * len(args),
        out_specs=[VMEM] * len(outs),
        scratch_shapes=[pltpu.VMEM(s, F32) if isinstance(s, tuple) else s for s in scratch],
        compiler_params=pltpu.CompilerParams(vmem_limit_bytes=24 * 1024 * 1024),
        cost_estimate=pl.CostEstimate(flops=flops, bytes_accessed=0, transcendentals=0) if flops else None,
    )(*args)


HALO = (EX, EY, NZ)
RIM = (10, EY, NZ)
FIELDS = (HALO, HALO, HALO, RIM, (3,) + RIM, (2,) + RIM, (3,) + RIM)


def shift(values, axis, by):
    n = lax.axis_size(axis)
    return lax.ppermute(values, axis, [(i, (i + by) % n) for i in range(n)])


def body(populations, concentration, potential, permittivity, fluid_mask, owners):
    block, row = shape(CX, CY, NZ), shape(8, NZ)
    pops, both, four = shape(19, CX, CY, NZ), shape(2, CX, CY, NZ), shape(4, CX, CY, NZ)
    y_one, y_two = (shape(CX, plan.y_rows, NZ) for plan in (ONE, TWO))
    x_one, x_two = (shape(plan.x_planes, CY, NZ) for plan in (ONE, TWO))
    y_hi, y_lo, dm, charge, fluid, owner = call(
        first_kernel, (y_one, y_one, four, block, block, row),
        (owners,) + tuple(pltpu.with_memory_space_constraint(v, pltpu.HBM) for v in (
            populations, concentration, potential, permittivity, fluid_mask)),
        (pops.shape, both.shape, block.shape, block.shape, pltpu.VMEM(block.shape, jnp.int32),
         pltpu.SemaphoreType.DMA((5,))),
        [SMEM] + [FAR] * 5)
    yl, yh = shift(y_hi, "gy", 1), shift(y_lo, "gy", -1)
    x_hi, x_lo, owner_one = call(
        x_one_kernel, (x_one, x_one, row),
        (potential, charge, concentration, populations, dm, permittivity, fluid, yl, yh))
    owner_two = shift(owner_one, "gy", 1)
    xl, xh = shift(x_hi, "gx", 1), shift(x_lo, "gx", -1)
    pop, phi, conc, charge, y_hi, y_lo, dm, rim, coef, inv, fl = call(
        step_one_kernel,
        (pops, block, both, block, y_two, y_two, four, shape(4, CY, NZ), shape(6, *HALO), shape(*HALO), shape(*RIM)),
        (populations, concentration, potential, permittivity, dm, charge, fluid, owner_two, yl, yh, xl, xh),
        (HALO,) + FIELDS + ((5,) + RIM, (19,) + RIM))
    yl, yh = shift(y_hi, "gy", 1), shift(y_lo, "gy", -1)
    x_hi, x_lo = call(x_two_kernel, (x_two, x_two), (phi, charge, conc, pop, dm, yl, yh))
    xl, xh = shift(x_hi, "gx", 1), shift(x_lo, "gx", -1)
    phi, mine, sh = call(
        ions_two_kernel, (block, shape(2 * CX + 1, CY, NZ), shape(5, *RIM)),
        (conc, phi, charge, dm, rim, coef, inv, fl, yl, yh, xl, xh), FIELDS)
    other = shift(mine, "gy", 1)
    (pop,) = call(flow_two_kernel, (pops,), (pop, fl, sh, yl, yh, xl, xh), ((19,) + RIM,), flops=40_000_000)
    (routed,) = call(
        route_kernel, (shape(4, 2 * CX, CY, NZ),), (mine, other, yh, owner, owner_two), ((4, 8, NZ),))
    came = lax.all_to_all(
        routed, "gy", 0, 0, axis_index_groups=[[0, 2, 4, 6], [1, 3, 5, 7]], tiled=True)
    (migrated,) = call(arrive_kernel, (shape(2 * CX, CY, NZ),), (owners, came), (), [SMEM, VMEM])
    return (pop, phi, migrated.reshape(2, CX, CY, NZ))


def solution(mesh):
    in_specs = (
        P(None, "gx", "gy", None),
        P(None, "gx", "gy", None),
        P("gx", "gy", None),
        P("gx", "gy", None),
        P("gx", "gy", None),
        P("gx", "gy"),
    )
    out_specs = (P(None, "gx", "gy", None), P("gx", "gy", None), P(None, "gx", "gy", None))
    return jax.shard_map(body, mesh=mesh, in_specs=in_specs, out_specs=out_specs, check_vma=False)
```

```python
import jax
import jax.numpy as jnp
from jax import lax
from jax.experimental import pallas as pl
from jax.experimental.pallas import tpu as pltpu
from jax.sharding import PartitionSpec as P

STEPS = 2
SWEEPS = 4
VEL = (
    (0, 0, 0), (1, 0, 0), (-1, 0, 0), (0, 1, 0), (0, -1, 0), (0, 0, 1), (0, 0, -1),
    (1, 1, 0), (-1, -1, 0), (1, -1, 0), (-1, 1, 0), (1, 0, 1), (-1, 0, -1), (1, 0, -1),
    (-1, 0, 1), (0, 1, 1), (0, -1, -1), (0, 1, -1), (0, -1, 1),
)
WEIGHT = (1.0 / 3.0,) + (1.0 / 18.0,) * 6 + (1.0 / 36.0,) * 12
OPP = (0, 2, 1, 4, 3, 6, 5, 8, 7, 10, 9, 12, 11, 14, 13, 16, 15, 18, 17)
TAU = 0.8
COUPLING = 0.05
DRIVE = 0.001
DIFF = (0.1, 0.15)
VALENCE = (1.0, -1.0)

CX, CY, NZ = 8, 16, 128
EX, EY = 20, 32
F32 = jnp.float32

X_IN_LO = tuple(i for i in range(19) if VEL[i][0] == 1)
X_IN_HI = tuple(i for i in range(19) if VEL[i][0] == -1)
Y_IN_LO = tuple(i for i in range(19) if VEL[i][1] == 1)
Y_IN_HI = tuple(i for i in range(19) if VEL[i][1] == -1)
LO_LO, HI_LO = VEL.index((1, 1, 0)), VEL.index((-1, 1, 0))
LO_HI, HI_HI = VEL.index((1, -1, 0)), VEL.index((-1, -1, 0))


def shape(*dims):
    return jax.ShapeDtypeStruct(dims, F32)


def turn(v, by, axis):
    return pltpu.roll(v, by % v.shape[axis], axis)


class Plan:
    def __init__(self, first):
        self.first = first
        rows = [("phi", 6)] + [("perm", 6)] * first + [("charge", 4), ("conc", 2)] + [("fluid", 1)] * first
        self.y = {}
        at = 0
        for name, n in rows + [("pop", 5), ("dm", 4)] + [("owner", 1)] * (not first):
            self.y[name] = at
            at += n
        self.y_rows = -(-at // 8) * 8
        self.skip = 0 if first else 2
        planes = [("phi", 6 - self.skip)] + [("perm", 6)] * first + [("charge", 4), ("conc", 2)]
        planes += [("fluid", 1)] * first + [("pop", 5), ("dm", 4)]
        self.x = {}
        at = 0
        for name, n in planes:
            self.x[name] = at
            at += n
        self.x_planes = at
        self.c = {"phi": 0, "perm": 3, "charge": 3 + 3 * first, "misc": 5 + 3 * first}
        self.tiles = 6 + 3 * first


ONE, TWO = Plan(True), Plan(False)
DEEP = ((1, 6, 6, 1), (2, 5, 5, 2), (3, 4, 4, 3))
CHARGE = ((1, 5, 4, 2), (2, 4, 3, 3))


def pack_y(plan, out, low, owner, phi, charge, conc, pop, dm, perm=None, fluid=None):
    y = plan.y
    six = slice(0, 6) if low else slice(10, 16)
    four = slice(1, 5) if low else slice(11, 15)
    row = slice(0, 1) if low else slice(15, 16)
    out[:, 0:6] = phi[:, six]
    if plan.first:
        out[:, y["perm"] : y["perm"] + 6] = perm[:, six]
        out[:, y["fluid"] : y["fluid"] + 1] = fluid[:, row]
    out[:, y["charge"] : y["charge"] + 4] = charge[:, four]
    for s in range(2):
        out[:, y["conc"] + s : y["conc"] + s + 1] = conc[s, :, row]
    for k, i in enumerate(Y_IN_HI if low else Y_IN_LO):
        out[:, y["pop"] + k : y["pop"] + k + 1] = pop[i, :, row]
    for k in range(4):
        out[:, y["dm"] + k : y["dm"] + k + 1] = dm[k, :, row]
    if not plan.first:
        out[0, y["owner"] : y["owner"] + 1] = owner


def pack_x(plan, out, low, phi, charge, conc, pop, dm, perm=None, fluid=None):
    x = plan.x

    def spread(to, field, first, last):
        lo = first - 1 if low else CX - last
        out[to : to + last - first + 1] = field[lo : lo + last - first + 1]

    spread(0, phi, 1 + plan.skip, 6)
    spread(x["charge"], charge, 2, 5)
    edge = 0 if low else CX - 1
    for s in range(2):
        out[x["conc"] + s] = conc[s, edge]
    if plan.first:
        spread(x["perm"], perm, 1, 6)
        out[x["fluid"]] = fluid[edge]
    for k, i in enumerate(X_IN_HI if low else X_IN_LO):
        out[x["pop"] + k] = pop[i, edge]
    for k in range(4):
        out[x["dm"] + k] = dm[k, edge]


def pack_corners(plan, out, low, xl, xh, rim=None):
    x = plan.x

    def rows(n):
        return slice(0, n) if low else slice(16 - n, 16)

    for side, msg, names in ((0, xl, X_IN_LO), (1, xh, X_IN_HI)):
        base = side * plan.tiles

        def phi(d, r):
            if d <= plan.skip:
                return rim[1 + d if side else 2 - d, r]
            return msg[x["phi"] + (d - 1 - plan.skip if side else 6 - d), r]

        def perm(d, r):
            return msg[x["perm"] + (d - 1 if side else 6 - d), r]

        def charge(d, r):
            if d == 1:
                return msg[x["conc"], r] - msg[x["conc"] + 1, r]
            return msg[x["charge"] + (d - 2 if side else 5 - d), r]

        fields = [("phi", phi, DEEP), ("charge", charge, CHARGE)] + [("perm", perm, DEEP)] * plan.first
        for name, load, pairs in fields:
            for k, (d, n, e, m) in enumerate(pairs):
                tile = base + plan.c[name] + k
                if low:
                    out[tile, 0:n] = load(d, rows(n))
                    out[tile, 8 - m : 8] = load(e, rows(m))
                else:
                    out[tile, 8 - n : 8] = load(d, rows(n))
                    out[tile, 0:m] = load(e, rows(m))
        pick = (LO_HI, HI_HI)[side] if low else (LO_LO, HI_LO)[side]
        misc = base + plan.c["misc"]
        if plan.first:
            out[misc, 0:1] = msg[x["fluid"], rows(1)]
        out[misc, 1:2] = msg[x["pop"] + names.index(pick), rows(1)]
        for k in range(4):
            out[misc, 2 + k : 3 + k] = msg[x["dm"] + k, rows(1)]
        out[misc, 6:7] = charge(5, rows(1))


def lay(ext, own, name, plan, msgs):
    xl, xh, yl, yh, cl, ch = msgs
    x, y = plan.x, plan.y
    skip = plan.skip if name == "phi" else 0
    n = 6 - skip
    ext[6:14, 8:24] = own
    ext[0:n, 8:24] = xl[x[name] : x[name] + n]
    ext[14 + skip : 20, 8:24] = xh[x[name] : x[name] + n]
    ext[6:14, 2:8] = yl[:, y[name] : y[name] + 6]
    ext[6:14, 24:30] = yh[:, y[name] : y[name] + 6]
    corners(ext, plan, name, DEEP, cl, ch)


def corners(ext, plan, name, pairs, cl, ch):
    for k, (d, n, e, m) in enumerate(pairs):
        for side, p, q in ((0, 6 - d, 6 - e), (1, 13 + d, 13 + e)):
            tile = side * plan.tiles + plan.c[name] + k
            ext[p, 8 - n : 8] = cl[tile, 8 - n : 8]
            ext[q, 8 - m : 8] = cl[tile, 0:m]
            ext[p, 24 : 24 + n] = ch[tile, 0:n]
            ext[q, 24 : 24 + m] = ch[tile, 8 - m : 8]


def moments(load):
    dens = load(0)
    mom = [None, None, None]
    for i in range(1, 19):
        v = load(i)
        dens = dens + v
        for c in range(3):
            if VEL[i][c]:
                t = v if VEL[i][c] > 0 else -v
                mom[c] = t if mom[c] is None else mom[c] + t
    return [dens] + mom


def first_kernel(*refs):
    far, near, sems = refs[:5], refs[12:17], refs[17]
    pop, conc, phi, perm, mask = near
    x_hi, x_lo, y_hi, y_lo, dm, charge, fluid = refs[5:12]
    copies = [pltpu.make_async_copy(a, b, sems.at[k]) for k, (a, b) in enumerate(zip(far, near))]
    for copy in copies:
        copy.start()
    for copy in copies:
        copy.wait()
    charge[...] = conc[0] - conc[1]
    fluid[...] = mask[...].astype(F32)

    def plane(x, _):
        for k, v in enumerate(moments(lambda i: pop[i, x])):
            dm[k, x] = v
        return 0

    lax.fori_loop(0, CX, plane, 0, unroll=2)
    for low, xo, yo in ((False, x_hi, y_hi), (True, x_lo, y_lo)):
        pack_x(ONE, xo, low, phi, charge, conc, pop, dm, perm, fluid)
        pack_y(ONE, yo, low, None, phi, charge, conc, pop, dm, perm, fluid)


def corner_one_kernel(xl, xh, c_hi, c_lo):
    pack_corners(ONE, c_hi, False, xl, xh)
    pack_corners(ONE, c_lo, True, xl, xh)


def corner_two_kernel(xl, xh, rim, c_hi, c_lo):
    pack_corners(TWO, c_hi, False, xl, xh, rim)
    pack_corners(TWO, c_lo, True, xl, xh, rim)


def lay_all(plan, phi, conc, dm, charge, msgs, pa, ce, dn, mm, cc):
    xl, xh, yl, yh, cl, ch = msgs
    x, y = plan.x, plan.y
    lay(pa, phi[...], "phi", plan, msgs)
    ce[6:14, 8:24] = charge[...]
    q = x["charge"]
    ce[1:5, 8:24] = xl[q : q + 4]
    ce[15:19, 8:24] = xh[q : q + 4]
    c = x["conc"]
    ce[5, 8:24] = xl[c] - xl[c + 1]
    ce[14, 8:24] = xh[c] - xh[c + 1]
    q, c = y["charge"], y["conc"]
    ce[6:14, 3:7] = yl[:, q : q + 4]
    ce[6:14, 7:8] = yl[:, c : c + 1] - yl[:, c + 1 : c + 2]
    ce[6:14, 24:25] = yh[:, c : c + 1] - yh[:, c + 1 : c + 2]
    ce[6:14, 25:29] = yh[:, q : q + 4]
    corners(ce, plan, "charge", CHARGE, cl, ch)
    misc = plan.c["misc"], plan.tiles + plan.c["misc"]
    for m, p in zip(misc, (1, 18)):
        ce[p, 7:8] = cl[m, 6:7]
        ce[p, 24:25] = ch[m, 6:7]
    for s in range(2):
        cc[s, 1:9, 8:24] = conc[s]
        cc[s, 0, 8:24] = xl[x["conc"] + s]
        cc[s, 9, 8:24] = xh[x["conc"] + s]
        cc[s, 1:9, 7:8] = yl[:, c + s : c + s + 1]
        cc[s, 1:9, 24:25] = yh[:, c + s : c + s + 1]
    for k, ext in enumerate((dn, mm.at[0], mm.at[1], mm.at[2])):
        ext[1:9, 8:24] = dm[k]
        for msg, m, p in ((xl, misc[0], 0), (xh, misc[1], 9)):
            ext[p, 8:24] = msg[x["dm"] + k]
            ext[p, 7:8] = cl[m, 2 + k : 3 + k]
            ext[p, 24:25] = ch[m, 2 + k : 3 + k]
        for msg, r in ((yl, 7), (yh, 24)):
            ext[1:9, r : r + 1] = msg[:, y["dm"] + k : y["dm"] + k + 1]


LO_T, MID_T, HI_T = slice(0, 8), slice(8, 24), slice(24, 32)


def sweeps(coef, inv, ce, src, dst):
    for sweep in range(SWEEPS):

        def relax(x, _, src=src, dst=dst):
            mid = src[x]
            acc = ce[x] * inv[x]
            acc += coef[0, x] * src[x - 1] + coef[1, x] * src[x + 1]
            acc += coef[2, x] * turn(mid, 1, 0) + coef[3, x] * turn(mid, -1, 0)
            acc += coef[4, x] * turn(mid, 1, 1) + coef[5, x] * turn(mid, -1, 1)
            dst[x] = acc
            return 0

        lax.fori_loop(1 + sweep, 19 - sweep, relax, 0, unroll=6)
        src, dst = dst, src
    return src


def motion(fin, ce, fl, dn, mm, vel, sh):
    def plane(p, _):
        mid = fin[p + 5]
        grad = [
            -0.5 * (fin[p + 6] - fin[p + 4]),
            -0.5 * (turn(mid, -1, 0) - turn(mid, 1, 0)),
            -0.5 * (turn(mid, -1, 1) - turn(mid, 1, 1)),
        ]
        f = fl[p]
        scale = COUPLING * ce[p + 5]
        force = [f * (scale * g + d) if d else f * (scale * g) for g, d in zip(grad, (DRIVE, 0, 0))]
        dens = dn[p]
        over = 1.0 / dens
        mom = [mm[c, p] for c in range(3)]
        for c in range(3):
            vel[c, p] = f * (mom[c] + 0.5 * force[c]) * over
        u = [(mom[c] + TAU * force[c]) * over for c in range(3)]
        for c in range(3):
            sh[c, p] = u[c]
        sh[3, p] = 1.0 - 1.5 * (u[0] * u[0] + u[1] * u[1] + u[2] * u[2])
        sh[4, p] = dens * (1.0 / TAU)
        return 0

    lax.fori_loop(0, 10, plane, 0, unroll=2)


def ions(fin, fl, cc, vel, store):
    def flux(s, ca, cb, pot_a, pot_b, ua, ub, wall):
        total = ca + cb
        speed = 0.25 * (ua + ub) - (0.5 * DIFF[s] * VALENCE[s]) * (pot_b - pot_a)
        return wall * (total * speed - DIFF[s] * (cb - ca))

    def x_face(s, p):
        wall = fl[p, MID_T] * fl[p + 1, MID_T]
        return flux(s, cc[s, p, MID_T], cc[s, p + 1, MID_T], fin[p + 5, MID_T], fin[p + 6, MID_T],
                    vel[0, p, MID_T], vel[0, p + 1, MID_T], wall)

    def plane(p, before):
        after = []
        f, pot, vy = fl[p], fin[p + 5], vel[1, p]
        for s in range(2):
            face = x_face(s, p)
            total = face - before[s]
            after.append(face)
            c = cc[s, p]
            face = flux(s, c, turn(c, -1, 0), pot, turn(pot, -1, 0), vy, turn(vy, -1, 0), f * turn(f, -1, 0))
            total = total + (face - turn(face, 1, 0))[MID_T]
            fm, cm, pm, vz = f[MID_T], c[MID_T], pot[MID_T], vel[2, p, MID_T]
            face = flux(s, cm, turn(cm, -1, 1), pm, turn(pm, -1, 1), vz, turn(vz, -1, 1), fm * turn(fm, -1, 1))
            total = total + face - turn(face, 1, 1)
            store(s, p - 1, cm - total)
        return tuple(after)

    lax.fori_loop(1, 9, plane, (x_face(0, 0), x_face(1, 0)), unroll=4)


def collide_and_stream(plan, pop, fl, sh, msgs, lv, pop_out, dm_out):
    xl, xh, yl, yh, cl, ch = msgs
    y_pop, x_pop = plan.y["pop"], plan.x["pop"]
    bad = float("nan")

    def load(p, rows):
        return [sh[c, p, rows] for c in range(5)] + [fl[p, rows] != 0.0]

    def relaxed_of(i, pop_i, part):
        pr = None
        for c in range(3):
            if VEL[i][c]:
                t = part[c] if VEL[i][c] > 0 else -part[c]
                pr = t if pr is None else pr + t
        poly = part[3]
        if pr is not None:
            poly = poly + pr * (3.0 + 4.5 * pr)
        return (1.0 - 1.0 / TAU) * pop_i + (WEIGHT[i] * part[4]) * poly

    def collide(p, _):
        x = p - 1
        part = load(p, MID_T)
        wet = part[5]
        for i in range(19):
            j = OPP[i]
            if i > j:
                continue
            pi = pop[i, x]
            ri = relaxed_of(i, pi, part)
            if i == j:
                pop_out[i, x] = jnp.where(wet, ri, pi)
                continue
            pj = pop[j, x]
            rj = relaxed_of(j, pj, part)
            lv[i, p, MID_T] = jnp.where(wet, ri, bad)
            lv[j, p, MID_T] = jnp.where(wet, rj, bad)
            pop_out[i, x] = jnp.where(wet, rj, pi)
            pop_out[j, x] = jnp.where(wet, ri, pj)
        for y, names, r in ((yl, Y_IN_LO, 7), (yh, Y_IN_HI, 24)):
            row = slice(r, r + 1)
            part = load(p, row)
            for k, i in enumerate(names):
                value = relaxed_of(i, y[x, y_pop + k : y_pop + k + 1], part)
                lv[i, p, row] = jnp.where(part[5], value, bad)
        return 0

    lax.fori_loop(1, 9, collide, 0)
    for p, side, x, names, low_pop, high_pop in (
        (0, 0, xl, X_IN_LO, LO_LO, LO_HI),
        (9, 1, xh, X_IN_HI, HI_LO, HI_HI),
    ):
        misc = side * plan.tiles + plan.c["misc"]
        part = load(p, MID_T)
        for k, i in enumerate(names):
            lv[i, p, MID_T] = jnp.where(part[5], relaxed_of(i, x[x_pop + k], part), bad)
        for c, r, i in ((cl, 7, low_pop), (ch, 24, high_pop)):
            row = slice(r, r + 1)
            part = load(p, row)
            lv[i, p, row] = jnp.where(part[5], relaxed_of(i, c[misc, 1:2], part), bad)

    def stream(x, _):
        wet = fl[x + 1, MID_T] != 0.0
        for i in range(1, 19):
            ex, ey, ez = VEL[i]
            came = lv[i, x + 1 - ex, 8 - ey : 24 - ey]
            if ez:
                came = turn(came, ez, 1)
            pop_out[i, x] = jnp.where(wet & (came == came), came, pop_out[i, x])
        if dm_out is not None:
            for k, v in enumerate(moments(lambda i: pop_out[i, x])):
                dm_out[k, x] = v
        return 0

    lax.fori_loop(0, CX, stream, 0, unroll=2)


def step_one_kernel(owner, pop, conc, phi, perm, dm, charge, fluid, xl, xh, yl, yh, cl, ch,
                    pop_out, phi_out, conc_out, charge_out, x_hi, x_lo, y_hi, y_lo, dm_out, rim, coef, inv, fl, owner_row,
                    pe, pa, pb, ce, dn, mm, cc, vel, sh, lv):
    msgs = (xl, xh, yl, yh, cl, ch)
    owner_row[...] = jnp.full((8, NZ), owner[0, 0], jnp.int32).astype(F32)
    lay(pe, perm[...], "perm", ONE, msgs)

    def coefs(x, _):
        mid = pe[x]
        faces = [0.5 * (mid + other) for other in (
            pe[x - 1], pe[x + 1], turn(mid, 1, 0), turn(mid, -1, 0), turn(mid, 1, 1), turn(mid, -1, 1))]
        over = 1.0 / (faces[0] + faces[1] + faces[2] + faces[3] + faces[4] + faces[5])
        inv[x] = over
        for k in range(6):
            coef[k, x] = faces[k] * over
        return 0

    lax.fori_loop(1, 19, coefs, 0, unroll=6)
    fl[1:9, 8:24] = fluid[...]
    x, y = ONE.x, ONE.y
    for side, msg, p in ((0, xl, 0), (1, xh, 9)):
        m = side * ONE.tiles + ONE.c["misc"]
        fl[p, 8:24] = msg[x["fluid"]]
        fl[p, 7:8] = cl[m, 0:1]
        fl[p, 24:25] = ch[m, 0:1]
    fl[1:9, 7:8] = yl[:, y["fluid"] : y["fluid"] + 1]
    fl[1:9, 24:25] = yh[:, y["fluid"] : y["fluid"] + 1]
    lay_all(ONE, phi, conc, dm, charge, msgs, pa, ce, dn, mm, cc)
    fin = sweeps(coef, inv, ce, pa, pb)
    phi_out[...] = fin[6:14, MID_T]
    rim[0:2] = fin[4:6, MID_T]
    rim[2:4] = fin[14:16, MID_T]
    motion(fin, ce, fl, dn, mm, vel, sh)

    def store(s, x, values):
        conc_out[s, x] = values

    ions(fin, fl, cc, vel, store)
    collide_and_stream(ONE, pop, fl, sh, msgs, lv, pop_out, dm_out)
    charge_out[...] = conc_out[0] - conc_out[1]
    for low, xo, yo in ((False, x_hi, y_hi), (True, x_lo, y_lo)):
        pack_x(TWO, xo, low, phi_out, charge_out, conc_out, pop_out, dm_out)
        pack_y(TWO, yo, low, owner_row[0:1], phi_out, charge_out, conc_out, pop_out, dm_out)


def ions_two_kernel(conc, phi, charge, dm, rim, coef, inv, fl, xl, xh, yl, yh, cl, ch,
                    phi_out, slab, sh, pa, pb, ce, dn, mm, cc, vel):
    lay_all(TWO, phi, conc, dm, charge, (xl, xh, yl, yh, cl, ch), pa, ce, dn, mm, cc)
    pa[4:6, MID_T] = rim[0:2]
    pa[14:16, MID_T] = rim[2:4]
    fin = sweeps(coef, inv, ce, pa, pb)
    phi_out[...] = fin[6:14, MID_T]
    motion(fin, ce, fl, dn, mm, vel, sh)

    def store(s, x, values):
        for k in range(4):
            slab[k, s * CX + x] = values

    ions(fin, fl, cc, vel, store)


def flow_two_kernel(pop, fl, sh, xl, xh, yl, yh, cl, ch, pop_out, lv):
    collide_and_stream(TWO, pop, fl, sh, (xl, xh, yl, yh, cl, ch), lv, pop_out, None)


def chip_of(slab):
    return jnp.floor(slab * 0.5)


def choose(came, chip, x):
    v = came[0, x]
    for k in range(1, 4):
        v = jnp.where(chip == float(k), came[k, x], v)
    return v


def route_kernel(came, yl, yh, out):
    o = TWO.y["owner"]
    mate = jnp.where(lax.rem(lax.axis_index("gy"), 2) == 0, yh[0, o : o + 1], yl[0, o : o + 1])
    for x in range(2 * CX):
        out[x] = choose(came, chip_of(mate), x)


def arrive_kernel(came, crossed, owner, out):
    slab = owner[0:1]
    core = jnp.full((1, NZ), lax.rem(lax.axis_index("gy"), 2), jnp.int32).astype(F32)
    here = slab - 2.0 * chip_of(slab) == core
    for x in range(2 * CX):
        out[x] = jnp.where(here, choose(came, chip_of(slab), x), crossed[x])


VMEM, FAR, SMEM = (pl.BlockSpec(memory_space=m) for m in (pltpu.VMEM, pltpu.HBM, pltpu.SMEM))


def call(kernel, outs, args, scratch=(), specs=None, flops=0):
    return pl.pallas_call(
        kernel,
        out_shape=outs,
        in_specs=specs or [VMEM] * len(args),
        out_specs=[VMEM] * len(outs),
        scratch_shapes=[pltpu.VMEM(s, F32) if isinstance(s, tuple) else s for s in scratch],
        compiler_params=pltpu.CompilerParams(vmem_limit_bytes=24 * 1024 * 1024),
        cost_estimate=pl.CostEstimate(flops=flops, bytes_accessed=0, transcendentals=0) if flops else None,
    )(*args)


HALO = (EX, EY, NZ)
RIM = (10, EY, NZ)
FIELDS = (HALO, HALO, HALO, RIM, (3,) + RIM, (2,) + RIM, (3,) + RIM)


def shift(values, axis, by):
    n = lax.axis_size(axis)
    return lax.ppermute(values, axis, [(i, (i + by) % n) for i in range(n)])


def exchange(x_hi, x_lo, y_hi, y_lo):
    yl, yh = shift(y_hi, "gy", 1), shift(y_lo, "gy", -1)
    xl, xh = shift(x_hi, "gx", 1), shift(x_lo, "gx", -1)
    return xl, xh, yl, yh


def body(populations, concentration, potential, permittivity, fluid_mask, owners):
    block, row = shape(CX, CY, NZ), shape(8, NZ)
    pops, both, four = shape(19, CX, CY, NZ), shape(2, CX, CY, NZ), shape(4, CX, CY, NZ)

    def messages(plan):
        x, y = shape(plan.x_planes, CY, NZ), shape(CX, plan.y_rows, NZ)
        return (x, x, y, y)

    def tiles(plan):
        return (shape(2 * plan.tiles, 8, NZ),) * 2

    *sent, dm, charge, fluid = call(
        first_kernel, messages(ONE) + (four, block, block),
        tuple(pltpu.with_memory_space_constraint(v, pltpu.HBM) for v in (
            populations, concentration, potential, permittivity, fluid_mask)),
        (pops.shape, both.shape, block.shape, block.shape, pltpu.VMEM(block.shape, jnp.int32),
         pltpu.SemaphoreType.DMA((5,))),
        [FAR] * 5)
    got = exchange(*sent)
    c_hi, c_lo = call(corner_one_kernel, tiles(ONE), got[:2])
    got += (shift(c_hi, "gy", 1), shift(c_lo, "gy", -1))
    pop, phi, conc, charge, *rest = call(
        step_one_kernel,
        (pops, block, both, block) + messages(TWO)
        + (four, shape(4, CY, NZ), shape(6, *HALO), shape(*HALO), shape(*RIM), row),
        (owners, populations, concentration, potential, permittivity, dm, charge, fluid) + got,
        (HALO,) + FIELDS + ((5,) + RIM, (19,) + RIM), [SMEM] + [VMEM] * 13)
    sent, (dm, rim, coef, inv, fl, owner) = rest[:4], rest[4:]
    got = exchange(*sent)
    c_hi, c_lo = call(corner_two_kernel, tiles(TWO), got[:2] + (rim,))
    got += (shift(c_hi, "gy", 1), shift(c_lo, "gy", -1))
    slab = shape(2 * CX, CY, NZ)
    phi, mine, sh = call(
        ions_two_kernel, (block, shape(4, *slab.shape), shape(5, *RIM)),
        (conc, phi, charge, dm, rim, coef, inv, fl) + got, FIELDS)
    (pop,) = call(flow_two_kernel, (pops,), (pop, fl, sh) + got, ((19,) + RIM,), flops=40_000_000)
    came = lax.all_to_all(
        mine, "gy", 0, 0, axis_index_groups=[[0, 2, 4, 6], [1, 3, 5, 7]], tiled=True)
    (cross,) = call(route_kernel, (slab,), (came, got[2], got[3]))
    crossed = lax.ppermute(cross, "gy", [(i, i ^ 1) for i in range(8)])
    (migrated,) = call(arrive_kernel, (slab,), (came, crossed, owner))
    return (pop, phi, migrated.reshape(2, CX, CY, NZ))


def solution(mesh):
    in_specs = (
        P(None, "gx", "gy", None),
        P(None, "gx", "gy", None),
        P("gx", "gy", None),
        P("gx", "gy", None),
        P("gx", "gy", None),
        P("gx", "gy"),
    )
    out_specs = (P(None, "gx", "gy", None), P("gx", "gy", None), P(None, "gx", "gy", None))
    return jax.shard_map(body, mesh=mesh, in_specs=in_specs, out_specs=out_specs, check_vma=False)
```

```python
import jax
import jax.numpy as jnp
from jax import lax
from jax.experimental import pallas as pl
from jax.experimental.pallas import tpu as pltpu
from jax.sharding import PartitionSpec as P

STEPS = 2
SWEEPS = 4
VEL = (
    (0, 0, 0), (1, 0, 0), (-1, 0, 0), (0, 1, 0), (0, -1, 0), (0, 0, 1), (0, 0, -1),
    (1, 1, 0), (-1, -1, 0), (1, -1, 0), (-1, 1, 0), (1, 0, 1), (-1, 0, -1), (1, 0, -1),
    (-1, 0, 1), (0, 1, 1), (0, -1, -1), (0, 1, -1), (0, -1, 1),
)
WEIGHT = (1.0 / 3.0,) + (1.0 / 18.0,) * 6 + (1.0 / 36.0,) * 12
OPP = (0, 2, 1, 4, 3, 6, 5, 8, 7, 10, 9, 12, 11, 14, 13, 16, 15, 18, 17)
TAU = 0.8
COUPLING = 0.05
DRIVE = 0.001
DIFF = (0.1, 0.15)
VALENCE = (1.0, -1.0)

CX, CY, NZ = 8, 16, 128
EX, EY = 20, 32
F32 = jnp.float32

X_IN_LO = tuple(i for i in range(19) if VEL[i][0] == 1)
X_IN_HI = tuple(i for i in range(19) if VEL[i][0] == -1)
Y_IN_LO = tuple(i for i in range(19) if VEL[i][1] == 1)
Y_IN_HI = tuple(i for i in range(19) if VEL[i][1] == -1)
LO_LO, HI_LO = VEL.index((1, 1, 0)), VEL.index((-1, 1, 0))
LO_HI, HI_HI = VEL.index((1, -1, 0)), VEL.index((-1, -1, 0))


def shape(*dims):
    return jax.ShapeDtypeStruct(dims, F32)


def turn(v, by, axis):
    return pltpu.roll(v, by % v.shape[axis], axis)


class Plan:
    def __init__(self, first):
        self.first = first
        rows = [("phi", 6)] + [("perm", 6)] * first + [("charge", 4), ("conc", 2)] + [("fluid", 1)] * first
        self.y = {}
        at = 0
        for name, n in rows + [("pop", 5), ("dm", 4)] + [("owner", 1)] * (not first):
            self.y[name] = at
            at += n
        self.y_rows = -(-at // 8) * 8
        self.skip = 0 if first else 2
        planes = [("phi", 6 - self.skip)] + [("perm", 6)] * first + [("charge", 4), ("conc", 2)]
        planes += [("fluid", 1)] * first + [("pop", 5), ("dm", 4)]
        self.x = {}
        at = 0
        for name, n in planes:
            self.x[name] = at
            at += n
        self.x_planes = at
        self.c = {"phi": 0, "perm": 3, "charge": 3 + 3 * first, "misc": 5 + 3 * first}
        self.tiles = 6 + 3 * first


ONE, TWO = Plan(True), Plan(False)
DEEP = ((1, 6, 6, 1), (2, 5, 5, 2), (3, 4, 4, 3))
CHARGE = ((1, 5, 4, 2), (2, 4, 3, 3))


def pack_y(plan, out, low, owner, phi, charge, conc, pop, dm, perm=None, fluid=None):
    y = plan.y
    six = slice(0, 6) if low else slice(10, 16)
    four = slice(1, 5) if low else slice(11, 15)
    row = slice(0, 1) if low else slice(15, 16)
    out[:, 0:6] = phi[:, six]
    if plan.first:
        out[:, y["perm"] : y["perm"] + 6] = perm[:, six]
        out[:, y["fluid"] : y["fluid"] + 1] = fluid[:, row]
    out[:, y["charge"] : y["charge"] + 4] = charge[:, four]
    for s in range(2):
        out[:, y["conc"] + s : y["conc"] + s + 1] = conc[s, :, row]
    for k, i in enumerate(Y_IN_HI if low else Y_IN_LO):
        out[:, y["pop"] + k : y["pop"] + k + 1] = pop[i, :, row]
    for k in range(4):
        out[:, y["dm"] + k : y["dm"] + k + 1] = dm[k, :, row]
    if not plan.first:
        out[0, y["owner"] : y["owner"] + 1] = owner


def pack_x(plan, out, low, phi, charge, conc, pop, dm, perm=None, fluid=None):
    x = plan.x

    def spread(to, field, first, last):
        lo = first - 1 if low else CX - last
        out[to : to + last - first + 1] = field[lo : lo + last - first + 1]

    spread(0, phi, 1 + plan.skip, 6)
    spread(x["charge"], charge, 2, 5)
    edge = 0 if low else CX - 1
    for s in range(2):
        out[x["conc"] + s] = conc[s, edge]
    if plan.first:
        spread(x["perm"], perm, 1, 6)
        out[x["fluid"]] = fluid[edge]
    for k, i in enumerate(X_IN_HI if low else X_IN_LO):
        out[x["pop"] + k] = pop[i, edge]
    for k in range(4):
        out[x["dm"] + k] = dm[k, edge]


def pack_corners(plan, out, low, xl, xh, rim=None):
    x = plan.x

    def rows(n):
        return slice(0, n) if low else slice(16 - n, 16)

    for side, msg, names in ((0, xl, X_IN_LO), (1, xh, X_IN_HI)):
        base = side * plan.tiles

        def phi(d, r):
            if d <= plan.skip:
                return rim[1 + d if side else 2 - d, r]
            return msg[x["phi"] + (d - 1 - plan.skip if side else 6 - d), r]

        def perm(d, r):
            return msg[x["perm"] + (d - 1 if side else 6 - d), r]

        def charge(d, r):
            if d == 1:
                return msg[x["conc"], r] - msg[x["conc"] + 1, r]
            return msg[x["charge"] + (d - 2 if side else 5 - d), r]

        fields = [("phi", phi, DEEP), ("charge", charge, CHARGE)] + [("perm", perm, DEEP)] * plan.first
        for name, load, pairs in fields:
            for k, (d, n, e, m) in enumerate(pairs):
                tile = base + plan.c[name] + k
                if low:
                    out[tile, 0:n] = load(d, rows(n))
                    out[tile, 8 - m : 8] = load(e, rows(m))
                else:
                    out[tile, 8 - n : 8] = load(d, rows(n))
                    out[tile, 0:m] = load(e, rows(m))
        pick = (LO_HI, HI_HI)[side] if low else (LO_LO, HI_LO)[side]
        misc = base + plan.c["misc"]
        if plan.first:
            out[misc, 0:1] = msg[x["fluid"], rows(1)]
        out[misc, 1:2] = msg[x["pop"] + names.index(pick), rows(1)]
        for k in range(4):
            out[misc, 2 + k : 3 + k] = msg[x["dm"] + k, rows(1)]
        out[misc, 6:7] = charge(5, rows(1))


def lay(ext, own, name, plan, msgs):
    xl, xh, yl, yh, cl, ch = msgs
    x, y = plan.x, plan.y
    skip = plan.skip if name == "phi" else 0
    n = 6 - skip
    ext[6:14, 8:24] = own
    ext[0:n, 8:24] = xl[x[name] : x[name] + n]
    ext[14 + skip : 20, 8:24] = xh[x[name] : x[name] + n]
    ext[6:14, 2:8] = yl[:, y[name] : y[name] + 6]
    ext[6:14, 24:30] = yh[:, y[name] : y[name] + 6]
    corners(ext, plan, name, DEEP, cl, ch)


def corners(ext, plan, name, pairs, cl, ch):
    for k, (d, n, e, m) in enumerate(pairs):
        for side, p, q in ((0, 6 - d, 6 - e), (1, 13 + d, 13 + e)):
            tile = side * plan.tiles + plan.c[name] + k
            ext[p, 8 - n : 8] = cl[tile, 8 - n : 8]
            ext[q, 8 - m : 8] = cl[tile, 0:m]
            ext[p, 24 : 24 + n] = ch[tile, 0:n]
            ext[q, 24 : 24 + m] = ch[tile, 8 - m : 8]


def moments(load):
    dens = load(0)
    mom = [None, None, None]
    for i in range(1, 19):
        v = load(i)
        dens = dens + v
        for c in range(3):
            if VEL[i][c]:
                t = v if VEL[i][c] > 0 else -v
                mom[c] = t if mom[c] is None else mom[c] + t
    return [dens] + mom


def first_kernel(*refs):
    far, near, sems = refs[:5], refs[12:17], refs[17]
    pop, conc, phi, perm, mask = near
    x_hi, x_lo, y_hi, y_lo, dm, charge, fluid = refs[5:12]
    copies = [pltpu.make_async_copy(a, b, sems.at[k]) for k, (a, b) in enumerate(zip(far, near))]
    for copy in copies:
        copy.start()
    for copy in copies:
        copy.wait()
    charge[...] = conc[0] - conc[1]
    fluid[...] = mask[...].astype(F32)

    def plane(x, _):
        for k, v in enumerate(moments(lambda i: pop[i, x])):
            dm[k, x] = v
        return 0

    lax.fori_loop(0, CX, plane, 0, unroll=2)
    for low, xo, yo in ((False, x_hi, y_hi), (True, x_lo, y_lo)):
        pack_x(ONE, xo, low, phi, charge, conc, pop, dm, perm, fluid)
        pack_y(ONE, yo, low, None, phi, charge, conc, pop, dm, perm, fluid)


def corner_one_kernel(xl, xh, c_hi, c_lo):
    pack_corners(ONE, c_hi, False, xl, xh)
    pack_corners(ONE, c_lo, True, xl, xh)


def corner_two_kernel(xl, xh, rim, c_hi, c_lo):
    pack_corners(TWO, c_hi, False, xl, xh, rim)
    pack_corners(TWO, c_lo, True, xl, xh, rim)


def lay_all(plan, phi, conc, dm, charge, msgs, pa, ce, dn, mm, cc):
    xl, xh, yl, yh, cl, ch = msgs
    x, y = plan.x, plan.y
    lay(pa, phi[...], "phi", plan, msgs)
    ce[6:14, 8:24] = charge[...]
    q = x["charge"]
    ce[1:5, 8:24] = xl[q : q + 4]
    ce[15:19, 8:24] = xh[q : q + 4]
    c = x["conc"]
    ce[5, 8:24] = xl[c] - xl[c + 1]
    ce[14, 8:24] = xh[c] - xh[c + 1]
    q, c = y["charge"], y["conc"]
    ce[6:14, 3:7] = yl[:, q : q + 4]
    ce[6:14, 7:8] = yl[:, c : c + 1] - yl[:, c + 1 : c + 2]
    ce[6:14, 24:25] = yh[:, c : c + 1] - yh[:, c + 1 : c + 2]
    ce[6:14, 25:29] = yh[:, q : q + 4]
    corners(ce, plan, "charge", CHARGE, cl, ch)
    misc = plan.c["misc"], plan.tiles + plan.c["misc"]
    for m, p in zip(misc, (1, 18)):
        ce[p, 7:8] = cl[m, 6:7]
        ce[p, 24:25] = ch[m, 6:7]
    for s in range(2):
        cc[s, 1:9, 8:24] = conc[s]
        cc[s, 0, 8:24] = xl[x["conc"] + s]
        cc[s, 9, 8:24] = xh[x["conc"] + s]
        cc[s, 1:9, 7:8] = yl[:, c + s : c + s + 1]
        cc[s, 1:9, 24:25] = yh[:, c + s : c + s + 1]
    for k, ext in enumerate((dn, mm.at[0], mm.at[1], mm.at[2])):
        ext[1:9, 8:24] = dm[k]
        for msg, m, p in ((xl, misc[0], 0), (xh, misc[1], 9)):
            ext[p, 8:24] = msg[x["dm"] + k]
            ext[p, 7:8] = cl[m, 2 + k : 3 + k]
            ext[p, 24:25] = ch[m, 2 + k : 3 + k]
        for msg, r in ((yl, 7), (yh, 24)):
            ext[1:9, r : r + 1] = msg[:, y["dm"] + k : y["dm"] + k + 1]


LO_T, MID_T, HI_T = slice(0, 8), slice(8, 24), slice(24, 32)


def sweeps(coef, inv, ce, src, dst):
    for sweep in range(SWEEPS):

        def relax(x, _, src=src, dst=dst):
            mid = src[x]
            acc = ce[x] * inv[x]
            acc += coef[0, x] * src[x - 1] + coef[1, x] * src[x + 1]
            acc += coef[2, x] * turn(mid, 1, 0) + coef[3, x] * turn(mid, -1, 0)
            acc += coef[4, x] * turn(mid, 1, 1) + coef[5, x] * turn(mid, -1, 1)
            dst[x] = acc
            return 0

        lax.fori_loop(1 + sweep, 19 - sweep, relax, 0, unroll=True)
        src, dst = dst, src
    return src


def motion(fin, ce, fl, dn, mm, vel, sh):
    def plane(p, _):
        mid = fin[p + 5]
        grad = [
            -0.5 * (fin[p + 6] - fin[p + 4]),
            -0.5 * (turn(mid, -1, 0) - turn(mid, 1, 0)),
            -0.5 * (turn(mid, -1, 1) - turn(mid, 1, 1)),
        ]
        f = fl[p]
        scale = COUPLING * ce[p + 5]
        force = [f * (scale * g + d) if d else f * (scale * g) for g, d in zip(grad, (DRIVE, 0, 0))]
        dens = dn[p]
        over = 1.0 / dens
        mom = [mm[c, p] for c in range(3)]
        for c in range(3):
            vel[c, p] = f * (mom[c] + 0.5 * force[c]) * over
        u = [(mom[c] + TAU * force[c]) * over for c in range(3)]
        for c in range(3):
            sh[c, p] = u[c]
        sh[3, p] = 1.0 - 1.5 * (u[0] * u[0] + u[1] * u[1] + u[2] * u[2])
        sh[4, p] = dens * (1.0 / TAU)
        return 0

    lax.fori_loop(0, 10, plane, 0, unroll=5)


def ions(fin, fl, cc, vel, store):
    def flux(s, ca, cb, pot_a, pot_b, ua, ub, wall):
        total = ca + cb
        speed = 0.25 * (ua + ub) - (0.5 * DIFF[s] * VALENCE[s]) * (pot_b - pot_a)
        return wall * (total * speed - DIFF[s] * (cb - ca))

    def x_face(s, p):
        wall = fl[p, MID_T] * fl[p + 1, MID_T]
        return flux(s, cc[s, p, MID_T], cc[s, p + 1, MID_T], fin[p + 5, MID_T], fin[p + 6, MID_T],
                    vel[0, p, MID_T], vel[0, p + 1, MID_T], wall)

    def plane(p, before):
        after = []
        f, pot, vy = fl[p], fin[p + 5], vel[1, p]
        for s in range(2):
            face = x_face(s, p)
            total = face - before[s]
            after.append(face)
            c = cc[s, p]
            face = flux(s, c, turn(c, -1, 0), pot, turn(pot, -1, 0), vy, turn(vy, -1, 0), f * turn(f, -1, 0))
            total = total + (face - turn(face, 1, 0))[MID_T]
            fm, cm, pm, vz = f[MID_T], c[MID_T], pot[MID_T], vel[2, p, MID_T]
            face = flux(s, cm, turn(cm, -1, 1), pm, turn(pm, -1, 1), vz, turn(vz, -1, 1), fm * turn(fm, -1, 1))
            total = total + face - turn(face, 1, 1)
            store(s, p - 1, cm - total)
        return tuple(after)

    lax.fori_loop(1, 9, plane, (x_face(0, 0), x_face(1, 0)), unroll=8)


def collide_and_stream(plan, pop, fl, sh, msgs, lv, pop_out, dm_out):
    xl, xh, yl, yh, cl, ch = msgs
    y_pop, x_pop = plan.y["pop"], plan.x["pop"]
    bad = float("nan")

    def load(p, rows):
        return [sh[c, p, rows] for c in range(5)] + [fl[p, rows] != 0.0]

    def relaxed_of(i, pop_i, part):
        pr = None
        for c in range(3):
            if VEL[i][c]:
                t = part[c] if VEL[i][c] > 0 else -part[c]
                pr = t if pr is None else pr + t
        poly = part[3]
        if pr is not None:
            poly = poly + pr * (3.0 + 4.5 * pr)
        return (1.0 - 1.0 / TAU) * pop_i + (WEIGHT[i] * part[4]) * poly

    def collide(p, _):
        x = p - 1
        part = load(p, MID_T)
        wet = part[5]
        for i in range(19):
            j = OPP[i]
            if i > j:
                continue
            pi = pop[i, x]
            ri = relaxed_of(i, pi, part)
            if i == j:
                pop_out[i, x] = jnp.where(wet, ri, pi)
                continue
            pj = pop[j, x]
            rj = relaxed_of(j, pj, part)
            lv[i, p, MID_T] = jnp.where(wet, ri, bad)
            lv[j, p, MID_T] = jnp.where(wet, rj, bad)
            pop_out[i, x] = jnp.where(wet, rj, pi)
            pop_out[j, x] = jnp.where(wet, ri, pj)
        for y, names, r in ((yl, Y_IN_LO, 7), (yh, Y_IN_HI, 24)):
            row = slice(r, r + 1)
            part = load(p, row)
            for k, i in enumerate(names):
                value = relaxed_of(i, y[x, y_pop + k : y_pop + k + 1], part)
                lv[i, p, row] = jnp.where(part[5], value, bad)
        return 0

    lax.fori_loop(1, 9, collide, 0)
    for p, side, x, names, low_pop, high_pop in (
        (0, 0, xl, X_IN_LO, LO_LO, LO_HI),
        (9, 1, xh, X_IN_HI, HI_LO, HI_HI),
    ):
        misc = side * plan.tiles + plan.c["misc"]
        part = load(p, MID_T)
        for k, i in enumerate(names):
            lv[i, p, MID_T] = jnp.where(part[5], relaxed_of(i, x[x_pop + k], part), bad)
        for c, r, i in ((cl, 7, low_pop), (ch, 24, high_pop)):
            row = slice(r, r + 1)
            part = load(p, row)
            lv[i, p, row] = jnp.where(part[5], relaxed_of(i, c[misc, 1:2], part), bad)

    def stream(x, _):
        wet = fl[x + 1, MID_T] != 0.0
        for i in range(1, 19):
            ex, ey, ez = VEL[i]
            came = lv[i, x + 1 - ex, 8 - ey : 24 - ey]
            if ez:
                came = turn(came, ez, 1)
            pop_out[i, x] = jnp.where(wet & (came == came), came, pop_out[i, x])
        if dm_out is not None:
            for k, v in enumerate(moments(lambda i: pop_out[i, x])):
                dm_out[k, x] = v
        return 0

    lax.fori_loop(0, CX, stream, 0, unroll=4)


def step_one_kernel(owner, pop, conc, phi, perm, dm, charge, fluid, xl, xh, yl, yh, cl, ch,
                    pop_out, phi_out, conc_out, charge_out, x_hi, x_lo, y_hi, y_lo, dm_out, rim, coef, inv, fl, owner_row,
                    pe, pa, pb, ce, dn, mm, cc, vel, sh, lv):
    msgs = (xl, xh, yl, yh, cl, ch)
    owner_row[...] = jnp.full((8, NZ), owner[0, 0], jnp.int32).astype(F32)
    lay(pe, perm[...], "perm", ONE, msgs)

    def coefs(x, _):
        mid = pe[x]
        faces = [0.5 * (mid + other) for other in (
            pe[x - 1], pe[x + 1], turn(mid, 1, 0), turn(mid, -1, 0), turn(mid, 1, 1), turn(mid, -1, 1))]
        over = 1.0 / (faces[0] + faces[1] + faces[2] + faces[3] + faces[4] + faces[5])
        inv[x] = over
        for k in range(6):
            coef[k, x] = faces[k] * over
        return 0

    lax.fori_loop(1, 19, coefs, 0, unroll=9)
    fl[1:9, 8:24] = fluid[...]
    x, y = ONE.x, ONE.y
    for side, msg, p in ((0, xl, 0), (1, xh, 9)):
        m = side * ONE.tiles + ONE.c["misc"]
        fl[p, 8:24] = msg[x["fluid"]]
        fl[p, 7:8] = cl[m, 0:1]
        fl[p, 24:25] = ch[m, 0:1]
    fl[1:9, 7:8] = yl[:, y["fluid"] : y["fluid"] + 1]
    fl[1:9, 24:25] = yh[:, y["fluid"] : y["fluid"] + 1]
    lay_all(ONE, phi, conc, dm, charge, msgs, pa, ce, dn, mm, cc)
    fin = sweeps(coef, inv, ce, pa, pb)
    phi_out[...] = fin[6:14, MID_T]
    rim[0:2] = fin[4:6, MID_T]
    rim[2:4] = fin[14:16, MID_T]
    motion(fin, ce, fl, dn, mm, vel, sh)

    def store(s, x, values):
        conc_out[s, x] = values

    ions(fin, fl, cc, vel, store)
    collide_and_stream(ONE, pop, fl, sh, msgs, lv, pop_out, dm_out)
    charge_out[...] = conc_out[0] - conc_out[1]
    for low, xo, yo in ((False, x_hi, y_hi), (True, x_lo, y_lo)):
        pack_x(TWO, xo, low, phi_out, charge_out, conc_out, pop_out, dm_out)
        pack_y(TWO, yo, low, owner_row[0:1], phi_out, charge_out, conc_out, pop_out, dm_out)


def ions_two_kernel(conc, phi, charge, dm, rim, coef, inv, fl, xl, xh, yl, yh, cl, ch,
                    phi_out, slab, sh, pa, pb, ce, dn, mm, cc, vel):
    lay_all(TWO, phi, conc, dm, charge, (xl, xh, yl, yh, cl, ch), pa, ce, dn, mm, cc)
    pa[4:6, MID_T] = rim[0:2]
    pa[14:16, MID_T] = rim[2:4]
    fin = sweeps(coef, inv, ce, pa, pb)
    phi_out[...] = fin[6:14, MID_T]
    motion(fin, ce, fl, dn, mm, vel, sh)

    def store(s, x, values):
        for k in range(4):
            slab[k, s * CX + x] = values

    ions(fin, fl, cc, vel, store)


def flow_two_kernel(pop, fl, sh, xl, xh, yl, yh, cl, ch, pop_out, mark, lv):
    mark[...] = fl[0, 8:16]
    collide_and_stream(TWO, pop, fl, sh, (xl, xh, yl, yh, cl, ch), lv, pop_out, None)


def chip_of(slab):
    return jnp.floor(slab * 0.5)


def choose(came, chip, x):
    v = came[0, x]
    for k in range(1, 4):
        v = jnp.where(chip == float(k), came[k, x], v)
    return v


def route_kernel(came, yl, yh, mark, out):
    o = TWO.y["owner"]
    mate = jnp.where(lax.rem(lax.axis_index("gy"), 2) == 0, yh[0, o : o + 1], yl[0, o : o + 1])
    for x in range(2 * CX):
        out[x] = choose(came, chip_of(mate), x)


def arrive_kernel(came, crossed, owner, out):
    slab = owner[0:1]
    core = jnp.full((1, NZ), lax.rem(lax.axis_index("gy"), 2), jnp.int32).astype(F32)
    here = slab - 2.0 * chip_of(slab) == core
    for x in range(2 * CX):
        out[x] = jnp.where(here, choose(came, chip_of(slab), x), crossed[x])


VMEM, FAR, SMEM = (pl.BlockSpec(memory_space=m) for m in (pltpu.VMEM, pltpu.HBM, pltpu.SMEM))


def call(kernel, outs, args, scratch=(), specs=None, flops=0):
    return pl.pallas_call(
        kernel,
        out_shape=outs,
        in_specs=specs or [VMEM] * len(args),
        out_specs=[VMEM] * len(outs),
        scratch_shapes=[pltpu.VMEM(s, F32) if isinstance(s, tuple) else s for s in scratch],
        compiler_params=pltpu.CompilerParams(vmem_limit_bytes=24 * 1024 * 1024),
        cost_estimate=pl.CostEstimate(flops=flops, bytes_accessed=0, transcendentals=0) if flops else None,
    )(*args)


HALO = (EX, EY, NZ)
RIM = (10, EY, NZ)
FIELDS = (HALO, HALO, HALO, RIM, (3,) + RIM, (2,) + RIM, (3,) + RIM)


def shift(values, axis, by):
    n = lax.axis_size(axis)
    return lax.ppermute(values, axis, [(i, (i + by) % n) for i in range(n)])


def exchange(x_hi, x_lo, y_hi, y_lo):
    yl, yh = shift(y_hi, "gy", 1), shift(y_lo, "gy", -1)
    xl, xh = shift(x_hi, "gx", 1), shift(x_lo, "gx", -1)
    return xl, xh, yl, yh


def body(populations, concentration, potential, permittivity, fluid_mask, owners):
    block, row = shape(CX, CY, NZ), shape(8, NZ)
    pops, both, four = shape(19, CX, CY, NZ), shape(2, CX, CY, NZ), shape(4, CX, CY, NZ)

    def messages(plan):
        x, y = shape(plan.x_planes, CY, NZ), shape(CX, plan.y_rows, NZ)
        return (x, x, y, y)

    def tiles(plan):
        return (shape(2 * plan.tiles, 8, NZ),) * 2

    *sent, dm, charge, fluid = call(
        first_kernel, messages(ONE) + (four, block, block),
        tuple(pltpu.with_memory_space_constraint(v, pltpu.HBM) for v in (
            populations, concentration, potential, permittivity, fluid_mask)),
        (pops.shape, both.shape, block.shape, block.shape, pltpu.VMEM(block.shape, jnp.int32),
         pltpu.SemaphoreType.DMA((5,))),
        [FAR] * 5)
    got = exchange(*sent)
    c_hi, c_lo = call(corner_one_kernel, tiles(ONE), got[:2])
    got += (shift(c_hi, "gy", 1), shift(c_lo, "gy", -1))
    pop, phi, conc, charge, *rest = call(
        step_one_kernel,
        (pops, block, both, block) + messages(TWO)
        + (four, shape(4, CY, NZ), shape(6, *HALO), shape(*HALO), shape(*RIM), row),
        (owners, populations, concentration, potential, permittivity, dm, charge, fluid) + got,
        (HALO,) + FIELDS + ((5,) + RIM, (19,) + RIM), [SMEM] + [VMEM] * 13)
    sent, (dm, rim, coef, inv, fl, owner) = rest[:4], rest[4:]
    got = exchange(*sent)
    c_hi, c_lo = call(corner_two_kernel, tiles(TWO), got[:2] + (rim,))
    got += (shift(c_hi, "gy", 1), shift(c_lo, "gy", -1))
    slab = shape(2 * CX, CY, NZ)
    phi, mine, sh = call(
        ions_two_kernel, (block, shape(4, *slab.shape), shape(5, *RIM)),
        (conc, phi, charge, dm, rim, coef, inv, fl) + got, FIELDS)
    pop, mark = call(flow_two_kernel, (pops, row), (pop, fl, sh) + got, ((19,) + RIM,), flops=40_000_000)
    came = lax.all_to_all(
        mine, "gy", 0, 0, axis_index_groups=[[0, 2, 4, 6], [1, 3, 5, 7]], tiled=True)
    (cross,) = call(route_kernel, (slab,), (came, got[2], got[3], mark))
    crossed = lax.ppermute(cross, "gy", [(i, i ^ 1) for i in range(8)])
    (migrated,) = call(arrive_kernel, (slab,), (came, crossed, owner))
    return (pop, phi, migrated.reshape(2, CX, CY, NZ))


def solution(mesh):
    in_specs = (
        P(None, "gx", "gy", None),
        P(None, "gx", "gy", None),
        P("gx", "gy", None),
        P("gx", "gy", None),
        P("gx", "gy", None),
        P("gx", "gy"),
    )
    out_specs = (P(None, "gx", "gy", None), P("gx", "gy", None), P(None, "gx", "gy", None))
    return jax.shard_map(body, mesh=mesh, in_specs=in_specs, out_specs=out_specs, check_vma=False)
```

```python
import jax
import jax.numpy as jnp
from jax import lax
from jax.experimental import pallas as pl
from jax.experimental.pallas import tpu as pltpu
from jax.sharding import PartitionSpec as P

STEPS = 2
SWEEPS = 4
VEL = (
    (0, 0, 0), (1, 0, 0), (-1, 0, 0), (0, 1, 0), (0, -1, 0), (0, 0, 1), (0, 0, -1),
    (1, 1, 0), (-1, -1, 0), (1, -1, 0), (-1, 1, 0), (1, 0, 1), (-1, 0, -1), (1, 0, -1),
    (-1, 0, 1), (0, 1, 1), (0, -1, -1), (0, 1, -1), (0, -1, 1),
)
WEIGHT = (1.0 / 3.0,) + (1.0 / 18.0,) * 6 + (1.0 / 36.0,) * 12
OPP = (0, 2, 1, 4, 3, 6, 5, 8, 7, 10, 9, 12, 11, 14, 13, 16, 15, 18, 17)
TAU = 0.8
COUPLING = 0.05
DRIVE = 0.001
DIFF = (0.1, 0.15)
VALENCE = (1.0, -1.0)

CX, CY, NZ = 8, 16, 128
EX, EY = 20, 32
F32 = jnp.float32

X_IN_LO = tuple(i for i in range(19) if VEL[i][0] == 1)
X_IN_HI = tuple(i for i in range(19) if VEL[i][0] == -1)
Y_IN_LO = tuple(i for i in range(19) if VEL[i][1] == 1)
Y_IN_HI = tuple(i for i in range(19) if VEL[i][1] == -1)
LO_LO, HI_LO = VEL.index((1, 1, 0)), VEL.index((-1, 1, 0))
LO_HI, HI_HI = VEL.index((1, -1, 0)), VEL.index((-1, -1, 0))


def shape(*dims):
    return jax.ShapeDtypeStruct(dims, F32)


def turn(v, by, axis):
    return pltpu.roll(v, by % v.shape[axis], axis)


class Plan:
    def __init__(self, first):
        self.first = first
        rows = [("phi", 6)] + [("perm", 6)] * first + [("charge", 4), ("conc", 2)] + [("fluid", 1)] * first
        self.y = {}
        at = 0
        for name, n in rows + [("pop", 5), ("dm", 4)] + [("owner", 1)] * (not first):
            self.y[name] = at
            at += n
        self.y_rows = -(-at // 8) * 8
        self.skip = 0 if first else 2
        planes = [("phi", 6 - self.skip)] + [("perm", 6)] * first + [("charge", 4), ("conc", 2)]
        planes += [("fluid", 1)] * first + [("pop", 5), ("dm", 4)]
        self.x = {}
        at = 0
        for name, n in planes:
            self.x[name] = at
            at += n
        self.x_planes = at
        self.c = {"phi": 0, "perm": 3, "charge": 3 + 3 * first, "misc": 5 + 3 * first}
        self.tiles = 6 + 3 * first


ONE, TWO = Plan(True), Plan(False)
DEEP = ((1, 6, 6, 1), (2, 5, 5, 2), (3, 4, 4, 3))
CHARGE = ((1, 5, 4, 2), (2, 4, 3, 3))


def pack_y(plan, out, low, owner, phi, charge, conc, pop, dm, perm=None, fluid=None):
    y = plan.y
    six = slice(0, 6) if low else slice(10, 16)
    four = slice(1, 5) if low else slice(11, 15)
    row = slice(0, 1) if low else slice(15, 16)
    out[:, 0:6] = phi[:, six]
    if plan.first:
        out[:, y["perm"] : y["perm"] + 6] = perm[:, six]
        out[:, y["fluid"] : y["fluid"] + 1] = fluid[:, row]
    out[:, y["charge"] : y["charge"] + 4] = charge[:, four]
    for s in range(2):
        out[:, y["conc"] + s : y["conc"] + s + 1] = conc[s, :, row]
    for k, i in enumerate(Y_IN_HI if low else Y_IN_LO):
        out[:, y["pop"] + k : y["pop"] + k + 1] = pop[i, :, row]
    for k in range(4):
        out[:, y["dm"] + k : y["dm"] + k + 1] = dm[k, :, row]
    if not plan.first:
        out[0, y["owner"] : y["owner"] + 1] = owner


def pack_x(plan, out, low, phi, charge, conc, pop, dm, perm=None, fluid=None):
    x = plan.x

    def spread(to, field, first, last):
        lo = first - 1 if low else CX - last
        out[to : to + last - first + 1] = field[lo : lo + last - first + 1]

    spread(0, phi, 1 + plan.skip, 6)
    spread(x["charge"], charge, 2, 5)
    edge = 0 if low else CX - 1
    for s in range(2):
        out[x["conc"] + s] = conc[s, edge]
    if plan.first:
        spread(x["perm"], perm, 1, 6)
        out[x["fluid"]] = fluid[edge]
    for k, i in enumerate(X_IN_HI if low else X_IN_LO):
        out[x["pop"] + k] = pop[i, edge]
    for k in range(4):
        out[x["dm"] + k] = dm[k, edge]


def pack_corners(plan, out, low, xl, xh, rim=None):
    x = plan.x

    def rows(n):
        return slice(0, n) if low else slice(16 - n, 16)

    for side, msg, names in ((0, xl, X_IN_LO), (1, xh, X_IN_HI)):
        base = side * plan.tiles

        def phi(d, r):
            if d <= plan.skip:
                return rim[1 + d if side else 2 - d, r]
            return msg[x["phi"] + (d - 1 - plan.skip if side else 6 - d), r]

        def perm(d, r):
            return msg[x["perm"] + (d - 1 if side else 6 - d), r]

        def charge(d, r):
            if d == 1:
                return msg[x["conc"], r] - msg[x["conc"] + 1, r]
            return msg[x["charge"] + (d - 2 if side else 5 - d), r]

        fields = [("phi", phi, DEEP), ("charge", charge, CHARGE)] + [("perm", perm, DEEP)] * plan.first
        for name, load, pairs in fields:
            for k, (d, n, e, m) in enumerate(pairs):
                tile = base + plan.c[name] + k
                if low:
                    out[tile, 0:n] = load(d, rows(n))
                    out[tile, 8 - m : 8] = load(e, rows(m))
                else:
                    out[tile, 8 - n : 8] = load(d, rows(n))
                    out[tile, 0:m] = load(e, rows(m))
        pick = (LO_HI, HI_HI)[side] if low else (LO_LO, HI_LO)[side]
        misc = base + plan.c["misc"]
        if plan.first:
            out[misc, 0:1] = msg[x["fluid"], rows(1)]
        out[misc, 1:2] = msg[x["pop"] + names.index(pick), rows(1)]
        for k in range(4):
            out[misc, 2 + k : 3 + k] = msg[x["dm"] + k, rows(1)]
        out[misc, 6:7] = charge(5, rows(1))


def lay(ext, own, name, plan, msgs):
    xl, xh, yl, yh, cl, ch = msgs
    x, y = plan.x, plan.y
    skip = plan.skip if name == "phi" else 0
    n = 6 - skip
    ext[6:14, 8:24] = own
    ext[0:n, 8:24] = xl[x[name] : x[name] + n]
    ext[14 + skip : 20, 8:24] = xh[x[name] : x[name] + n]
    ext[6:14, 2:8] = yl[:, y[name] : y[name] + 6]
    ext[6:14, 24:30] = yh[:, y[name] : y[name] + 6]
    corners(ext, plan, name, DEEP, cl, ch)


def corners(ext, plan, name, pairs, cl, ch):
    for k, (d, n, e, m) in enumerate(pairs):
        for side, p, q in ((0, 6 - d, 6 - e), (1, 13 + d, 13 + e)):
            tile = side * plan.tiles + plan.c[name] + k
            ext[p, 8 - n : 8] = cl[tile, 8 - n : 8]
            ext[q, 8 - m : 8] = cl[tile, 0:m]
            ext[p, 24 : 24 + n] = ch[tile, 0:n]
            ext[q, 24 : 24 + m] = ch[tile, 8 - m : 8]


def moments(load):
    dens = load(0)
    mom = [None, None, None]
    for i in range(1, 19):
        v = load(i)
        dens = dens + v
        for c in range(3):
            if VEL[i][c]:
                t = v if VEL[i][c] > 0 else -v
                mom[c] = t if mom[c] is None else mom[c] + t
    return [dens] + mom


def first_kernel(*refs):
    far, near, sems = refs[:5], refs[12:17], refs[17]
    pop, conc, phi, perm, mask = near
    x_hi, x_lo, y_hi, y_lo, dm, charge, fluid = refs[5:12]
    copies = [pltpu.make_async_copy(a, b, sems.at[k]) for k, (a, b) in enumerate(zip(far, near))]
    for copy in copies:
        copy.start()
    for copy in copies:
        copy.wait()
    charge[...] = conc[0] - conc[1]
    fluid[...] = mask[...].astype(F32)

    def plane(x, _):
        for k, v in enumerate(moments(lambda i: pop[i, x])):
            dm[k, x] = v
        return 0

    lax.fori_loop(0, CX, plane, 0, unroll=2)
    for low, xo, yo in ((False, x_hi, y_hi), (True, x_lo, y_lo)):
        pack_x(ONE, xo, low, phi, charge, conc, pop, dm, perm, fluid)
        pack_y(ONE, yo, low, None, phi, charge, conc, pop, dm, perm, fluid)


def corner_one_kernel(xl, xh, c_hi, c_lo):
    pack_corners(ONE, c_hi, False, xl, xh)
    pack_corners(ONE, c_lo, True, xl, xh)


def owner_kernel(owner, out):
    out[...] = jnp.full((8, NZ), owner[0, 0], jnp.int32).astype(F32)


def corner_two_kernel(xl, xh, rim, yl, c_hi, c_lo):
    pack_corners(TWO, c_hi, False, xl, xh, rim)
    pack_corners(TWO, c_lo, True, xl, xh, rim)
    c_hi[TWO.c["misc"], 7:8] = yl[0, TWO.y["owner"] : TWO.y["owner"] + 1]


def lay_all(plan, phi, conc, dm, charge, msgs, pa, ce, dn, mm, cc):
    xl, xh, yl, yh, cl, ch = msgs
    x, y = plan.x, plan.y
    lay(pa, phi[...], "phi", plan, msgs)
    ce[6:14, 8:24] = charge[...]
    q = x["charge"]
    ce[1:5, 8:24] = xl[q : q + 4]
    ce[15:19, 8:24] = xh[q : q + 4]
    c = x["conc"]
    ce[5, 8:24] = xl[c] - xl[c + 1]
    ce[14, 8:24] = xh[c] - xh[c + 1]
    q, c = y["charge"], y["conc"]
    ce[6:14, 3:7] = yl[:, q : q + 4]
    ce[6:14, 7:8] = yl[:, c : c + 1] - yl[:, c + 1 : c + 2]
    ce[6:14, 24:25] = yh[:, c : c + 1] - yh[:, c + 1 : c + 2]
    ce[6:14, 25:29] = yh[:, q : q + 4]
    corners(ce, plan, "charge", CHARGE, cl, ch)
    misc = plan.c["misc"], plan.tiles + plan.c["misc"]
    for m, p in zip(misc, (1, 18)):
        ce[p, 7:8] = cl[m, 6:7]
        ce[p, 24:25] = ch[m, 6:7]
    for s in range(2):
        cc[s, 1:9, 8:24] = conc[s]
        cc[s, 0, 8:24] = xl[x["conc"] + s]
        cc[s, 9, 8:24] = xh[x["conc"] + s]
        cc[s, 1:9, 7:8] = yl[:, c + s : c + s + 1]
        cc[s, 1:9, 24:25] = yh[:, c + s : c + s + 1]
    for k, ext in enumerate((dn, mm.at[0], mm.at[1], mm.at[2])):
        ext[1:9, 8:24] = dm[k]
        for msg, m, p in ((xl, misc[0], 0), (xh, misc[1], 9)):
            ext[p, 8:24] = msg[x["dm"] + k]
            ext[p, 7:8] = cl[m, 2 + k : 3 + k]
            ext[p, 24:25] = ch[m, 2 + k : 3 + k]
        for msg, r in ((yl, 7), (yh, 24)):
            ext[1:9, r : r + 1] = msg[:, y["dm"] + k : y["dm"] + k + 1]


LO_T, MID_T, HI_T = slice(0, 8), slice(8, 24), slice(24, 32)


def sweeps(coef, inv, ce, src, dst):
    for sweep in range(SWEEPS):

        def relax(x, _, src=src, dst=dst):
            mid = src[x]
            acc = ce[x] * inv[x]
            acc += coef[0, x] * src[x - 1] + coef[1, x] * src[x + 1]
            acc += coef[2, x] * turn(mid, 1, 0) + coef[3, x] * turn(mid, -1, 0)
            acc += coef[4, x] * turn(mid, 1, 1) + coef[5, x] * turn(mid, -1, 1)
            dst[x] = acc
            return 0

        lax.fori_loop(1 + sweep, 19 - sweep, relax, 0, unroll=True)
        src, dst = dst, src
    return src


def motion(fin, ce, fl, dn, mm, vel, sh):
    def plane(p, _):
        mid = fin[p + 5]
        grad = [
            -0.5 * (fin[p + 6] - fin[p + 4]),
            -0.5 * (turn(mid, -1, 0) - turn(mid, 1, 0)),
            -0.5 * (turn(mid, -1, 1) - turn(mid, 1, 1)),
        ]
        f = fl[p]
        scale = COUPLING * ce[p + 5]
        force = [f * (scale * g + d) if d else f * (scale * g) for g, d in zip(grad, (DRIVE, 0, 0))]
        dens = dn[p]
        over = 1.0 / dens
        mom = [mm[c, p] for c in range(3)]
        for c in range(3):
            vel[c, p] = f * (mom[c] + 0.5 * force[c]) * over
        u = [(mom[c] + TAU * force[c]) * over for c in range(3)]
        for c in range(3):
            sh[c, p] = u[c]
        sh[3, p] = 1.0 - 1.5 * (u[0] * u[0] + u[1] * u[1] + u[2] * u[2])
        sh[4, p] = dens * (1.0 / TAU)
        return 0

    lax.fori_loop(0, 10, plane, 0, unroll=5)


def ions(fin, fl, cc, vel, store):
    def flux(s, ca, cb, pot_a, pot_b, ua, ub, wall):
        total = ca + cb
        speed = 0.25 * (ua + ub) - (0.5 * DIFF[s] * VALENCE[s]) * (pot_b - pot_a)
        return wall * (total * speed - DIFF[s] * (cb - ca))

    def x_face(s, p):
        wall = fl[p, MID_T] * fl[p + 1, MID_T]
        return flux(s, cc[s, p, MID_T], cc[s, p + 1, MID_T], fin[p + 5, MID_T], fin[p + 6, MID_T],
                    vel[0, p, MID_T], vel[0, p + 1, MID_T], wall)

    def plane(p, before):
        after = []
        f, pot, vy = fl[p], fin[p + 5], vel[1, p]
        for s in range(2):
            face = x_face(s, p)
            total = face - before[s]
            after.append(face)
            c = cc[s, p]
            face = flux(s, c, turn(c, -1, 0), pot, turn(pot, -1, 0), vy, turn(vy, -1, 0), f * turn(f, -1, 0))
            total = total + (face - turn(face, 1, 0))[MID_T]
            fm, cm, pm, vz = f[MID_T], c[MID_T], pot[MID_T], vel[2, p, MID_T]
            face = flux(s, cm, turn(cm, -1, 1), pm, turn(pm, -1, 1), vz, turn(vz, -1, 1), fm * turn(fm, -1, 1))
            total = total + face - turn(face, 1, 1)
            store(s, p - 1, cm - total)
        return tuple(after)

    lax.fori_loop(1, 9, plane, (x_face(0, 0), x_face(1, 0)), unroll=8)


def collide_and_stream(plan, pop, fl, sh, msgs, lv, pop_out, dm_out):
    xl, xh, yl, yh, cl, ch = msgs
    y_pop, x_pop = plan.y["pop"], plan.x["pop"]
    bad = float("nan")

    def load(p, rows):
        return [sh[c, p, rows] for c in range(5)] + [fl[p, rows] != 0.0]

    def relaxed_of(i, pop_i, part):
        pr = None
        for c in range(3):
            if VEL[i][c]:
                t = part[c] if VEL[i][c] > 0 else -part[c]
                pr = t if pr is None else pr + t
        poly = part[3]
        if pr is not None:
            poly = poly + pr * (3.0 + 4.5 * pr)
        return (1.0 - 1.0 / TAU) * pop_i + (WEIGHT[i] * part[4]) * poly

    def collide(p, _):
        x = p - 1
        part = load(p, MID_T)
        wet = part[5]
        for i in range(19):
            j = OPP[i]
            if i > j:
                continue
            pi = pop[i, x]
            ri = relaxed_of(i, pi, part)
            if i == j:
                pop_out[i, x] = jnp.where(wet, ri, pi)
                continue
            pj = pop[j, x]
            rj = relaxed_of(j, pj, part)
            lv[i, p, MID_T] = jnp.where(wet, ri, bad)
            lv[j, p, MID_T] = jnp.where(wet, rj, bad)
            pop_out[i, x] = jnp.where(wet, rj, pi)
            pop_out[j, x] = jnp.where(wet, ri, pj)
        for y, names, r in ((yl, Y_IN_LO, 7), (yh, Y_IN_HI, 24)):
            row = slice(r, r + 1)
            part = load(p, row)
            for k, i in enumerate(names):
                value = relaxed_of(i, y[x, y_pop + k : y_pop + k + 1], part)
                lv[i, p, row] = jnp.where(part[5], value, bad)
        return 0

    lax.fori_loop(1, 9, collide, 0)
    for p, side, x, names, low_pop, high_pop in (
        (0, 0, xl, X_IN_LO, LO_LO, LO_HI),
        (9, 1, xh, X_IN_HI, HI_LO, HI_HI),
    ):
        misc = side * plan.tiles + plan.c["misc"]
        part = load(p, MID_T)
        for k, i in enumerate(names):
            lv[i, p, MID_T] = jnp.where(part[5], relaxed_of(i, x[x_pop + k], part), bad)
        for c, r, i in ((cl, 7, low_pop), (ch, 24, high_pop)):
            row = slice(r, r + 1)
            part = load(p, row)
            lv[i, p, row] = jnp.where(part[5], relaxed_of(i, c[misc, 1:2], part), bad)

    def stream(x, _):
        wet = fl[x + 1, MID_T] != 0.0
        for i in range(1, 19):
            ex, ey, ez = VEL[i]
            came = lv[i, x + 1 - ex, 8 - ey : 24 - ey]
            if ez:
                came = turn(came, ez, 1)
            pop_out[i, x] = jnp.where(wet & (came == came), came, pop_out[i, x])
        if dm_out is not None:
            for k, v in enumerate(moments(lambda i: pop_out[i, x])):
                dm_out[k, x] = v
        return 0

    lax.fori_loop(0, CX, stream, 0, unroll=4)


def step_one_kernel(below, pop, conc, phi, perm, dm, charge, fluid, xl, xh, yl, yh, cl, ch,
                    pop_out, phi_out, conc_out, charge_out, x_hi, x_lo, y_hi, y_lo, dm_out, rim, coef, inv, fl,
                    pe, pa, pb, ce, dn, mm, cc, vel, sh, lv):
    msgs = (xl, xh, yl, yh, cl, ch)
    lay(pe, perm[...], "perm", ONE, msgs)

    def coefs(x, _):
        mid = pe[x]
        faces = [0.5 * (mid + other) for other in (
            pe[x - 1], pe[x + 1], turn(mid, 1, 0), turn(mid, -1, 0), turn(mid, 1, 1), turn(mid, -1, 1))]
        over = 1.0 / (faces[0] + faces[1] + faces[2] + faces[3] + faces[4] + faces[5])
        inv[x] = over
        for k in range(6):
            coef[k, x] = faces[k] * over
        return 0

    lax.fori_loop(1, 19, coefs, 0, unroll=9)
    fl[1:9, 8:24] = fluid[...]
    x, y = ONE.x, ONE.y
    for side, msg, p in ((0, xl, 0), (1, xh, 9)):
        m = side * ONE.tiles + ONE.c["misc"]
        fl[p, 8:24] = msg[x["fluid"]]
        fl[p, 7:8] = cl[m, 0:1]
        fl[p, 24:25] = ch[m, 0:1]
    fl[1:9, 7:8] = yl[:, y["fluid"] : y["fluid"] + 1]
    fl[1:9, 24:25] = yh[:, y["fluid"] : y["fluid"] + 1]
    lay_all(ONE, phi, conc, dm, charge, msgs, pa, ce, dn, mm, cc)
    fin = sweeps(coef, inv, ce, pa, pb)
    phi_out[...] = fin[6:14, MID_T]
    rim[0:2] = fin[4:6, MID_T]
    rim[2:4] = fin[14:16, MID_T]
    motion(fin, ce, fl, dn, mm, vel, sh)

    def store(s, x, values):
        conc_out[s, x] = values

    ions(fin, fl, cc, vel, store)
    collide_and_stream(ONE, pop, fl, sh, msgs, lv, pop_out, dm_out)
    charge_out[...] = conc_out[0] - conc_out[1]
    for low, xo, yo in ((False, x_hi, y_hi), (True, x_lo, y_lo)):
        pack_x(TWO, xo, low, phi_out, charge_out, conc_out, pop_out, dm_out)
        pack_y(TWO, yo, low, below[0:1], phi_out, charge_out, conc_out, pop_out, dm_out)


def ions_two_kernel(conc, phi, charge, dm, rim, coef, inv, fl, xl, xh, yl, yh, cl, ch,
                    phi_out, slab, sh, pa, pb, ce, dn, mm, cc, vel):
    lay_all(TWO, phi, conc, dm, charge, (xl, xh, yl, yh, cl, ch), pa, ce, dn, mm, cc)
    pa[4:6, MID_T] = rim[0:2]
    pa[14:16, MID_T] = rim[2:4]
    fin = sweeps(coef, inv, ce, pa, pb)
    phi_out[...] = fin[6:14, MID_T]
    motion(fin, ce, fl, dn, mm, vel, sh)

    def store(s, x, values):
        slab[s * CX + x] = values

    ions(fin, fl, cc, vel, store)
    slab[2 * CX, 0:8] = jnp.broadcast_to(cl[TWO.c["misc"], 7:8], (8, NZ))


def flow_two_kernel(pop, fl, sh, xl, xh, yl, yh, cl, ch, pop_out, lv):
    collide_and_stream(TWO, pop, fl, sh, (xl, xh, yl, yh, cl, ch), lv, pop_out, None)


def place(up):
    me = lax.rem(lax.axis_index("gy") + up, 8)
    return jnp.full((1, NZ), me, jnp.int32).astype(F32)


def route_kernel(mine, below, above, out):
    want = below[2 * CX, 0:1]
    for x in range(2 * CX):
        out[x] = jnp.where(want == place(0), mine[x], jnp.where(want == place(1), above[x], below[x]))


def arrive_kernel(mine, below, above, below_two, above_two, far, owner, out):
    slab = owner[0:1]
    near = ((0, mine), (7, below), (1, above), (6, below_two), (2, above_two))
    for x in range(2 * CX):
        v = far[x]
        for up, values in near:
            v = jnp.where(slab == place(up), values[x], v)
        out[x] = v


VMEM, FAR, SMEM = (pl.BlockSpec(memory_space=m) for m in (pltpu.VMEM, pltpu.HBM, pltpu.SMEM))


def call(kernel, outs, args, scratch=(), specs=None, flops=0):
    return pl.pallas_call(
        kernel,
        out_shape=outs,
        in_specs=specs or [VMEM] * len(args),
        out_specs=[VMEM] * len(outs),
        scratch_shapes=[pltpu.VMEM(s, F32) if isinstance(s, tuple) else s for s in scratch],
        compiler_params=pltpu.CompilerParams(vmem_limit_bytes=24 * 1024 * 1024),
        cost_estimate=pl.CostEstimate(flops=flops, bytes_accessed=0, transcendentals=0) if flops else None,
    )(*args)


HALO = (EX, EY, NZ)
RIM = (10, EY, NZ)
FIELDS = (HALO, HALO, HALO, RIM, (3,) + RIM, (2,) + RIM, (3,) + RIM)


def shift(values, axis, by):
    n = lax.axis_size(axis)
    return lax.ppermute(values, axis, [(i, (i + by) % n) for i in range(n)])


def exchange(x_hi, x_lo, y_hi, y_lo):
    yl, yh = shift(y_hi, "gy", 1), shift(y_lo, "gy", -1)
    xl, xh = shift(x_hi, "gx", 1), shift(x_lo, "gx", -1)
    return xl, xh, yl, yh


def body(populations, concentration, potential, permittivity, fluid_mask, owners):
    block, row = shape(CX, CY, NZ), shape(8, NZ)
    pops, both, four = shape(19, CX, CY, NZ), shape(2, CX, CY, NZ), shape(4, CX, CY, NZ)

    def messages(plan):
        x, y = shape(plan.x_planes, CY, NZ), shape(CX, plan.y_rows, NZ)
        return (x, x, y, y)

    def tiles(plan):
        return (shape(2 * plan.tiles, 8, NZ),) * 2

    *sent, dm, charge, fluid = call(
        first_kernel, messages(ONE) + (four, block, block),
        tuple(pltpu.with_memory_space_constraint(v, pltpu.HBM) for v in (
            populations, concentration, potential, permittivity, fluid_mask)),
        (pops.shape, both.shape, block.shape, block.shape, pltpu.VMEM(block.shape, jnp.int32),
         pltpu.SemaphoreType.DMA((5,))),
        [FAR] * 5)
    got = exchange(*sent)
    c_hi, c_lo = call(corner_one_kernel, tiles(ONE), got[:2])
    got += (shift(c_hi, "gy", 1), shift(c_lo, "gy", -1))
    (owner,) = call(owner_kernel, (row,), (owners,), (), [SMEM])
    below = shift(owner, "gy", 1)
    pop, phi, conc, charge, *rest = call(
        step_one_kernel,
        (pops, block, both, block) + messages(TWO)
        + (four, shape(4, CY, NZ), shape(6, *HALO), shape(*HALO), shape(*RIM)),
        (below, populations, concentration, potential, permittivity, dm, charge, fluid) + got,
        (HALO,) + FIELDS + ((5,) + RIM, (19,) + RIM))
    sent, (dm, rim, coef, inv, fl) = rest[:4], rest[4:]
    got = exchange(*sent)
    c_hi, c_lo = call(corner_two_kernel, tiles(TWO), got[:2] + (rim, got[2]))
    got += (shift(c_hi, "gy", 1), shift(c_lo, "gy", -1))
    slab = shape(2 * CX, CY, NZ)
    phi, mine, sh = call(
        ions_two_kernel, (block, shape(2 * CX + 1, CY, NZ), shape(5, *RIM)),
        (conc, phi, charge, dm, rim, coef, inv, fl) + got, FIELDS)
    below, above = shift(mine, "gy", 1), shift(mine, "gy", -1)
    (pop,) = call(flow_two_kernel, (pops,), (pop, fl, sh) + got, ((19,) + RIM,), flops=40_000_000)
    (routed,) = call(route_kernel, (slab,), (mine, below, above))
    far = shift(routed, "gy", 4)
    below_two, above_two = shift(below, "gy", 1), shift(above, "gy", -1)
    (migrated,) = call(arrive_kernel, (slab,), (mine, below, above, below_two, above_two, far, owner))
    return (pop, phi, migrated.reshape(2, CX, CY, NZ))


def solution(mesh):
    in_specs = (
        P(None, "gx", "gy", None),
        P(None, "gx", "gy", None),
        P("gx", "gy", None),
        P("gx", "gy", None),
        P("gx", "gy", None),
        P("gx", "gy"),
    )
    out_specs = (P(None, "gx", "gy", None), P("gx", "gy", None), P(None, "gx", "gy", None))
    return jax.shard_map(body, mesh=mesh, in_specs=in_specs, out_specs=out_specs, check_vma=False)
```

```python
import jax
import jax.numpy as jnp
from jax import lax
from jax.experimental import pallas as pl
from jax.experimental.pallas import tpu as pltpu
from jax.sharding import PartitionSpec as P

STEPS = 2
SWEEPS = 4
VEL = (
    (0, 0, 0), (1, 0, 0), (-1, 0, 0), (0, 1, 0), (0, -1, 0), (0, 0, 1), (0, 0, -1),
    (1, 1, 0), (-1, -1, 0), (1, -1, 0), (-1, 1, 0), (1, 0, 1), (-1, 0, -1), (1, 0, -1),
    (-1, 0, 1), (0, 1, 1), (0, -1, -1), (0, 1, -1), (0, -1, 1),
)
WEIGHT = (1.0 / 3.0,) + (1.0 / 18.0,) * 6 + (1.0 / 36.0,) * 12
OPP = (0, 2, 1, 4, 3, 6, 5, 8, 7, 10, 9, 12, 11, 14, 13, 16, 15, 18, 17)
TAU = 0.8
COUPLING = 0.05
DRIVE = 0.001
DIFF = (0.1, 0.15)
VALENCE = (1.0, -1.0)

CX, CY, NZ = 8, 16, 128
EX, EY = 20, 32
F32 = jnp.float32

X_IN_LO = tuple(i for i in range(19) if VEL[i][0] == 1)
X_IN_HI = tuple(i for i in range(19) if VEL[i][0] == -1)
Y_IN_LO = tuple(i for i in range(19) if VEL[i][1] == 1)
Y_IN_HI = tuple(i for i in range(19) if VEL[i][1] == -1)
LO_LO, HI_LO = VEL.index((1, 1, 0)), VEL.index((-1, 1, 0))
LO_HI, HI_HI = VEL.index((1, -1, 0)), VEL.index((-1, -1, 0))


def shape(*dims):
    return jax.ShapeDtypeStruct(dims, F32)


def turn(v, by, axis):
    return pltpu.roll(v, by % v.shape[axis], axis)


class Plan:
    def __init__(self, first):
        self.first = first
        rows = [("phi", 6)] + [("perm", 6)] * first + [("charge", 4), ("conc", 2)] + [("fluid", 1)] * first
        self.y = {}
        at = 0
        for name, n in rows + [("pop", 5), ("dm", 4)]:
            self.y[name] = at
            at += n
        self.y_rows = -(-at // 8) * 8
        self.skip = 0 if first else 2
        planes = [("phi", 6 - self.skip)] + [("perm", 6)] * first + [("charge", 4), ("conc", 2)]
        planes += [("fluid", 1)] * first + [("pop", 5), ("dm", 4)]
        self.x = {}
        at = 0
        for name, n in planes:
            self.x[name] = at
            at += n
        self.x_planes = at
        self.c = {"phi": 0, "perm": 3, "charge": 3 + 3 * first, "misc": 5 + 3 * first}
        self.tiles = 6 + 3 * first


ONE, TWO = Plan(True), Plan(False)
DEEP = ((1, 6, 6, 1), (2, 5, 5, 2), (3, 4, 4, 3))
CHARGE = ((1, 5, 4, 2), (2, 4, 3, 3))


def pack_y(plan, out, low, phi, charge, conc, pop, dm, perm=None, fluid=None):
    y = plan.y
    six = slice(0, 6) if low else slice(10, 16)
    four = slice(1, 5) if low else slice(11, 15)
    row = slice(0, 1) if low else slice(15, 16)
    out[:, 0:6] = phi[:, six]
    if plan.first:
        out[:, y["perm"] : y["perm"] + 6] = perm[:, six]
        out[:, y["fluid"] : y["fluid"] + 1] = fluid[:, row]
    out[:, y["charge"] : y["charge"] + 4] = charge[:, four]
    for s in range(2):
        out[:, y["conc"] + s : y["conc"] + s + 1] = conc[s, :, row]
    for k, i in enumerate(Y_IN_HI if low else Y_IN_LO):
        out[:, y["pop"] + k : y["pop"] + k + 1] = pop[i, :, row]
    for k in range(4):
        out[:, y["dm"] + k : y["dm"] + k + 1] = dm[k, :, row]


def pack_x(plan, out, low, phi, charge, conc, pop, dm, perm=None, fluid=None):
    x = plan.x

    def spread(to, field, first, last):
        lo = first - 1 if low else CX - last
        out[to : to + last - first + 1] = field[lo : lo + last - first + 1]

    spread(0, phi, 1 + plan.skip, 6)
    spread(x["charge"], charge, 2, 5)
    edge = 0 if low else CX - 1
    for s in range(2):
        out[x["conc"] + s] = conc[s, edge]
    if plan.first:
        spread(x["perm"], perm, 1, 6)
        out[x["fluid"]] = fluid[edge]
    for k, i in enumerate(X_IN_HI if low else X_IN_LO):
        out[x["pop"] + k] = pop[i, edge]
    for k in range(4):
        out[x["dm"] + k] = dm[k, edge]


def pack_corners(plan, out, low, xl, xh, rim=None):
    x = plan.x

    def rows(n):
        return slice(0, n) if low else slice(16 - n, 16)

    for side, msg, names in ((0, xl, X_IN_LO), (1, xh, X_IN_HI)):
        base = side * plan.tiles

        def phi(d, r):
            if d <= plan.skip:
                return rim[1 + d if side else 2 - d, r]
            return msg[x["phi"] + (d - 1 - plan.skip if side else 6 - d), r]

        def perm(d, r):
            return msg[x["perm"] + (d - 1 if side else 6 - d), r]

        def charge(d, r):
            if d == 1:
                return msg[x["conc"], r] - msg[x["conc"] + 1, r]
            return msg[x["charge"] + (d - 2 if side else 5 - d), r]

        fields = [("phi", phi, DEEP), ("charge", charge, CHARGE)] + [("perm", perm, DEEP)] * plan.first
        for name, load, pairs in fields:
            for k, (d, n, e, m) in enumerate(pairs):
                tile = base + plan.c[name] + k
                if low:
                    out[tile, 0:n] = load(d, rows(n))
                    out[tile, 8 - m : 8] = load(e, rows(m))
                else:
                    out[tile, 8 - n : 8] = load(d, rows(n))
                    out[tile, 0:m] = load(e, rows(m))
        pick = (LO_HI, HI_HI)[side] if low else (LO_LO, HI_LO)[side]
        misc = base + plan.c["misc"]
        if plan.first:
            out[misc, 0:1] = msg[x["fluid"], rows(1)]
        out[misc, 1:2] = msg[x["pop"] + names.index(pick), rows(1)]
        for k in range(4):
            out[misc, 2 + k : 3 + k] = msg[x["dm"] + k, rows(1)]
        out[misc, 6:7] = charge(5, rows(1))


def lay(ext, own, name, plan, msgs):
    xl, xh, yl, yh, cl, ch = msgs
    x, y = plan.x, plan.y
    skip = plan.skip if name == "phi" else 0
    n = 6 - skip
    ext[6:14, 8:24] = own
    ext[0:n, 8:24] = xl[x[name] : x[name] + n]
    ext[14 + skip : 20, 8:24] = xh[x[name] : x[name] + n]
    ext[6:14, 2:8] = yl[:, y[name] : y[name] + 6]
    ext[6:14, 24:30] = yh[:, y[name] : y[name] + 6]
    corners(ext, plan, name, DEEP, cl, ch)


def corners(ext, plan, name, pairs, cl, ch):
    for k, (d, n, e, m) in enumerate(pairs):
        for side, p, q in ((0, 6 - d, 6 - e), (1, 13 + d, 13 + e)):
            tile = side * plan.tiles + plan.c[name] + k
            ext[p, 8 - n : 8] = cl[tile, 8 - n : 8]
            ext[q, 8 - m : 8] = cl[tile, 0:m]
            ext[p, 24 : 24 + n] = ch[tile, 0:n]
            ext[q, 24 : 24 + m] = ch[tile, 8 - m : 8]


def moments(load):
    dens = load(0)
    mom = [None, None, None]
    for i in range(1, 19):
        v = load(i)
        dens = dens + v
        for c in range(3):
            if VEL[i][c]:
                t = v if VEL[i][c] > 0 else -v
                mom[c] = t if mom[c] is None else mom[c] + t
    return [dens] + mom


def first_kernel(*refs):
    far, near, sems = refs[:5], refs[12:17], refs[17]
    pop, conc, phi, perm, mask = near
    x_hi, x_lo, y_hi, y_lo, dm, charge, fluid = refs[5:12]
    copies = [pltpu.make_async_copy(a, b, sems.at[k]) for k, (a, b) in enumerate(zip(far, near))]
    for copy in copies:
        copy.start()
    for copy in copies:
        copy.wait()
    charge[...] = conc[0] - conc[1]
    fluid[...] = mask[...].astype(F32)

    def plane(x, _):
        for k, v in enumerate(moments(lambda i: pop[i, x])):
            dm[k, x] = v
        return 0

    lax.fori_loop(0, CX, plane, 0, unroll=2)
    for low, xo, yo in ((False, x_hi, y_hi), (True, x_lo, y_lo)):
        pack_x(ONE, xo, low, phi, charge, conc, pop, dm, perm, fluid)
        pack_y(ONE, yo, low, phi, charge, conc, pop, dm, perm, fluid)


def corner_one_kernel(xl, xh, c_hi, c_lo):
    pack_corners(ONE, c_hi, False, xl, xh)
    pack_corners(ONE, c_lo, True, xl, xh)


def corner_two_kernel(xl, xh, rim, c_hi, c_lo):
    pack_corners(TWO, c_hi, False, xl, xh, rim)
    pack_corners(TWO, c_lo, True, xl, xh, rim)


def lay_all(plan, phi, conc, dm, charge, msgs, pa, ce, dn, mm, cc):
    xl, xh, yl, yh, cl, ch = msgs
    x, y = plan.x, plan.y
    lay(pa, phi[...], "phi", plan, msgs)
    ce[6:14, 8:24] = charge[...]
    q = x["charge"]
    ce[1:5, 8:24] = xl[q : q + 4]
    ce[15:19, 8:24] = xh[q : q + 4]
    c = x["conc"]
    ce[5, 8:24] = xl[c] - xl[c + 1]
    ce[14, 8:24] = xh[c] - xh[c + 1]
    q, c = y["charge"], y["conc"]
    ce[6:14, 3:7] = yl[:, q : q + 4]
    ce[6:14, 7:8] = yl[:, c : c + 1] - yl[:, c + 1 : c + 2]
    ce[6:14, 24:25] = yh[:, c : c + 1] - yh[:, c + 1 : c + 2]
    ce[6:14, 25:29] = yh[:, q : q + 4]
    corners(ce, plan, "charge", CHARGE, cl, ch)
    misc = plan.c["misc"], plan.tiles + plan.c["misc"]
    for m, p in zip(misc, (1, 18)):
        ce[p, 7:8] = cl[m, 6:7]
        ce[p, 24:25] = ch[m, 6:7]
    for s in range(2):
        cc[s, 1:9, 8:24] = conc[s]
        cc[s, 0, 8:24] = xl[x["conc"] + s]
        cc[s, 9, 8:24] = xh[x["conc"] + s]
        cc[s, 1:9, 7:8] = yl[:, c + s : c + s + 1]
        cc[s, 1:9, 24:25] = yh[:, c + s : c + s + 1]
    for k, ext in enumerate((dn, mm.at[0], mm.at[1], mm.at[2])):
        ext[1:9, 8:24] = dm[k]
        for msg, m, p in ((xl, misc[0], 0), (xh, misc[1], 9)):
            ext[p, 8:24] = msg[x["dm"] + k]
            ext[p, 7:8] = cl[m, 2 + k : 3 + k]
            ext[p, 24:25] = ch[m, 2 + k : 3 + k]
        for msg, r in ((yl, 7), (yh, 24)):
            ext[1:9, r : r + 1] = msg[:, y["dm"] + k : y["dm"] + k + 1]


LO_T, MID_T, HI_T = slice(0, 8), slice(8, 24), slice(24, 32)


def sweeps(coef, inv, ce, src, dst):
    for sweep in range(SWEEPS):

        def relax(x, _, src=src, dst=dst):
            mid = src[x]
            acc = ce[x] * inv[x]
            acc += coef[0, x] * src[x - 1] + coef[1, x] * src[x + 1]
            acc += coef[2, x] * turn(mid, 1, 0) + coef[3, x] * turn(mid, -1, 0)
            acc += coef[4, x] * turn(mid, 1, 1) + coef[5, x] * turn(mid, -1, 1)
            dst[x] = acc
            return 0

        lax.fori_loop(1 + sweep, 19 - sweep, relax, 0, unroll=True)
        src, dst = dst, src
    return src


def motion(fin, ce, fl, dn, mm, vel, sh):
    def plane(p, _):
        mid = fin[p + 5]
        grad = [
            -0.5 * (fin[p + 6] - fin[p + 4]),
            -0.5 * (turn(mid, -1, 0) - turn(mid, 1, 0)),
            -0.5 * (turn(mid, -1, 1) - turn(mid, 1, 1)),
        ]
        f = fl[p]
        scale = COUPLING * ce[p + 5]
        force = [f * (scale * g + d) if d else f * (scale * g) for g, d in zip(grad, (DRIVE, 0, 0))]
        dens = dn[p]
        over = 1.0 / dens
        mom = [mm[c, p] for c in range(3)]
        for c in range(3):
            vel[c, p] = f * (mom[c] + 0.5 * force[c]) * over
        u = [(mom[c] + TAU * force[c]) * over for c in range(3)]
        for c in range(3):
            sh[c, p] = u[c]
        sh[3, p] = 1.0 - 1.5 * (u[0] * u[0] + u[1] * u[1] + u[2] * u[2])
        sh[4, p] = dens * (1.0 / TAU)
        return 0

    lax.fori_loop(0, 10, plane, 0, unroll=5)


def ions(fin, fl, cc, vel, store):
    def flux(s, ca, cb, pot_a, pot_b, ua, ub, wall):
        total = ca + cb
        speed = 0.25 * (ua + ub) - (0.5 * DIFF[s] * VALENCE[s]) * (pot_b - pot_a)
        return wall * (total * speed - DIFF[s] * (cb - ca))

    def x_face(s, p):
        wall = fl[p, MID_T] * fl[p + 1, MID_T]
        return flux(s, cc[s, p, MID_T], cc[s, p + 1, MID_T], fin[p + 5, MID_T], fin[p + 6, MID_T],
                    vel[0, p, MID_T], vel[0, p + 1, MID_T], wall)

    def plane(p, before):
        after = []
        f, pot, vy = fl[p], fin[p + 5], vel[1, p]
        for s in range(2):
            face = x_face(s, p)
            total = face - before[s]
            after.append(face)
            c = cc[s, p]
            face = flux(s, c, turn(c, -1, 0), pot, turn(pot, -1, 0), vy, turn(vy, -1, 0), f * turn(f, -1, 0))
            total = total + (face - turn(face, 1, 0))[MID_T]
            fm, cm, pm, vz = f[MID_T], c[MID_T], pot[MID_T], vel[2, p, MID_T]
            face = flux(s, cm, turn(cm, -1, 1), pm, turn(pm, -1, 1), vz, turn(vz, -1, 1), fm * turn(fm, -1, 1))
            total = total + face - turn(face, 1, 1)
            store(s, p - 1, cm - total)
        return tuple(after)

    lax.fori_loop(1, 9, plane, (x_face(0, 0), x_face(1, 0)), unroll=8)


def collide_and_stream(plan, pop, fl, sh, msgs, lv, pop_out, dm_out):
    xl, xh, yl, yh, cl, ch = msgs
    y_pop, x_pop = plan.y["pop"], plan.x["pop"]
    bad = float("nan")

    def load(p, rows):
        return [sh[c, p, rows] for c in range(5)] + [fl[p, rows] != 0.0]

    def relaxed_of(i, pop_i, part):
        pr = None
        for c in range(3):
            if VEL[i][c]:
                t = part[c] if VEL[i][c] > 0 else -part[c]
                pr = t if pr is None else pr + t
        poly = part[3]
        if pr is not None:
            poly = poly + pr * (3.0 + 4.5 * pr)
        return (1.0 - 1.0 / TAU) * pop_i + (WEIGHT[i] * part[4]) * poly

    def collide(p, _):
        x = p - 1
        part = load(p, MID_T)
        wet = part[5]
        for i in range(19):
            j = OPP[i]
            if i > j:
                continue
            pi = pop[i, x]
            ri = relaxed_of(i, pi, part)
            if i == j:
                pop_out[i, x] = jnp.where(wet, ri, pi)
                continue
            pj = pop[j, x]
            rj = relaxed_of(j, pj, part)
            lv[i, p, MID_T] = jnp.where(wet, ri, bad)
            lv[j, p, MID_T] = jnp.where(wet, rj, bad)
            pop_out[i, x] = jnp.where(wet, rj, pi)
            pop_out[j, x] = jnp.where(wet, ri, pj)
        for y, names, r in ((yl, Y_IN_LO, 7), (yh, Y_IN_HI, 24)):
            row = slice(r, r + 1)
            part = load(p, row)
            for k, i in enumerate(names):
                value = relaxed_of(i, y[x, y_pop + k : y_pop + k + 1], part)
                lv[i, p, row] = jnp.where(part[5], value, bad)
        return 0

    lax.fori_loop(1, 9, collide, 0)
    for p, side, x, names, low_pop, high_pop in (
        (0, 0, xl, X_IN_LO, LO_LO, LO_HI),
        (9, 1, xh, X_IN_HI, HI_LO, HI_HI),
    ):
        misc = side * plan.tiles + plan.c["misc"]
        part = load(p, MID_T)
        for k, i in enumerate(names):
            lv[i, p, MID_T] = jnp.where(part[5], relaxed_of(i, x[x_pop + k], part), bad)
        for c, r, i in ((cl, 7, low_pop), (ch, 24, high_pop)):
            row = slice(r, r + 1)
            part = load(p, row)
            lv[i, p, row] = jnp.where(part[5], relaxed_of(i, c[misc, 1:2], part), bad)

    def stream(x, _):
        wet = fl[x + 1, MID_T] != 0.0
        for i in range(1, 19):
            ex, ey, ez = VEL[i]
            came = lv[i, x + 1 - ex, 8 - ey : 24 - ey]
            if ez:
                came = turn(came, ez, 1)
            pop_out[i, x] = jnp.where(wet & (came == came), came, pop_out[i, x])
        if dm_out is not None:
            for k, v in enumerate(moments(lambda i: pop_out[i, x])):
                dm_out[k, x] = v
        return 0

    lax.fori_loop(0, CX, stream, 0, unroll=4)


def step_one_kernel(owner, pop, conc, phi, perm, dm, charge, fluid, xl, xh, yl, yh, cl, ch,
                    pop_out, phi_out, conc_out, charge_out, x_hi, x_lo, y_hi, y_lo, dm_out, rim, coef, inv, fl, owner_row,
                    pe, pa, pb, ce, dn, mm, cc, vel, sh, lv):
    msgs = (xl, xh, yl, yh, cl, ch)
    owner_row[...] = jnp.full((8, NZ), owner[0, 0], jnp.int32).astype(F32)
    lay(pe, perm[...], "perm", ONE, msgs)

    def coefs(x, _):
        mid = pe[x]
        faces = [0.5 * (mid + other) for other in (
            pe[x - 1], pe[x + 1], turn(mid, 1, 0), turn(mid, -1, 0), turn(mid, 1, 1), turn(mid, -1, 1))]
        over = 1.0 / (faces[0] + faces[1] + faces[2] + faces[3] + faces[4] + faces[5])
        inv[x] = over
        for k in range(6):
            coef[k, x] = faces[k] * over
        return 0

    lax.fori_loop(1, 19, coefs, 0, unroll=9)
    fl[1:9, 8:24] = fluid[...]
    x, y = ONE.x, ONE.y
    for side, msg, p in ((0, xl, 0), (1, xh, 9)):
        m = side * ONE.tiles + ONE.c["misc"]
        fl[p, 8:24] = msg[x["fluid"]]
        fl[p, 7:8] = cl[m, 0:1]
        fl[p, 24:25] = ch[m, 0:1]
    fl[1:9, 7:8] = yl[:, y["fluid"] : y["fluid"] + 1]
    fl[1:9, 24:25] = yh[:, y["fluid"] : y["fluid"] + 1]
    lay_all(ONE, phi, conc, dm, charge, msgs, pa, ce, dn, mm, cc)
    fin = sweeps(coef, inv, ce, pa, pb)
    phi_out[...] = fin[6:14, MID_T]
    rim[0:2] = fin[4:6, MID_T]
    rim[2:4] = fin[14:16, MID_T]
    motion(fin, ce, fl, dn, mm, vel, sh)

    def store(s, x, values):
        conc_out[s, x] = values

    ions(fin, fl, cc, vel, store)
    collide_and_stream(ONE, pop, fl, sh, msgs, lv, pop_out, dm_out)
    charge_out[...] = conc_out[0] - conc_out[1]
    for low, xo, yo in ((False, x_hi, y_hi), (True, x_lo, y_lo)):
        pack_x(TWO, xo, low, phi_out, charge_out, conc_out, pop_out, dm_out)
        pack_y(TWO, yo, low, phi_out, charge_out, conc_out, pop_out, dm_out)


def ions_two_kernel(conc, phi, charge, dm, rim, coef, inv, fl, xl, xh, yl, yh, cl, ch,
                    phi_out, slab, sh, pa, pb, ce, dn, mm, cc, vel):
    lay_all(TWO, phi, conc, dm, charge, (xl, xh, yl, yh, cl, ch), pa, ce, dn, mm, cc)
    pa[4:6, MID_T] = rim[0:2]
    pa[14:16, MID_T] = rim[2:4]
    fin = sweeps(coef, inv, ce, pa, pb)
    phi_out[...] = fin[6:14, MID_T]
    motion(fin, ce, fl, dn, mm, vel, sh)

    def store(s, x, values):
        slab[s * CX + x] = values

    ions(fin, fl, cc, vel, store)


def flow_two_kernel(pop, fl, sh, xl, xh, yl, yh, cl, ch, pop_out, lv):
    collide_and_stream(TWO, pop, fl, sh, (xl, xh, yl, yh, cl, ch), lv, pop_out, None)


def place(up):
    me = lax.rem(lax.axis_index("gy") + up, 8)
    return jnp.full((1, NZ), me, jnp.int32).astype(F32)


def route_kernel(mine, below, above, wanted, out):
    want = wanted[0:1]
    for x in range(2 * CX):
        out[x] = jnp.where(want == place(0), mine[x], jnp.where(want == place(1), above[x], below[x]))


def arrive_kernel(mine, below, above, below_two, above_two, far, owner, out):
    slab = owner[0:1]
    near = ((0, mine), (7, below), (1, above), (6, below_two), (2, above_two))
    for x in range(2 * CX):
        v = far[x]
        for up, values in near:
            v = jnp.where(slab == place(up), values[x], v)
        out[x] = v


VMEM, FAR, SMEM = (pl.BlockSpec(memory_space=m) for m in (pltpu.VMEM, pltpu.HBM, pltpu.SMEM))


def call(kernel, outs, args, scratch=(), specs=None, flops=0):
    return pl.pallas_call(
        kernel,
        out_shape=outs,
        in_specs=specs or [VMEM] * len(args),
        out_specs=[VMEM] * len(outs),
        scratch_shapes=[pltpu.VMEM(s, F32) if isinstance(s, tuple) else s for s in scratch],
        compiler_params=pltpu.CompilerParams(vmem_limit_bytes=24 * 1024 * 1024),
        cost_estimate=pl.CostEstimate(flops=flops, bytes_accessed=0, transcendentals=0) if flops else None,
    )(*args)


HALO = (EX, EY, NZ)
RIM = (10, EY, NZ)
FIELDS = (HALO, HALO, HALO, RIM, (3,) + RIM, (2,) + RIM, (3,) + RIM)


def shift(values, axis, by):
    n = lax.axis_size(axis)
    return lax.ppermute(values, axis, [(i, (i + by) % n) for i in range(n)])


def exchange(x_hi, x_lo, y_hi, y_lo):
    yl, yh = shift(y_hi, "gy", 1), shift(y_lo, "gy", -1)
    xl, xh = shift(x_hi, "gx", 1), shift(x_lo, "gx", -1)
    return xl, xh, yl, yh


def body(populations, concentration, potential, permittivity, fluid_mask, owners):
    block, row = shape(CX, CY, NZ), shape(8, NZ)
    pops, both, four = shape(19, CX, CY, NZ), shape(2, CX, CY, NZ), shape(4, CX, CY, NZ)

    def messages(plan):
        x, y = shape(plan.x_planes, CY, NZ), shape(CX, plan.y_rows, NZ)
        return (x, x, y, y)

    def tiles(plan):
        return (shape(2 * plan.tiles, 8, NZ),) * 2

    *sent, dm, charge, fluid = call(
        first_kernel, messages(ONE) + (four, block, block),
        tuple(pltpu.with_memory_space_constraint(v, pltpu.HBM) for v in (
            populations, concentration, potential, permittivity, fluid_mask)),
        (pops.shape, both.shape, block.shape, block.shape, pltpu.VMEM(block.shape, jnp.int32),
         pltpu.SemaphoreType.DMA((5,))),
        [FAR] * 5)
    got = exchange(*sent)
    c_hi, c_lo = call(corner_one_kernel, tiles(ONE), got[:2])
    got += (shift(c_hi, "gy", 1), shift(c_lo, "gy", -1))
    pop, phi, conc, charge, *rest = call(
        step_one_kernel,
        (pops, block, both, block) + messages(TWO)
        + (four, shape(4, CY, NZ), shape(6, *HALO), shape(*HALO), shape(*RIM), row),
        (owners, populations, concentration, potential, permittivity, dm, charge, fluid) + got,
        (HALO,) + FIELDS + ((5,) + RIM, (19,) + RIM), [SMEM] + [VMEM] * 13)
    sent, (dm, rim, coef, inv, fl, owner) = rest[:4], rest[4:]
    got = exchange(*sent)
    c_hi, c_lo = call(corner_two_kernel, tiles(TWO), got[:2] + (rim,))
    got += (shift(c_hi, "gy", 1), shift(c_lo, "gy", -1))
    slab = shape(2 * CX, CY, NZ)
    phi, mine, sh = call(
        ions_two_kernel, (block, slab, shape(5, *RIM)),
        (conc, phi, charge, dm, rim, coef, inv, fl) + got, FIELDS)
    below, above = shift(mine, "gy", 1), shift(mine, "gy", -1)
    (pop,) = call(flow_two_kernel, (pops,), (pop, fl, sh) + got, ((19,) + RIM,), flops=40_000_000)
    wanted = shift(owner, "gy", 4)
    (routed,) = call(route_kernel, (slab,), (mine, below, above, wanted))
    far = shift(routed, "gy", 4)
    below_two, above_two = shift(below, "gy", 1), shift(above, "gy", -1)
    (migrated,) = call(arrive_kernel, (slab,), (mine, below, above, below_two, above_two, far, owner))
    return (pop, phi, migrated.reshape(2, CX, CY, NZ))


def solution(mesh):
    in_specs = (
        P(None, "gx", "gy", None),
        P(None, "gx", "gy", None),
        P("gx", "gy", None),
        P("gx", "gy", None),
        P("gx", "gy", None),
        P("gx", "gy"),
    )
    out_specs = (P(None, "gx", "gy", None), P("gx", "gy", None), P(None, "gx", "gy", None))
    return jax.shard_map(body, mesh=mesh, in_specs=in_specs, out_specs=out_specs, check_vma=False)
```

```python
import jax
import jax.numpy as jnp
from jax import lax
from jax.experimental import pallas as pl
from jax.experimental.pallas import tpu as pltpu
from jax.sharding import PartitionSpec as P

STEPS = 2
SWEEPS = 4
VEL = (
    (0, 0, 0), (1, 0, 0), (-1, 0, 0), (0, 1, 0), (0, -1, 0), (0, 0, 1), (0, 0, -1),
    (1, 1, 0), (-1, -1, 0), (1, -1, 0), (-1, 1, 0), (1, 0, 1), (-1, 0, -1), (1, 0, -1),
    (-1, 0, 1), (0, 1, 1), (0, -1, -1), (0, 1, -1), (0, -1, 1),
)
WEIGHT = (1.0 / 3.0,) + (1.0 / 18.0,) * 6 + (1.0 / 36.0,) * 12
OPP = (0, 2, 1, 4, 3, 6, 5, 8, 7, 10, 9, 12, 11, 14, 13, 16, 15, 18, 17)
TAU = 0.8
COUPLING = 0.05
DRIVE = 0.001
DIFF = (0.1, 0.15)
VALENCE = (1.0, -1.0)

CX, CY, NZ = 8, 16, 128
EX, EY = 20, 32
F32 = jnp.float32

X_IN_LO = tuple(i for i in range(19) if VEL[i][0] == 1)
X_IN_HI = tuple(i for i in range(19) if VEL[i][0] == -1)
Y_IN_LO = tuple(i for i in range(19) if VEL[i][1] == 1)
Y_IN_HI = tuple(i for i in range(19) if VEL[i][1] == -1)
LO_LO, HI_LO = VEL.index((1, 1, 0)), VEL.index((-1, 1, 0))
LO_HI, HI_HI = VEL.index((1, -1, 0)), VEL.index((-1, -1, 0))


def shape(*dims):
    return jax.ShapeDtypeStruct(dims, F32)


def turn(v, by, axis):
    return pltpu.roll(v, by % v.shape[axis], axis)


class Plan:
    def __init__(self, first):
        self.first = first
        rows = [("phi", 6)] + [("perm", 6)] * first + [("charge", 4), ("conc", 2)] + [("fluid", 1)] * first
        self.y = {}
        at = 0
        for name, n in rows + [("pop", 5), ("dm", 4)] + [("owner", 1)] * (not first):
            self.y[name] = at
            at += n
        self.y_rows = -(-at // 8) * 8
        self.skip = 0 if first else 2
        planes = [("phi", 6 - self.skip)] + [("perm", 6)] * first + [("charge", 4), ("conc", 2)]
        planes += [("fluid", 1)] * first + [("pop", 5), ("dm", 4)]
        self.x = {}
        at = 0
        for name, n in planes:
            self.x[name] = at
            at += n
        self.x_planes = at
        self.c = {"phi": 0, "perm": 3, "charge": 3 + 3 * first, "misc": 5 + 3 * first}
        self.tiles = 6 + 3 * first


ONE, TWO = Plan(True), Plan(False)
DEEP = ((1, 6, 6, 1), (2, 5, 5, 2), (3, 4, 4, 3))
CHARGE = ((1, 5, 4, 2), (2, 4, 3, 3))


def pack_y(plan, out, low, owner, phi, charge, conc, pop, dm, perm=None, fluid=None):
    y = plan.y
    six = slice(0, 6) if low else slice(10, 16)
    four = slice(1, 5) if low else slice(11, 15)
    row = slice(0, 1) if low else slice(15, 16)
    out[:, 0:6] = phi[:, six]
    if plan.first:
        out[:, y["perm"] : y["perm"] + 6] = perm[:, six]
        out[:, y["fluid"] : y["fluid"] + 1] = fluid[:, row]
    out[:, y["charge"] : y["charge"] + 4] = charge[:, four]
    for s in range(2):
        out[:, y["conc"] + s : y["conc"] + s + 1] = conc[s, :, row]
    for k, i in enumerate(Y_IN_HI if low else Y_IN_LO):
        out[:, y["pop"] + k : y["pop"] + k + 1] = pop[i, :, row]
    for k in range(4):
        out[:, y["dm"] + k : y["dm"] + k + 1] = dm[k, :, row]
    if not plan.first:
        out[0, y["owner"] : y["owner"] + 1] = owner


def pack_x(plan, out, low, phi, charge, conc, pop, dm, perm=None, fluid=None):
    x = plan.x

    def spread(to, field, first, last):
        lo = first - 1 if low else CX - last
        out[to : to + last - first + 1] = field[lo : lo + last - first + 1]

    spread(0, phi, 1 + plan.skip, 6)
    spread(x["charge"], charge, 2, 5)
    edge = 0 if low else CX - 1
    for s in range(2):
        out[x["conc"] + s] = conc[s, edge]
    if plan.first:
        spread(x["perm"], perm, 1, 6)
        out[x["fluid"]] = fluid[edge]
    for k, i in enumerate(X_IN_HI if low else X_IN_LO):
        out[x["pop"] + k] = pop[i, edge]
    for k in range(4):
        out[x["dm"] + k] = dm[k, edge]


def pack_corners(plan, out, low, xl, xh, rim=None):
    x = plan.x

    def rows(n):
        return slice(0, n) if low else slice(16 - n, 16)

    for side, msg, names in ((0, xl, X_IN_LO), (1, xh, X_IN_HI)):
        base = side * plan.tiles

        def phi(d, r):
            if d <= plan.skip:
                return rim[1 + d if side else 2 - d, r]
            return msg[x["phi"] + (d - 1 - plan.skip if side else 6 - d), r]

        def perm(d, r):
            return msg[x["perm"] + (d - 1 if side else 6 - d), r]

        def charge(d, r):
            if d == 1:
                return msg[x["conc"], r] - msg[x["conc"] + 1, r]
            return msg[x["charge"] + (d - 2 if side else 5 - d), r]

        fields = [("phi", phi, DEEP), ("charge", charge, CHARGE)] + [("perm", perm, DEEP)] * plan.first
        for name, load, pairs in fields:
            for k, (d, n, e, m) in enumerate(pairs):
                tile = base + plan.c[name] + k
                if low:
                    out[tile, 0:n] = load(d, rows(n))
                    out[tile, 8 - m : 8] = load(e, rows(m))
                else:
                    out[tile, 8 - n : 8] = load(d, rows(n))
                    out[tile, 0:m] = load(e, rows(m))
        pick = (LO_HI, HI_HI)[side] if low else (LO_LO, HI_LO)[side]
        misc = base + plan.c["misc"]
        if plan.first:
            out[misc, 0:1] = msg[x["fluid"], rows(1)]
        out[misc, 1:2] = msg[x["pop"] + names.index(pick), rows(1)]
        for k in range(4):
            out[misc, 2 + k : 3 + k] = msg[x["dm"] + k, rows(1)]
        out[misc, 6:7] = charge(5, rows(1))


def lay(ext, own, name, plan, msgs):
    xl, xh, yl, yh, cl, ch = msgs
    x, y = plan.x, plan.y
    skip = plan.skip if name == "phi" else 0
    n = 6 - skip
    ext[6:14, 8:24] = own
    ext[0:n, 8:24] = xl[x[name] : x[name] + n]
    ext[14 + skip : 20, 8:24] = xh[x[name] : x[name] + n]
    ext[6:14, 2:8] = yl[:, y[name] : y[name] + 6]
    ext[6:14, 24:30] = yh[:, y[name] : y[name] + 6]
    corners(ext, plan, name, DEEP, cl, ch)


def corners(ext, plan, name, pairs, cl, ch):
    for k, (d, n, e, m) in enumerate(pairs):
        for side, p, q in ((0, 6 - d, 6 - e), (1, 13 + d, 13 + e)):
            tile = side * plan.tiles + plan.c[name] + k
            ext[p, 8 - n : 8] = cl[tile, 8 - n : 8]
            ext[q, 8 - m : 8] = cl[tile, 0:m]
            ext[p, 24 : 24 + n] = ch[tile, 0:n]
            ext[q, 24 : 24 + m] = ch[tile, 8 - m : 8]


def moments(load):
    dens = load(0)
    mom = [None, None, None]
    for i in range(1, 19):
        v = load(i)
        dens = dens + v
        for c in range(3):
            if VEL[i][c]:
                t = v if VEL[i][c] > 0 else -v
                mom[c] = t if mom[c] is None else mom[c] + t
    return [dens] + mom


def first_kernel(*refs):
    far, near, sems = refs[:5], refs[12:17], refs[17]
    pop, conc, phi, perm, mask = near
    x_hi, x_lo, y_hi, y_lo, dm, charge, fluid = refs[5:12]
    copies = [pltpu.make_async_copy(a, b, sems.at[k]) for k, (a, b) in enumerate(zip(far, near))]
    for copy in copies:
        copy.start()
    for copy in copies:
        copy.wait()
    charge[...] = conc[0] - conc[1]
    fluid[...] = mask[...].astype(F32)

    def plane(x, _):
        for k, v in enumerate(moments(lambda i: pop[i, x])):
            dm[k, x] = v
        return 0

    lax.fori_loop(0, CX, plane, 0, unroll=2)
    for low, xo, yo in ((False, x_hi, y_hi), (True, x_lo, y_lo)):
        pack_x(ONE, xo, low, phi, charge, conc, pop, dm, perm, fluid)
        pack_y(ONE, yo, low, None, phi, charge, conc, pop, dm, perm, fluid)


def corner_one_kernel(owner, xl, xh, c_hi, c_lo, owner_row):
    owner_row[...] = jnp.full((8, NZ), owner[0, 0], jnp.int32).astype(F32)
    pack_corners(ONE, c_hi, False, xl, xh)
    c_hi[ONE.c["misc"], 7:8] = owner_row[0:1]
    pack_corners(ONE, c_lo, True, xl, xh)


def corner_two_kernel(xl, xh, rim, c_hi, c_lo):
    pack_corners(TWO, c_hi, False, xl, xh, rim)
    pack_corners(TWO, c_lo, True, xl, xh, rim)


def lay_all(plan, phi, conc, dm, charge, msgs, pa, ce, dn, mm, cc):
    xl, xh, yl, yh, cl, ch = msgs
    x, y = plan.x, plan.y
    lay(pa, phi[...], "phi", plan, msgs)
    ce[6:14, 8:24] = charge[...]
    q = x["charge"]
    ce[1:5, 8:24] = xl[q : q + 4]
    ce[15:19, 8:24] = xh[q : q + 4]
    c = x["conc"]
    ce[5, 8:24] = xl[c] - xl[c + 1]
    ce[14, 8:24] = xh[c] - xh[c + 1]
    q, c = y["charge"], y["conc"]
    ce[6:14, 3:7] = yl[:, q : q + 4]
    ce[6:14, 7:8] = yl[:, c : c + 1] - yl[:, c + 1 : c + 2]
    ce[6:14, 24:25] = yh[:, c : c + 1] - yh[:, c + 1 : c + 2]
    ce[6:14, 25:29] = yh[:, q : q + 4]
    corners(ce, plan, "charge", CHARGE, cl, ch)
    misc = plan.c["misc"], plan.tiles + plan.c["misc"]
    for m, p in zip(misc, (1, 18)):
        ce[p, 7:8] = cl[m, 6:7]
        ce[p, 24:25] = ch[m, 6:7]
    for s in range(2):
        cc[s, 1:9, 8:24] = conc[s]
        cc[s, 0, 8:24] = xl[x["conc"] + s]
        cc[s, 9, 8:24] = xh[x["conc"] + s]
        cc[s, 1:9, 7:8] = yl[:, c + s : c + s + 1]
        cc[s, 1:9, 24:25] = yh[:, c + s : c + s + 1]
    for k, ext in enumerate((dn, mm.at[0], mm.at[1], mm.at[2])):
        ext[1:9, 8:24] = dm[k]
        for msg, m, p in ((xl, misc[0], 0), (xh, misc[1], 9)):
            ext[p, 8:24] = msg[x["dm"] + k]
            ext[p, 7:8] = cl[m, 2 + k : 3 + k]
            ext[p, 24:25] = ch[m, 2 + k : 3 + k]
        for msg, r in ((yl, 7), (yh, 24)):
            ext[1:9, r : r + 1] = msg[:, y["dm"] + k : y["dm"] + k + 1]


LO_T, MID_T, HI_T = slice(0, 8), slice(8, 24), slice(24, 32)


def sweeps(coef, inv, ce, src, dst):
    for sweep in range(SWEEPS):

        def relax(x, _, src=src, dst=dst):
            mid = src[x]
            acc = ce[x] * inv[x]
            acc += coef[0, x] * src[x - 1] + coef[1, x] * src[x + 1]
            acc += coef[2, x] * turn(mid, 1, 0) + coef[3, x] * turn(mid, -1, 0)
            acc += coef[4, x] * turn(mid, 1, 1) + coef[5, x] * turn(mid, -1, 1)
            dst[x] = acc
            return 0

        lax.fori_loop(1 + sweep, 19 - sweep, relax, 0, unroll=True)
        src, dst = dst, src
    return src


def motion(fin, ce, fl, dn, mm, vel, sh):
    def plane(p, _):
        mid = fin[p + 5]
        grad = [
            -0.5 * (fin[p + 6] - fin[p + 4]),
            -0.5 * (turn(mid, -1, 0) - turn(mid, 1, 0)),
            -0.5 * (turn(mid, -1, 1) - turn(mid, 1, 1)),
        ]
        f = fl[p]
        scale = COUPLING * ce[p + 5]
        force = [f * (scale * g + d) if d else f * (scale * g) for g, d in zip(grad, (DRIVE, 0, 0))]
        dens = dn[p]
        over = 1.0 / dens
        mom = [mm[c, p] for c in range(3)]
        for c in range(3):
            vel[c, p] = f * (mom[c] + 0.5 * force[c]) * over
        u = [(mom[c] + TAU * force[c]) * over for c in range(3)]
        for c in range(3):
            sh[c, p] = u[c]
        sh[3, p] = 1.0 - 1.5 * (u[0] * u[0] + u[1] * u[1] + u[2] * u[2])
        sh[4, p] = dens * (1.0 / TAU)
        return 0

    lax.fori_loop(0, 10, plane, 0, unroll=5)


def ions(fin, fl, cc, vel, store):
    def flux(s, ca, cb, pot_a, pot_b, ua, ub, wall):
        total = ca + cb
        speed = 0.25 * (ua + ub) - (0.5 * DIFF[s] * VALENCE[s]) * (pot_b - pot_a)
        return wall * (total * speed - DIFF[s] * (cb - ca))

    def x_face(s, p):
        wall = fl[p, MID_T] * fl[p + 1, MID_T]
        return flux(s, cc[s, p, MID_T], cc[s, p + 1, MID_T], fin[p + 5, MID_T], fin[p + 6, MID_T],
                    vel[0, p, MID_T], vel[0, p + 1, MID_T], wall)

    def plane(p, before):
        after = []
        f, pot, vy = fl[p], fin[p + 5], vel[1, p]
        for s in range(2):
            face = x_face(s, p)
            total = face - before[s]
            after.append(face)
            c = cc[s, p]
            face = flux(s, c, turn(c, -1, 0), pot, turn(pot, -1, 0), vy, turn(vy, -1, 0), f * turn(f, -1, 0))
            total = total + (face - turn(face, 1, 0))[MID_T]
            fm, cm, pm, vz = f[MID_T], c[MID_T], pot[MID_T], vel[2, p, MID_T]
            face = flux(s, cm, turn(cm, -1, 1), pm, turn(pm, -1, 1), vz, turn(vz, -1, 1), fm * turn(fm, -1, 1))
            total = total + face - turn(face, 1, 1)
            store(s, p - 1, cm - total)
        return tuple(after)

    lax.fori_loop(1, 9, plane, (x_face(0, 0), x_face(1, 0)), unroll=8)


def collide_and_stream(plan, pop, fl, sh, msgs, lv, pop_out, dm_out):
    xl, xh, yl, yh, cl, ch = msgs
    y_pop, x_pop = plan.y["pop"], plan.x["pop"]
    bad = float("nan")

    def load(p, rows):
        return [sh[c, p, rows] for c in range(5)] + [fl[p, rows] != 0.0]

    def relaxed_of(i, pop_i, part):
        pr = None
        for c in range(3):
            if VEL[i][c]:
                t = part[c] if VEL[i][c] > 0 else -part[c]
                pr = t if pr is None else pr + t
        poly = part[3]
        if pr is not None:
            poly = poly + pr * (3.0 + 4.5 * pr)
        return (1.0 - 1.0 / TAU) * pop_i + (WEIGHT[i] * part[4]) * poly

    def collide(p, _):
        x = p - 1
        part = load(p, MID_T)
        wet = part[5]
        for i in range(19):
            j = OPP[i]
            if i > j:
                continue
            pi = pop[i, x]
            ri = relaxed_of(i, pi, part)
            if i == j:
                pop_out[i, x] = jnp.where(wet, ri, pi)
                continue
            pj = pop[j, x]
            rj = relaxed_of(j, pj, part)
            lv[i, p, MID_T] = jnp.where(wet, ri, bad)
            lv[j, p, MID_T] = jnp.where(wet, rj, bad)
            pop_out[i, x] = jnp.where(wet, rj, pi)
            pop_out[j, x] = jnp.where(wet, ri, pj)
        for y, names, r in ((yl, Y_IN_LO, 7), (yh, Y_IN_HI, 24)):
            row = slice(r, r + 1)
            part = load(p, row)
            for k, i in enumerate(names):
                value = relaxed_of(i, y[x, y_pop + k : y_pop + k + 1], part)
                lv[i, p, row] = jnp.where(part[5], value, bad)
        return 0

    lax.fori_loop(1, 9, collide, 0)
    for p, side, x, names, low_pop, high_pop in (
        (0, 0, xl, X_IN_LO, LO_LO, LO_HI),
        (9, 1, xh, X_IN_HI, HI_LO, HI_HI),
    ):
        misc = side * plan.tiles + plan.c["misc"]
        part = load(p, MID_T)
        for k, i in enumerate(names):
            lv[i, p, MID_T] = jnp.where(part[5], relaxed_of(i, x[x_pop + k], part), bad)
        for c, r, i in ((cl, 7, low_pop), (ch, 24, high_pop)):
            row = slice(r, r + 1)
            part = load(p, row)
            lv[i, p, row] = jnp.where(part[5], relaxed_of(i, c[misc, 1:2], part), bad)

    def stream(x, _):
        wet = fl[x + 1, MID_T] != 0.0
        for i in range(1, 19):
            ex, ey, ez = VEL[i]
            came = lv[i, x + 1 - ex, 8 - ey : 24 - ey]
            if ez:
                came = turn(came, ez, 1)
            pop_out[i, x] = jnp.where(wet & (came == came), came, pop_out[i, x])
        if dm_out is not None:
            for k, v in enumerate(moments(lambda i: pop_out[i, x])):
                dm_out[k, x] = v
        return 0

    lax.fori_loop(0, CX, stream, 0, unroll=4)


def step_one_kernel(pop, conc, phi, perm, dm, charge, fluid, xl, xh, yl, yh, cl, ch,
                    pop_out, phi_out, conc_out, charge_out, x_hi, x_lo, y_hi, y_lo, dm_out, rim, coef, inv, fl,
                    pe, pa, pb, ce, dn, mm, cc, vel, sh, lv):
    msgs = (xl, xh, yl, yh, cl, ch)
    lay(pe, perm[...], "perm", ONE, msgs)

    def coefs(x, _):
        mid = pe[x]
        faces = [0.5 * (mid + other) for other in (
            pe[x - 1], pe[x + 1], turn(mid, 1, 0), turn(mid, -1, 0), turn(mid, 1, 1), turn(mid, -1, 1))]
        over = 1.0 / (faces[0] + faces[1] + faces[2] + faces[3] + faces[4] + faces[5])
        inv[x] = over
        for k in range(6):
            coef[k, x] = faces[k] * over
        return 0

    lax.fori_loop(1, 19, coefs, 0, unroll=9)
    fl[1:9, 8:24] = fluid[...]
    x, y = ONE.x, ONE.y
    for side, msg, p in ((0, xl, 0), (1, xh, 9)):
        m = side * ONE.tiles + ONE.c["misc"]
        fl[p, 8:24] = msg[x["fluid"]]
        fl[p, 7:8] = cl[m, 0:1]
        fl[p, 24:25] = ch[m, 0:1]
    fl[1:9, 7:8] = yl[:, y["fluid"] : y["fluid"] + 1]
    fl[1:9, 24:25] = yh[:, y["fluid"] : y["fluid"] + 1]
    lay_all(ONE, phi, conc, dm, charge, msgs, pa, ce, dn, mm, cc)
    fin = sweeps(coef, inv, ce, pa, pb)
    phi_out[...] = fin[6:14, MID_T]
    rim[0:2] = fin[4:6, MID_T]
    rim[2:4] = fin[14:16, MID_T]
    motion(fin, ce, fl, dn, mm, vel, sh)

    def store(s, x, values):
        conc_out[s, x] = values

    ions(fin, fl, cc, vel, store)
    collide_and_stream(ONE, pop, fl, sh, msgs, lv, pop_out, dm_out)
    charge_out[...] = conc_out[0] - conc_out[1]
    for low, xo, yo in ((False, x_hi, y_hi), (True, x_lo, y_lo)):
        pack_x(TWO, xo, low, phi_out, charge_out, conc_out, pop_out, dm_out)
        pack_y(TWO, yo, low, cl[ONE.c["misc"], 7:8], phi_out, charge_out, conc_out, pop_out, dm_out)


def ions_two_kernel(conc, phi, charge, dm, rim, coef, inv, fl, xl, xh, yl, yh, cl, ch,
                    phi_out, slab, sh, pa, pb, ce, dn, mm, cc, vel):
    lay_all(TWO, phi, conc, dm, charge, (xl, xh, yl, yh, cl, ch), pa, ce, dn, mm, cc)
    pa[4:6, MID_T] = rim[0:2]
    pa[14:16, MID_T] = rim[2:4]
    fin = sweeps(coef, inv, ce, pa, pb)
    phi_out[...] = fin[6:14, MID_T]
    motion(fin, ce, fl, dn, mm, vel, sh)

    def store(s, x, values):
        slab[s * CX + x] = values

    ions(fin, fl, cc, vel, store)
    slab[2 * CX, 0:8] = jnp.broadcast_to(yl[0, TWO.y["owner"] : TWO.y["owner"] + 1], (8, NZ))


def flow_two_kernel(pop, fl, sh, xl, xh, yl, yh, cl, ch, pop_out, lv):
    collide_and_stream(TWO, pop, fl, sh, (xl, xh, yl, yh, cl, ch), lv, pop_out, None)


def place(up):
    me = lax.rem(lax.axis_index("gy") + up, 8)
    return jnp.full((1, NZ), me, jnp.int32).astype(F32)


def route_kernel(mine, below, above, out, on):
    want = below[2 * CX, 0:1]
    for x in range(2 * CX):
        out[x] = jnp.where(want == place(0), mine[x], above[x])
        on[x] = below[x]


def arrive_kernel(mine, below, above, below_two, above_two, below_three, far, owner, out):
    slab = owner[0:1]
    near = ((0, mine), (7, below), (1, above), (6, below_two), (2, above_two), (5, below_three))
    for x in range(2 * CX):
        v = far[x]
        for up, values in near:
            v = jnp.where(slab == place(up), values[x], v)
        out[x] = v


VMEM, FAR, SMEM = (pl.BlockSpec(memory_space=m) for m in (pltpu.VMEM, pltpu.HBM, pltpu.SMEM))


def call(kernel, outs, args, scratch=(), specs=None, flops=0):
    return pl.pallas_call(
        kernel,
        out_shape=outs,
        in_specs=specs or [VMEM] * len(args),
        out_specs=[VMEM] * len(outs),
        scratch_shapes=[pltpu.VMEM(s, F32) if isinstance(s, tuple) else s for s in scratch],
        compiler_params=pltpu.CompilerParams(vmem_limit_bytes=24 * 1024 * 1024),
        cost_estimate=pl.CostEstimate(flops=flops, bytes_accessed=0, transcendentals=0) if flops else None,
    )(*args)


HALO = (EX, EY, NZ)
RIM = (10, EY, NZ)
FIELDS = (HALO, HALO, HALO, RIM, (3,) + RIM, (2,) + RIM, (3,) + RIM)


def shift(values, axis, by):
    n = lax.axis_size(axis)
    return lax.ppermute(values, axis, [(i, (i + by) % n) for i in range(n)])


def exchange(x_hi, x_lo, y_hi, y_lo):
    yl, yh = shift(y_hi, "gy", 1), shift(y_lo, "gy", -1)
    xl, xh = shift(x_hi, "gx", 1), shift(x_lo, "gx", -1)
    return xl, xh, yl, yh


def body(populations, concentration, potential, permittivity, fluid_mask, owners):
    block, row = shape(CX, CY, NZ), shape(8, NZ)
    pops, both, four = shape(19, CX, CY, NZ), shape(2, CX, CY, NZ), shape(4, CX, CY, NZ)

    def messages(plan):
        x, y = shape(plan.x_planes, CY, NZ), shape(CX, plan.y_rows, NZ)
        return (x, x, y, y)

    def tiles(plan):
        return (shape(2 * plan.tiles, 8, NZ),) * 2

    *sent, dm, charge, fluid = call(
        first_kernel, messages(ONE) + (four, block, block),
        tuple(pltpu.with_memory_space_constraint(v, pltpu.HBM) for v in (
            populations, concentration, potential, permittivity, fluid_mask)),
        (pops.shape, both.shape, block.shape, block.shape, pltpu.VMEM(block.shape, jnp.int32),
         pltpu.SemaphoreType.DMA((5,))),
        [FAR] * 5)
    got = exchange(*sent)
    c_hi, c_lo, owner = call(corner_one_kernel, tiles(ONE) + (row,), (owners,) + got[:2], (), [SMEM, VMEM, VMEM])
    got += (shift(c_hi, "gy", 1), shift(c_lo, "gy", -1))
    pop, phi, conc, charge, *rest = call(
        step_one_kernel,
        (pops, block, both, block) + messages(TWO)
        + (four, shape(4, CY, NZ), shape(6, *HALO), shape(*HALO), shape(*RIM)),
        (populations, concentration, potential, permittivity, dm, charge, fluid) + got,
        (HALO,) + FIELDS + ((5,) + RIM, (19,) + RIM))
    sent, (dm, rim, coef, inv, fl) = rest[:4], rest[4:]
    got = exchange(*sent)
    c_hi, c_lo = call(corner_two_kernel, tiles(TWO), got[:2] + (rim,))
    got += (shift(c_hi, "gy", 1), shift(c_lo, "gy", -1))
    slab = shape(2 * CX, CY, NZ)
    phi, mine, sh = call(
        ions_two_kernel, (block, shape(2 * CX + 1, CY, NZ), shape(5, *RIM)),
        (conc, phi, charge, dm, rim, coef, inv, fl) + got, FIELDS)
    below, above = shift(mine, "gy", 1), shift(mine, "gy", -1)
    (pop,) = call(flow_two_kernel, (pops,), (pop, fl, sh) + got, ((19,) + RIM,), flops=40_000_000)
    routed, on = call(route_kernel, (slab, slab), (mine, below, above))
    far = shift(routed, "gy", 5)
    below_two, above_two = shift(on, "gy", 1), shift(above, "gy", -1)
    below_three = shift(below_two, "gy", 1)
    (migrated,) = call(
        arrive_kernel, (slab,), (mine, below, above, below_two, above_two, below_three, far, owner))
    return (pop, phi, migrated.reshape(2, CX, CY, NZ))


def solution(mesh):
    in_specs = (
        P(None, "gx", "gy", None),
        P(None, "gx", "gy", None),
        P("gx", "gy", None),
        P("gx", "gy", None),
        P("gx", "gy", None),
        P("gx", "gy"),
    )
    out_specs = (P(None, "gx", "gy", None), P("gx", "gy", None), P(None, "gx", "gy", None))
    return jax.shard_map(body, mesh=mesh, in_specs=in_specs, out_specs=out_specs, check_vma=False)
```

```python
import jax
import jax.numpy as jnp
from jax import lax
from jax.experimental import pallas as pl
from jax.experimental.pallas import tpu as pltpu
from jax.sharding import PartitionSpec as P

STEPS = 2
SWEEPS = 4
VEL = (
    (0, 0, 0), (1, 0, 0), (-1, 0, 0), (0, 1, 0), (0, -1, 0), (0, 0, 1), (0, 0, -1),
    (1, 1, 0), (-1, -1, 0), (1, -1, 0), (-1, 1, 0), (1, 0, 1), (-1, 0, -1), (1, 0, -1),
    (-1, 0, 1), (0, 1, 1), (0, -1, -1), (0, 1, -1), (0, -1, 1),
)
WEIGHT = (1.0 / 3.0,) + (1.0 / 18.0,) * 6 + (1.0 / 36.0,) * 12
OPP = (0, 2, 1, 4, 3, 6, 5, 8, 7, 10, 9, 12, 11, 14, 13, 16, 15, 18, 17)
TAU = 0.8
COUPLING = 0.05
DRIVE = 0.001
DIFF = (0.1, 0.15)
VALENCE = (1.0, -1.0)

CX, CY, NZ = 8, 16, 128
EX, EY = 20, 32
F32 = jnp.float32

X_IN_LO = tuple(i for i in range(19) if VEL[i][0] == 1)
X_IN_HI = tuple(i for i in range(19) if VEL[i][0] == -1)
Y_IN_LO = tuple(i for i in range(19) if VEL[i][1] == 1)
Y_IN_HI = tuple(i for i in range(19) if VEL[i][1] == -1)
LO_LO, HI_LO = VEL.index((1, 1, 0)), VEL.index((-1, 1, 0))
LO_HI, HI_HI = VEL.index((1, -1, 0)), VEL.index((-1, -1, 0))


def shape(*dims):
    return jax.ShapeDtypeStruct(dims, F32)


def turn(v, by, axis):
    return pltpu.roll(v, by % v.shape[axis], axis)


class Plan:
    def __init__(self, first):
        self.first = first
        rows = [("phi", 6)] + [("perm", 6)] * first + [("charge", 4), ("conc", 2)] + [("fluid", 1)] * first
        self.y = {}
        at = 0
        for name, n in rows + [("pop", 5), ("dm", 4)] + [("owner", 1)] * (not first):
            self.y[name] = at
            at += n
        self.y_rows = -(-at // 8) * 8
        self.skip = 0 if first else 2
        planes = [("phi", 6 - self.skip)] + [("perm", 6)] * first + [("charge", 4), ("conc", 2)]
        planes += [("fluid", 1)] * first + [("pop", 5), ("dm", 4)]
        self.x = {}
        at = 0
        for name, n in planes:
            self.x[name] = at
            at += n
        self.x_planes = at
        self.c = {"phi": 0, "perm": 3, "charge": 3 + 3 * first, "misc": 5 + 3 * first}
        self.tiles = 6 + 3 * first


ONE, TWO = Plan(True), Plan(False)
DEEP = ((1, 6, 6, 1), (2, 5, 5, 2), (3, 4, 4, 3))
CHARGE = ((1, 5, 4, 2), (2, 4, 3, 3))


def pack_y(plan, out, low, owner, phi, charge, conc, pop, dm, perm=None, fluid=None):
    y = plan.y
    six = slice(0, 6) if low else slice(10, 16)
    four = slice(1, 5) if low else slice(11, 15)
    row = slice(0, 1) if low else slice(15, 16)
    out[:, 0:6] = phi[:, six]
    if plan.first:
        out[:, y["perm"] : y["perm"] + 6] = perm[:, six]
        out[:, y["fluid"] : y["fluid"] + 1] = fluid[:, row]
    out[:, y["charge"] : y["charge"] + 4] = charge[:, four]
    for s in range(2):
        out[:, y["conc"] + s : y["conc"] + s + 1] = conc[s, :, row]
    for k, i in enumerate(Y_IN_HI if low else Y_IN_LO):
        out[:, y["pop"] + k : y["pop"] + k + 1] = pop[i, :, row]
    for k in range(4):
        out[:, y["dm"] + k : y["dm"] + k + 1] = dm[k, :, row]
    if not plan.first:
        out[0, y["owner"] : y["owner"] + 1] = owner


def pack_x(plan, out, low, phi, charge, conc, pop, dm, perm=None, fluid=None):
    x = plan.x

    def spread(to, field, first, last):
        lo = first - 1 if low else CX - last
        out[to : to + last - first + 1] = field[lo : lo + last - first + 1]

    spread(0, phi, 1 + plan.skip, 6)
    spread(x["charge"], charge, 2, 5)
    edge = 0 if low else CX - 1
    for s in range(2):
        out[x["conc"] + s] = conc[s, edge]
    if plan.first:
        spread(x["perm"], perm, 1, 6)
        out[x["fluid"]] = fluid[edge]
    for k, i in enumerate(X_IN_HI if low else X_IN_LO):
        out[x["pop"] + k] = pop[i, edge]
    for k in range(4):
        out[x["dm"] + k] = dm[k, edge]


def pack_corners(plan, out, low, xl, xh, rim=None):
    x = plan.x

    def rows(n):
        return slice(0, n) if low else slice(16 - n, 16)

    for side, msg, names in ((0, xl, X_IN_LO), (1, xh, X_IN_HI)):
        base = side * plan.tiles

        def phi(d, r):
            if d <= plan.skip:
                return rim[1 + d if side else 2 - d, r]
            return msg[x["phi"] + (d - 1 - plan.skip if side else 6 - d), r]

        def perm(d, r):
            return msg[x["perm"] + (d - 1 if side else 6 - d), r]

        def charge(d, r):
            if d == 1:
                return msg[x["conc"], r] - msg[x["conc"] + 1, r]
            return msg[x["charge"] + (d - 2 if side else 5 - d), r]

        fields = [("phi", phi, DEEP), ("charge", charge, CHARGE)] + [("perm", perm, DEEP)] * plan.first
        for name, load, pairs in fields:
            for k, (d, n, e, m) in enumerate(pairs):
                tile = base + plan.c[name] + k
                if low:
                    out[tile, 0:n] = load(d, rows(n))
                    out[tile, 8 - m : 8] = load(e, rows(m))
                else:
                    out[tile, 8 - n : 8] = load(d, rows(n))
                    out[tile, 0:m] = load(e, rows(m))
        pick = (LO_HI, HI_HI)[side] if low else (LO_LO, HI_LO)[side]
        misc = base + plan.c["misc"]
        if plan.first:
            out[misc, 0:1] = msg[x["fluid"], rows(1)]
        out[misc, 1:2] = msg[x["pop"] + names.index(pick), rows(1)]
        for k in range(4):
            out[misc, 2 + k : 3 + k] = msg[x["dm"] + k, rows(1)]
        out[misc, 6:7] = charge(5, rows(1))


def lay(ext, own, name, plan, msgs):
    xl, xh, yl, yh, cl, ch = msgs
    x, y = plan.x, plan.y
    skip = plan.skip if name == "phi" else 0
    n = 6 - skip
    ext[6:14, 8:24] = own
    ext[0:n, 8:24] = xl[x[name] : x[name] + n]
    ext[14 + skip : 20, 8:24] = xh[x[name] : x[name] + n]
    ext[6:14, 2:8] = yl[:, y[name] : y[name] + 6]
    ext[6:14, 24:30] = yh[:, y[name] : y[name] + 6]
    corners(ext, plan, name, DEEP, cl, ch)


def corners(ext, plan, name, pairs, cl, ch):
    for k, (d, n, e, m) in enumerate(pairs):
        for side, p, q in ((0, 6 - d, 6 - e), (1, 13 + d, 13 + e)):
            tile = side * plan.tiles + plan.c[name] + k
            ext[p, 8 - n : 8] = cl[tile, 8 - n : 8]
            ext[q, 8 - m : 8] = cl[tile, 0:m]
            ext[p, 24 : 24 + n] = ch[tile, 0:n]
            ext[q, 24 : 24 + m] = ch[tile, 8 - m : 8]


def moments(load):
    dens = load(0)
    mom = [None, None, None]
    for i in range(1, 19):
        v = load(i)
        dens = dens + v
        for c in range(3):
            if VEL[i][c]:
                t = v if VEL[i][c] > 0 else -v
                mom[c] = t if mom[c] is None else mom[c] + t
    return [dens] + mom


def first_kernel(*refs):
    far, near, sems = refs[:5], refs[12:17], refs[17]
    pop, conc, phi, perm, mask = near
    x_hi, x_lo, y_hi, y_lo, dm, charge, fluid = refs[5:12]
    copies = [pltpu.make_async_copy(a, b, sems.at[k]) for k, (a, b) in enumerate(zip(far, near))]
    for copy in copies:
        copy.start()
    for copy in copies:
        copy.wait()
    charge[...] = conc[0] - conc[1]
    fluid[...] = mask[...].astype(F32)

    def plane(x, _):
        for k, v in enumerate(moments(lambda i: pop[i, x])):
            dm[k, x] = v
        return 0

    lax.fori_loop(0, CX, plane, 0, unroll=2)
    for low, xo, yo in ((False, x_hi, y_hi), (True, x_lo, y_lo)):
        pack_x(ONE, xo, low, phi, charge, conc, pop, dm, perm, fluid)
        pack_y(ONE, yo, low, None, phi, charge, conc, pop, dm, perm, fluid)


def corner_one_kernel(owner, xl, xh, c_hi, c_lo, owner_row):
    owner_row[...] = jnp.full((8, NZ), owner[0, 0], jnp.int32).astype(F32)
    pack_corners(ONE, c_hi, False, xl, xh)
    c_hi[ONE.c["misc"], 7:8] = owner_row[0:1]
    pack_corners(ONE, c_lo, True, xl, xh)
    c_lo[ONE.c["misc"], 7:8] = owner_row[0:1]


def corner_two_kernel(xl, xh, rim, c_hi, c_lo):
    pack_corners(TWO, c_hi, False, xl, xh, rim)
    pack_corners(TWO, c_lo, True, xl, xh, rim)


def lay_all(plan, phi, conc, dm, charge, msgs, pa, ce, dn, mm, cc):
    xl, xh, yl, yh, cl, ch = msgs
    x, y = plan.x, plan.y
    lay(pa, phi[...], "phi", plan, msgs)
    ce[6:14, 8:24] = charge[...]
    q = x["charge"]
    ce[1:5, 8:24] = xl[q : q + 4]
    ce[15:19, 8:24] = xh[q : q + 4]
    c = x["conc"]
    ce[5, 8:24] = xl[c] - xl[c + 1]
    ce[14, 8:24] = xh[c] - xh[c + 1]
    q, c = y["charge"], y["conc"]
    ce[6:14, 3:7] = yl[:, q : q + 4]
    ce[6:14, 7:8] = yl[:, c : c + 1] - yl[:, c + 1 : c + 2]
    ce[6:14, 24:25] = yh[:, c : c + 1] - yh[:, c + 1 : c + 2]
    ce[6:14, 25:29] = yh[:, q : q + 4]
    corners(ce, plan, "charge", CHARGE, cl, ch)
    misc = plan.c["misc"], plan.tiles + plan.c["misc"]
    for m, p in zip(misc, (1, 18)):
        ce[p, 7:8] = cl[m, 6:7]
        ce[p, 24:25] = ch[m, 6:7]
    for s in range(2):
        cc[s, 1:9, 8:24] = conc[s]
        cc[s, 0, 8:24] = xl[x["conc"] + s]
        cc[s, 9, 8:24] = xh[x["conc"] + s]
        cc[s, 1:9, 7:8] = yl[:, c + s : c + s + 1]
        cc[s, 1:9, 24:25] = yh[:, c + s : c + s + 1]
    for k, ext in enumerate((dn, mm.at[0], mm.at[1], mm.at[2])):
        ext[1:9, 8:24] = dm[k]
        for msg, m, p in ((xl, misc[0], 0), (xh, misc[1], 9)):
            ext[p, 8:24] = msg[x["dm"] + k]
            ext[p, 7:8] = cl[m, 2 + k : 3 + k]
            ext[p, 24:25] = ch[m, 2 + k : 3 + k]
        for msg, r in ((yl, 7), (yh, 24)):
            ext[1:9, r : r + 1] = msg[:, y["dm"] + k : y["dm"] + k + 1]


LO_T, MID_T, HI_T = slice(0, 8), slice(8, 24), slice(24, 32)


def sweeps(coef, inv, ce, src, dst):
    for sweep in range(SWEEPS):

        def relax(x, _, src=src, dst=dst):
            mid = src[x]
            acc = ce[x] * inv[x]
            acc += coef[0, x] * src[x - 1] + coef[1, x] * src[x + 1]
            acc += coef[2, x] * turn(mid, 1, 0) + coef[3, x] * turn(mid, -1, 0)
            acc += coef[4, x] * turn(mid, 1, 1) + coef[5, x] * turn(mid, -1, 1)
            dst[x] = acc
            return 0

        lax.fori_loop(1 + sweep, 19 - sweep, relax, 0, unroll=True)
        src, dst = dst, src
    return src


def motion(fin, ce, fl, dn, mm, vel, sh):
    def plane(p, _):
        mid = fin[p + 5]
        grad = [
            -0.5 * (fin[p + 6] - fin[p + 4]),
            -0.5 * (turn(mid, -1, 0) - turn(mid, 1, 0)),
            -0.5 * (turn(mid, -1, 1) - turn(mid, 1, 1)),
        ]
        f = fl[p]
        scale = COUPLING * ce[p + 5]
        force = [f * (scale * g + d) if d else f * (scale * g) for g, d in zip(grad, (DRIVE, 0, 0))]
        dens = dn[p]
        over = 1.0 / dens
        mom = [mm[c, p] for c in range(3)]
        for c in range(3):
            vel[c, p] = f * (mom[c] + 0.5 * force[c]) * over
        u = [(mom[c] + TAU * force[c]) * over for c in range(3)]
        for c in range(3):
            sh[c, p] = u[c]
        sh[3, p] = 1.0 - 1.5 * (u[0] * u[0] + u[1] * u[1] + u[2] * u[2])
        sh[4, p] = dens * (1.0 / TAU)
        return 0

    lax.fori_loop(0, 10, plane, 0, unroll=5)


def ions(fin, fl, cc, vel, store):
    def flux(s, ca, cb, pot_a, pot_b, ua, ub, wall):
        total = ca + cb
        speed = 0.25 * (ua + ub) - (0.5 * DIFF[s] * VALENCE[s]) * (pot_b - pot_a)
        return wall * (total * speed - DIFF[s] * (cb - ca))

    def x_face(s, p):
        wall = fl[p, MID_T] * fl[p + 1, MID_T]
        return flux(s, cc[s, p, MID_T], cc[s, p + 1, MID_T], fin[p + 5, MID_T], fin[p + 6, MID_T],
                    vel[0, p, MID_T], vel[0, p + 1, MID_T], wall)

    def plane(p, before):
        after = []
        f, pot, vy = fl[p], fin[p + 5], vel[1, p]
        for s in range(2):
            face = x_face(s, p)
            total = face - before[s]
            after.append(face)
            c = cc[s, p]
            face = flux(s, c, turn(c, -1, 0), pot, turn(pot, -1, 0), vy, turn(vy, -1, 0), f * turn(f, -1, 0))
            total = total + (face - turn(face, 1, 0))[MID_T]
            fm, cm, pm, vz = f[MID_T], c[MID_T], pot[MID_T], vel[2, p, MID_T]
            face = flux(s, cm, turn(cm, -1, 1), pm, turn(pm, -1, 1), vz, turn(vz, -1, 1), fm * turn(fm, -1, 1))
            total = total + face - turn(face, 1, 1)
            store(s, p - 1, cm - total)
        return tuple(after)

    lax.fori_loop(1, 9, plane, (x_face(0, 0), x_face(1, 0)), unroll=8)


def collide_and_stream(plan, pop, fl, sh, msgs, lv, pop_out, dm_out):
    xl, xh, yl, yh, cl, ch = msgs
    y_pop, x_pop = plan.y["pop"], plan.x["pop"]
    bad = float("nan")

    def load(p, rows):
        return [sh[c, p, rows] for c in range(5)] + [fl[p, rows] != 0.0]

    def relaxed_of(i, pop_i, part):
        pr = None
        for c in range(3):
            if VEL[i][c]:
                t = part[c] if VEL[i][c] > 0 else -part[c]
                pr = t if pr is None else pr + t
        poly = part[3]
        if pr is not None:
            poly = poly + pr * (3.0 + 4.5 * pr)
        return (1.0 - 1.0 / TAU) * pop_i + (WEIGHT[i] * part[4]) * poly

    def collide(p, _):
        x = p - 1
        part = load(p, MID_T)
        wet = part[5]
        for i in range(19):
            j = OPP[i]
            if i > j:
                continue
            pi = pop[i, x]
            ri = relaxed_of(i, pi, part)
            if i == j:
                pop_out[i, x] = jnp.where(wet, ri, pi)
                continue
            pj = pop[j, x]
            rj = relaxed_of(j, pj, part)
            lv[i, p, MID_T] = jnp.where(wet, ri, bad)
            lv[j, p, MID_T] = jnp.where(wet, rj, bad)
            pop_out[i, x] = jnp.where(wet, rj, pi)
            pop_out[j, x] = jnp.where(wet, ri, pj)
        for y, names, r in ((yl, Y_IN_LO, 7), (yh, Y_IN_HI, 24)):
            row = slice(r, r + 1)
            part = load(p, row)
            for k, i in enumerate(names):
                value = relaxed_of(i, y[x, y_pop + k : y_pop + k + 1], part)
                lv[i, p, row] = jnp.where(part[5], value, bad)
        return 0

    lax.fori_loop(1, 9, collide, 0)
    for p, side, x, names, low_pop, high_pop in (
        (0, 0, xl, X_IN_LO, LO_LO, LO_HI),
        (9, 1, xh, X_IN_HI, HI_LO, HI_HI),
    ):
        misc = side * plan.tiles + plan.c["misc"]
        part = load(p, MID_T)
        for k, i in enumerate(names):
            lv[i, p, MID_T] = jnp.where(part[5], relaxed_of(i, x[x_pop + k], part), bad)
        for c, r, i in ((cl, 7, low_pop), (ch, 24, high_pop)):
            row = slice(r, r + 1)
            part = load(p, row)
            lv[i, p, row] = jnp.where(part[5], relaxed_of(i, c[misc, 1:2], part), bad)

    def stream(x, _):
        wet = fl[x + 1, MID_T] != 0.0
        for i in range(1, 19):
            ex, ey, ez = VEL[i]
            came = lv[i, x + 1 - ex, 8 - ey : 24 - ey]
            if ez:
                came = turn(came, ez, 1)
            pop_out[i, x] = jnp.where(wet & (came == came), came, pop_out[i, x])
        if dm_out is not None:
            for k, v in enumerate(moments(lambda i: pop_out[i, x])):
                dm_out[k, x] = v
        return 0

    lax.fori_loop(0, CX, stream, 0, unroll=4)


def step_one_kernel(pop, conc, phi, perm, dm, charge, fluid, xl, xh, yl, yh, cl, ch,
                    pop_out, phi_out, conc_out, charge_out, x_hi, x_lo, y_hi, y_lo, dm_out, rim, coef, inv, fl,
                    pe, pa, pb, ce, dn, mm, cc, vel, sh, lv):
    msgs = (xl, xh, yl, yh, cl, ch)
    lay(pe, perm[...], "perm", ONE, msgs)

    def coefs(x, _):
        mid = pe[x]
        faces = [0.5 * (mid + other) for other in (
            pe[x - 1], pe[x + 1], turn(mid, 1, 0), turn(mid, -1, 0), turn(mid, 1, 1), turn(mid, -1, 1))]
        over = 1.0 / (faces[0] + faces[1] + faces[2] + faces[3] + faces[4] + faces[5])
        inv[x] = over
        for k in range(6):
            coef[k, x] = faces[k] * over
        return 0

    lax.fori_loop(1, 19, coefs, 0, unroll=9)
    fl[1:9, 8:24] = fluid[...]
    x, y = ONE.x, ONE.y
    for side, msg, p in ((0, xl, 0), (1, xh, 9)):
        m = side * ONE.tiles + ONE.c["misc"]
        fl[p, 8:24] = msg[x["fluid"]]
        fl[p, 7:8] = cl[m, 0:1]
        fl[p, 24:25] = ch[m, 0:1]
    fl[1:9, 7:8] = yl[:, y["fluid"] : y["fluid"] + 1]
    fl[1:9, 24:25] = yh[:, y["fluid"] : y["fluid"] + 1]
    lay_all(ONE, phi, conc, dm, charge, msgs, pa, ce, dn, mm, cc)
    fin = sweeps(coef, inv, ce, pa, pb)
    phi_out[...] = fin[6:14, MID_T]
    rim[0:2] = fin[4:6, MID_T]
    rim[2:4] = fin[14:16, MID_T]
    motion(fin, ce, fl, dn, mm, vel, sh)

    def store(s, x, values):
        conc_out[s, x] = values

    ions(fin, fl, cc, vel, store)
    collide_and_stream(ONE, pop, fl, sh, msgs, lv, pop_out, dm_out)
    charge_out[...] = conc_out[0] - conc_out[1]
    for low, xo, yo in ((False, x_hi, y_hi), (True, x_lo, y_lo)):
        pack_x(TWO, xo, low, phi_out, charge_out, conc_out, pop_out, dm_out)
        pack_y(TWO, yo, low, (ch if low else cl)[ONE.c["misc"], 7:8], phi_out, charge_out, conc_out, pop_out, dm_out)


def ions_two_kernel(conc, phi, charge, dm, rim, coef, inv, fl, xl, xh, yl, yh, cl, ch,
                    phi_out, slab, sh, pa, pb, ce, dn, mm, cc, vel):
    lay_all(TWO, phi, conc, dm, charge, (xl, xh, yl, yh, cl, ch), pa, ce, dn, mm, cc)
    pa[4:6, MID_T] = rim[0:2]
    pa[14:16, MID_T] = rim[2:4]
    fin = sweeps(coef, inv, ce, pa, pb)
    phi_out[...] = fin[6:14, MID_T]
    motion(fin, ce, fl, dn, mm, vel, sh)

    def store(s, x, values):
        slab[s * CX + x] = values

    ions(fin, fl, cc, vel, store)
    for msg, rows in ((yl, LO_T), (yh, slice(8, 16))):
        slab[2 * CX, rows] = jnp.broadcast_to(msg[0, TWO.y["owner"] : TWO.y["owner"] + 1], (8, NZ))


def flow_two_kernel(pop, fl, sh, xl, xh, yl, yh, cl, ch, pop_out, lv):
    collide_and_stream(TWO, pop, fl, sh, (xl, xh, yl, yh, cl, ch), lv, pop_out, None)


def place(up):
    me = lax.rem(lax.axis_index("gy") + up, 8)
    return jnp.full((1, NZ), me, jnp.int32).astype(F32)


def route_kernel(mine, below, above, up, down):
    want_up, want_down = above[2 * CX, 8:9], below[2 * CX, 0:1]
    for x in range(2 * CX):
        up[x] = jnp.where(want_up == place(0), mine[x], jnp.where(want_up == place(1), above[x], below[x]))
        down[x] = jnp.where(want_down == place(0), mine[x], below[x])


def arrive_kernel(mine, below, above, from_low, from_high, owner, out):
    slab = owner[0:1]
    near = ((0, mine), (7, below), (1, above), (2, from_high), (3, from_high))
    for x in range(2 * CX):
        v = from_low[x]
        for up, values in near:
            v = jnp.where(slab == place(up), values[x], v)
        out[x] = v


VMEM, FAR, SMEM = (pl.BlockSpec(memory_space=m) for m in (pltpu.VMEM, pltpu.HBM, pltpu.SMEM))


def call(kernel, outs, args, scratch=(), specs=None, flops=0):
    return pl.pallas_call(
        kernel,
        out_shape=outs,
        in_specs=specs or [VMEM] * len(args),
        out_specs=[VMEM] * len(outs),
        scratch_shapes=[pltpu.VMEM(s, F32) if isinstance(s, tuple) else s for s in scratch],
        compiler_params=pltpu.CompilerParams(vmem_limit_bytes=24 * 1024 * 1024),
        cost_estimate=pl.CostEstimate(flops=flops, bytes_accessed=0, transcendentals=0) if flops else None,
    )(*args)


HALO = (EX, EY, NZ)
RIM = (10, EY, NZ)
FIELDS = (HALO, HALO, HALO, RIM, (3,) + RIM, (2,) + RIM, (3,) + RIM)


def shift(values, axis, by):
    n = lax.axis_size(axis)
    return lax.ppermute(values, axis, [(i, (i + by) % n) for i in range(n)])


def exchange(x_hi, x_lo, y_hi, y_lo):
    yl, yh = shift(y_hi, "gy", 1), shift(y_lo, "gy", -1)
    xl, xh = shift(x_hi, "gx", 1), shift(x_lo, "gx", -1)
    return xl, xh, yl, yh


def body(populations, concentration, potential, permittivity, fluid_mask, owners):
    block, row = shape(CX, CY, NZ), shape(8, NZ)
    pops, both, four = shape(19, CX, CY, NZ), shape(2, CX, CY, NZ), shape(4, CX, CY, NZ)

    def messages(plan):
        x, y = shape(plan.x_planes, CY, NZ), shape(CX, plan.y_rows, NZ)
        return (x, x, y, y)

    def tiles(plan):
        return (shape(2 * plan.tiles, 8, NZ),) * 2

    *sent, dm, charge, fluid = call(
        first_kernel, messages(ONE) + (four, block, block),
        tuple(pltpu.with_memory_space_constraint(v, pltpu.HBM) for v in (
            populations, concentration, potential, permittivity, fluid_mask)),
        (pops.shape, both.shape, block.shape, block.shape, pltpu.VMEM(block.shape, jnp.int32),
         pltpu.SemaphoreType.DMA((5,))),
        [FAR] * 5)
    got = exchange(*sent)
    c_hi, c_lo, owner = call(corner_one_kernel, tiles(ONE) + (row,), (owners,) + got[:2], (), [SMEM, VMEM, VMEM])
    got += (shift(c_hi, "gy", 1), shift(c_lo, "gy", -1))
    pop, phi, conc, charge, *rest = call(
        step_one_kernel,
        (pops, block, both, block) + messages(TWO)
        + (four, shape(4, CY, NZ), shape(6, *HALO), shape(*HALO), shape(*RIM)),
        (populations, concentration, potential, permittivity, dm, charge, fluid) + got,
        (HALO,) + FIELDS + ((5,) + RIM, (19,) + RIM))
    sent, (dm, rim, coef, inv, fl) = rest[:4], rest[4:]
    got = exchange(*sent)
    c_hi, c_lo = call(corner_two_kernel, tiles(TWO), got[:2] + (rim,))
    got += (shift(c_hi, "gy", 1), shift(c_lo, "gy", -1))
    slab = shape(2 * CX, CY, NZ)
    phi, mine, sh = call(
        ions_two_kernel, (block, shape(2 * CX + 1, CY, NZ), shape(5, *RIM)),
        (conc, phi, charge, dm, rim, coef, inv, fl) + got, FIELDS)
    below, above = shift(mine, "gy", 1), shift(mine, "gy", -1)
    (pop,) = call(flow_two_kernel, (pops,), (pop, fl, sh) + got, ((19,) + RIM,), flops=40_000_000)
    up, down = call(route_kernel, (slab, slab), (mine, below, above))
    from_low, from_high = shift(up, "gy", 3), shift(down, "gy", -3)
    (migrated,) = call(arrive_kernel, (slab,), (mine, below, above, from_low, from_high, owner))
    return (pop, phi, migrated.reshape(2, CX, CY, NZ))


def solution(mesh):
    in_specs = (
        P(None, "gx", "gy", None),
        P(None, "gx", "gy", None),
        P("gx", "gy", None),
        P("gx", "gy", None),
        P("gx", "gy", None),
        P("gx", "gy"),
    )
    out_specs = (P(None, "gx", "gy", None), P("gx", "gy", None), P(None, "gx", "gy", None))
    return jax.shard_map(body, mesh=mesh, in_specs=in_specs, out_specs=out_specs, check_vma=False)
```
